256 devices in a mesh: ctx: 32 (over z, x), tp: 8 (over y, core).
Axes of the slice: x: 4, y: 4, z: 8, core: 2. Of those that a mesh axis runs over, the one named last changes fastest.
Arguments:
- qkv: bfloat16 [16384, 3, 4096], P('ctx', None, 'tp'), may hold values from -6 to 6
- short_filter: float32 [7, 3, 4096], P(None, None, 'tp'), may hold values from -2.4 to 2.4
- long_filter: bfloat16 [128, 4096], P(None, 'tp'), may hold values from -0.5 to 0.5
- out_weight: bfloat16 [4096, 4096], P('tp'), may hold values from -0.125 to 0.125
- cotangent: bfloat16 [16384, 4096], P('ctx', 'tp'), may hold values from -6 to 6
- valid_len: int32 [32], P('ctx'), may hold values from 128 to 512, as said below
Outputs:
- mixed: bfloat16 [16384, 4096], P('ctx', 'tp')
- d_qkv: bfloat16 [16384, 3, 4096], P('ctx', None, 'tp')
- d_weight: float32 [4096, 4096], P('tp', 'ctx')
The draws below stay inside these ranges and needn't reach their ends.
Inputs may be any that keep to these rules, and one draw needn't show every extreme that they name: `valid_len`: shards of even index are fully valid.
All inputs are finite; a program needn't handle non-finite values.
Results may differ from the reference program's by a relative error of at most 0.0058.
Values may be sent and summed in bfloat16 or wider, within the bound.
No kernel may reach another device: no remote copies, remote signals or barrier semaphores. Data moves between devices by JAX's collectives and lax.ppermute only.
A program may use at most 128 MiB of HBM per device.

```python
import jax
import jax.numpy as jnp
from jax import lax

D = 4096
SHORT = 7
LONG = 128
TOK_DEV = 512
TOKENS = 16384
N_CTX = 32


def draw_valid_len(key, part):
    key = jax.random.fold_in(key, 7)
    lengths = jax.random.randint(key, (N_CTX,), TOK_DEV // 4, TOK_DEV + 1)
    return jnp.where(jnp.arange(N_CTX) % 2 == 0, TOK_DEV, lengths).astype(jnp.int32)


def strengthened(drawn, own_key, source, target, blocks, factor):
    def block_of(dim):
        return (jnp.arange(drawn.shape[dim]) // (drawn.shape[dim] // blocks)).reshape((-1,) + (1,) * (drawn.ndim - 1 - dim))

    one_side = jax.random.permutation(own_key, blocks)[block_of(target)]
    other_side = (block_of(target) + blocks // 2) % blocks
    return jnp.where((block_of(source) == one_side) | (block_of(source) == other_side), factor * drawn, drawn)


def levels(stream_key, shape, split, low, top_value):
    level, own = 1.0, jax.random.fold_in(stream_key, 6)
    for position, blocks in split:
        heights = jnp.exp(jax.random.uniform(jax.random.fold_in(own, position), (blocks,), jnp.float32, low / len(split), top_value / len(split)))
        level = level * jnp.repeat(heights, shape[position] // blocks).reshape([-1 if axis == position else 1 for axis in range(len(shape))])
    return level


def normal_values(key, extent, deviation, limit, split=(), dtype=jnp.bfloat16):
    entries = deviation * jax.random.normal(key, extent, jnp.float32)
    if split:
        entries = entries * levels(key, extent, split, -0.22, 0.18)
    return jnp.clip(entries, -limit, limit).astype(dtype)


def gaussian_with(rng, shape, spread, most, shards, heavy, held_as=jnp.bfloat16):
    values = spread * jax.random.normal(rng, shape, jnp.float32)
    if shards:
        values = values * levels(rng, shape, shards, -0.22, 0.18)
    return jnp.clip(strengthened(values, jax.random.fold_in(rng, 3), *heavy), -most, most).astype(held_as)


def setup_inputs(seed: int = 0) -> dict:
    keys = jax.random.split(jax.random.key(seed), 7)
    qkv = normal_values(keys[0], (TOKENS, 3, D), 1.0, 6.0, ((0, 32), (2, 8)))
    short_filter = normal_values(keys[1], (SHORT, 3, D), 0.4, 2.4, ((2, 8),), jnp.float32)
    long_filter = normal_values(keys[2], (LONG, D), LONG ** -0.5, 0.5, ((1, 8),))
    out_weight = gaussian_with(keys[3], (D, D), D ** -0.5, 0.125, ((0, 8),), (0, 1, 8, 2.0))
    cotangent = gaussian_with(keys[4], (TOKENS, D), 1.0, 6.0, ((0, 32), (1, 8)), (0, 1, 32, 2.75))
    valid_len = draw_valid_len(jax.random.fold_in(keys[6], 71), 0)
    return dict(qkv=qkv, short_filter=short_filter, long_filter=long_filter, out_weight=out_weight, cotangent=cotangent, valid_len=valid_len)


def band_table(causal):
    out_idx = jnp.arange(LONG)[:, None, None]
    in_idx = jnp.arange(2 * LONG)[None, :, None]
    tap_idx = jnp.arange(LONG)[None, None, :]
    if causal:
        return (out_idx + LONG - in_idx == tap_idx).astype(jnp.float32)
    return (in_idx - out_idx == tap_idx).astype(jnp.float32)

def banded(windows, filters, table):
    blocks, width, channels = windows.shape
    group = min(channels, 256)
    count = channels // group
    win_groups = windows.reshape(blocks, width, count, group).transpose(2, 0, 1, 3)
    filt_groups = filters.reshape(LONG, count, group).transpose(1, 0, 2)

    def apply_group(pair):
        window_part, filt_part = pair
        toeplitz = jnp.einsum('ijl,lc->cij', table, filt_part, precision=lax.Precision.HIGHEST)
        return jnp.einsum('cij,bjc->bic', toeplitz, window_part, precision=lax.Precision.HIGHEST)
    result = lax.map(apply_group, (win_groups, filt_groups))
    return result.transpose(1, 2, 0, 3).reshape(blocks * LONG, channels)

def long_causal(values, filters):
    length, channels = values.shape
    blocks = length // LONG
    current = values.astype(jnp.float32)
    before = jnp.pad(current, ((LONG, 0), (0, 0)))[:length]
    windows = jnp.concatenate([before.reshape(blocks, LONG, channels), current.reshape(blocks, LONG, channels)], axis=1)
    return banded(windows, filters.astype(jnp.float32), band_table(True))

def long_anti(values, filters):
    length, channels = values.shape
    blocks = length // LONG
    current = values.astype(jnp.float32)
    after_rows = jnp.pad(current, ((0, LONG), (0, 0)))[LONG:]
    windows = jnp.concatenate([current.reshape(blocks, LONG, channels), after_rows.reshape(blocks, LONG, channels)], axis=1)
    return banded(windows, filters.astype(jnp.float32), band_table(False))

def reference(qkv, short_filter, long_filter, out_weight, cotangent, valid_len):
    positions = jnp.arange(TOKENS)
    limits = jnp.repeat(valid_len, TOK_DEV, total_repeat_length=TOKENS)
    live_mask = (positions % TOK_DEV < limits).astype(jnp.float32)[:, None]
    streams = qkv.astype(jnp.float32) * live_mask[:, :, None]
    padded = jnp.pad(streams, ((SHORT - 1, 0), (0, 0), (0, 0)))
    filtered = jnp.zeros_like(streams)
    for tap_index in range(SHORT):
        filtered = filtered + short_filter[tap_index] * padded[SHORT - 1 - tap_index:SHORT - 1 - tap_index + TOKENS]
    q_side, k_side, v_side = (filtered[:, 0], filtered[:, 1], filtered[:, 2])
    gated = (k_side * v_side).astype(jnp.bfloat16)
    conv_out = long_causal(gated, long_filter)
    mix_in = (live_mask * q_side * conv_out).astype(jnp.bfloat16)
    mixed = jnp.dot(mix_in, out_weight, preferred_element_type=jnp.float32).astype(jnp.bfloat16)
    d_mix = live_mask * jnp.dot(cotangent, out_weight.T, preferred_element_type=jnp.float32)
    d_conv = (d_mix * q_side).astype(jnp.bfloat16)
    d_q = d_mix * conv_out
    d_gated = long_anti(d_conv, long_filter)
    d_filtered = jnp.stack([d_q, d_gated * v_side, d_gated * k_side], axis=1)
    padded_back = jnp.pad(d_filtered, ((0, SHORT - 1), (0, 0), (0, 0)))
    summed = jnp.zeros_like(d_filtered)
    for tap_index in range(SHORT):
        summed = summed + short_filter[tap_index] * padded_back[tap_index:tap_index + TOKENS]
    d_qkv = (summed * live_mask[:, :, None]).astype(jnp.bfloat16)
    grad_scale = 1.0 / jnp.sqrt(jnp.float32(TOKENS))
    d_weight = jnp.dot(mix_in.T, cotangent, preferred_element_type=jnp.float32) * grad_scale
    return (mixed, d_qkv, d_weight)
```

```python
import functools

import jax
import jax.numpy as jnp
import ml_dtypes
import numpy as np
from jax import lax
from jax.experimental import pallas as pl
from jax.experimental.pallas import tpu as pltpu
from jax.sharding import PartitionSpec as P

SHORT = 7
LONG = 128
ROWS = 512
CH = 512
LANES = 128
TAIL = 144
RIM = 16
STEP = 64
NZ, NX, NY = 8, 4, 4
F32, BF16 = jnp.float32, jnp.bfloat16


def split_bf16(table):
    high = table.astype(ml_dtypes.bfloat16)
    low = (table - high.astype(np.float64)).astype(ml_dtypes.bfloat16)
    return high, low


def tables():
    size = 2 * LONG
    freq = np.arange(LONG)[:, None]
    angle = 2.0 * np.pi * freq * np.arange(size)[None, :] / size
    real = np.concatenate([np.cos(angle), np.sin(angle)], axis=0)
    real[LONG] = (-1.0) ** np.arange(size)
    high, low = split_bf16(real[:, :LONG])
    forward = np.concatenate([high, low], axis=1)
    weight = np.full((2 * LONG, 1), 2.0 / size)
    weight[0] = weight[LONG] = 1.0 / size
    inverse = (real * weight).T
    causal = np.concatenate(split_bf16(inverse[LONG:]), axis=0)
    anti = np.concatenate(split_bf16(inverse[:LONG]), axis=0)
    return forward, causal, anti


def signs(rows):
    row = lax.broadcasted_iota(jnp.int32, (rows, LANES), 0)
    return jnp.where(row % 2 == 0, 1.0, -1.0).astype(F32)


def spectrum(forward, block):
    return jnp.dot(forward, jnp.concatenate([block, block], axis=0), preferred_element_type=F32)


def filter_spectrum(forward, taps):
    both = spectrum(forward, taps)
    cos_part, sin_part = both[:LONG], both[LONG:]
    first = lax.broadcasted_iota(jnp.int32, (LONG, LANES), 0) == 0
    return cos_part, jnp.where(first, 0.0, sin_part), jnp.where(first, sin_part, cos_part)


def back(table, product):
    high = product.astype(BF16)
    low = (product - high.astype(F32)).astype(BF16)
    half = table.shape[0] // 2
    both = jnp.dot(table, high, preferred_element_type=F32)
    rest = jnp.dot(table[:half], low, preferred_element_type=F32)
    return both[:half] + both[half:] + rest


def live_rows(valid, start, rows):
    row = lax.broadcasted_iota(jnp.int32, (rows, LANES), 0) + start
    return jnp.where(row < valid, 1.0, 0.0).astype(F32)


def forward_kernel(
    valid_ref, qkv_ref, halo_ref, short_ref, long_ref, fwd_ref, inv_ref,
    mix_ref, q_ref, k_ref, v_ref, conv_ref, ext_ref, gate_ref,
):
    valid = valid_ref[0]
    ext_ref[0, TAIL - RIM : TAIL] = halo_ref[0:RIM].astype(F32)
    ext_ref[1, 0:TAIL] = halo_ref[RIM : RIM + TAIL].astype(F32)
    ext_ref[2, 0:TAIL] = halo_ref[RIM + TAIL : RIM + 2 * TAIL].astype(F32)
    for start in range(0, ROWS, STEP):
        live = live_rows(valid, start, STEP)
        for stream in range(3):
            ext_ref[stream, TAIL + start : TAIL + start + STEP] = (
                qkv_ref[stream, start : start + STEP].astype(F32) * live
            )

    def filtered(stream, start):
        total = short_ref[stream, 0:1] * ext_ref[stream, start : start + STEP]
        for tap in range(1, SHORT):
            total += short_ref[stream, tap : tap + 1] * ext_ref[stream, start - tap : start - tap + STEP]
        return total

    for start in range(-LONG, ROWS, STEP):
        k_side = filtered(1, TAIL + start)
        v_side = filtered(2, TAIL + start)
        if start >= 0:
            k_ref[start : start + STEP] = k_side
            v_ref[start : start + STEP] = v_side
            q_ref[start : start + STEP] = filtered(0, TAIL + start)
        gate_ref[LONG + start : LONG + start + STEP] = (k_side * v_side).astype(BF16)

    fwd = fwd_ref[...]
    inv = inv_ref[...]
    cos_h, sin_h, alt_h = filter_spectrum(fwd, long_ref[...])
    sign = signs(2 * LONG)
    before = spectrum(fwd, gate_ref[0:LONG])
    for block in range(ROWS // LONG):
        start = block * LONG
        now = spectrum(fwd, gate_ref[LONG + start : 2 * LONG + start])
        window = before + sign * now
        before = now
        cos_x, sin_x = window[:LONG], window[LONG:]
        product = jnp.concatenate(
            [cos_x * cos_h - sin_x * sin_h, cos_x * sin_h + sin_x * alt_h], axis=0
        )
        conv = back(inv, product)
        conv_ref[start : start + LONG] = conv
        live = live_rows(valid, start, LONG)
        mix_ref[start : start + LONG] = (live * q_ref[start : start + LONG] * conv).astype(BF16)


def backward_kernel(
    valid_ref, dconv_ref, msg_ref, dq_ref, k_ref, v_ref, short_ref, long_ref, fwd_ref, inv_ref,
    out_ref, ext_ref, gate_ref,
):
    valid = valid_ref[0]
    fwd = fwd_ref[...]
    inv = inv_ref[...]
    gate_ref[0:TAIL] = msg_ref[0:TAIL]
    gate_ref[TAIL : 2 * LONG] = jnp.zeros((2 * LONG - TAIL, LANES), BF16)
    cos_h, sin_h, alt_h = filter_spectrum(fwd, long_ref[...])
    sign = signs(2 * LONG)
    blocks = ROWS // LONG
    ext_ref[0, 0:ROWS] = dq_ref[...]
    ext_ref[0, ROWS : ROWS + RIM] = msg_ref[TAIL : TAIL + RIM].astype(F32)
    now = spectrum(fwd, dconv_ref[0:LONG])
    for block in range(blocks + 1):
        start = block * LONG
        if block + 1 < blocks:
            after = spectrum(fwd, dconv_ref[start + LONG : start + 2 * LONG])
        else:
            rim = (block + 1 - blocks) * LONG
            after = spectrum(fwd, gate_ref[rim : rim + LONG])
        window = now + sign * after
        now = after
        cos_x, sin_x = window[:LONG], window[LONG:]
        product = jnp.concatenate(
            [cos_x * cos_h + sin_x * sin_h, sin_x * alt_h - cos_x * sin_h], axis=0
        )
        gated = back(inv, product)
        if block < blocks:
            ext_ref[1, start : start + LONG] = gated * v_ref[start : start + LONG]
            ext_ref[2, start : start + LONG] = gated * k_ref[start : start + LONG]
        else:
            rim = gated[:RIM]
            v_rim = msg_ref[TAIL + RIM : TAIL + 2 * RIM].astype(F32)
            k_rim = msg_ref[TAIL + 2 * RIM : TAIL + 3 * RIM].astype(F32)
            ext_ref[1, ROWS : ROWS + RIM] = rim * v_rim
            ext_ref[2, ROWS : ROWS + RIM] = rim * k_rim
    for start in range(0, ROWS, STEP):
        live = live_rows(valid, start, STEP)
        for stream in range(3):
            total = short_ref[stream, 0:1] * ext_ref[stream, start : start + STEP]
            for tap in range(1, SHORT):
                total += short_ref[stream, tap : tap + 1] * ext_ref[stream, start + tap : start + tap + STEP]
            out_ref[stream, start : start + STEP] = (total * live).astype(BF16)


def params(mib=40):
    return pltpu.CompilerParams(vmem_limit_bytes=mib * 2**20)


def cost(flops, moved):
    return pl.CostEstimate(flops=flops, bytes_accessed=moved, transcendentals=0)


SMEM = pl.BlockSpec(memory_space=pltpu.SMEM)
VMEM = pl.BlockSpec(memory_space=pltpu.VMEM)


def lane_spec(*lead):
    return pl.BlockSpec(lead + (LANES,), lambda i: (0,) * len(lead) + (i,))


def whole(*shape):
    return pl.BlockSpec(shape, lambda i: (0,) * len(shape))


def run_forward(valid, streams, halo, short, long_taps, fwd, inv):
    side = jax.ShapeDtypeStruct((ROWS, CH), F32)
    return pl.pallas_call(
        forward_kernel,
        grid=(CH // LANES,),
        in_specs=[
            SMEM, lane_spec(3, ROWS), lane_spec(RIM + 2 * TAIL), lane_spec(3, SHORT), lane_spec(LONG),
            whole(2 * LONG, 2 * LONG), whole(2 * LONG, 2 * LONG),
        ],
        out_specs=[lane_spec(ROWS)] * 5,
        out_shape=[jax.ShapeDtypeStruct((ROWS, CH), BF16), side, side, side, side],
        scratch_shapes=[
            pltpu.VMEM((3, TAIL + ROWS, LANES), F32),
            pltpu.VMEM((LONG + ROWS, LANES), BF16),
        ],
        compiler_params=params(),
        cost_estimate=cost(5_000_000_000, 7_000_000),
        name="forward",
    )(valid, streams, halo, short, long_taps, fwd, inv)


def run_backward(valid, d_conv, msg, d_q, k_side, v_side, short, long_taps, fwd, inv):
    return pl.pallas_call(
        backward_kernel,
        grid=(CH // LANES,),
        in_specs=[
            SMEM, lane_spec(ROWS), lane_spec(TAIL + 3 * RIM), lane_spec(ROWS), lane_spec(ROWS),
            lane_spec(ROWS), lane_spec(3, SHORT), lane_spec(LONG),
            whole(2 * LONG, 2 * LONG), whole(2 * LONG, 2 * LONG),
        ],
        out_specs=lane_spec(3, ROWS),
        out_shape=jax.ShapeDtypeStruct((3, ROWS, CH), BF16),
        scratch_shapes=[
            pltpu.VMEM((3, ROWS + RIM, LANES), F32),
            pltpu.VMEM((2 * LONG, LANES), BF16),
        ],
        compiler_params=params(),
        cost_estimate=cost(5_000_000_000, 7_000_000),
        name="backward",
    )(valid, d_conv, msg, d_q, k_side, v_side, short, long_taps, fwd, inv)


def project_kernel(order_ref, mix_ref, weight_ref, out_ref):
    out_ref[0] = jnp.dot(mix_ref[...], weight_ref[...], preferred_element_type=F32).astype(BF16)


def run_project(order, mix_in, weight):
    count = order.shape[0]
    return pl.pallas_call(
        project_kernel,
        grid_spec=pltpu.PrefetchScalarGridSpec(
            num_scalar_prefetch=1,
            grid=(count,),
            in_specs=[
                pl.BlockSpec((ROWS, CH), lambda i, order: (0, 0)),
                pl.BlockSpec((CH, CH), lambda i, order: (0, order[i])),
            ],
            out_specs=pl.BlockSpec((1, ROWS, CH), lambda i, order: (i, 0, 0)),
        ),
        out_shape=jax.ShapeDtypeStruct((count, ROWS, CH), BF16),
        compiler_params=params(),
        cost_estimate=cost(2 * count * ROWS * CH * CH, 4_500_000),
        name="project",
    )(order, mix_in, weight)


def project_add_kernel(order_ref, mix_ref, weight_ref, other_ref, one_ref, two_ref, three_ref, own_ref):
    step = pl.program_id(0)
    total = jnp.dot(mix_ref[...], weight_ref[...], preferred_element_type=F32)
    total += other_ref[0].astype(F32)
    for place, ref in enumerate((one_ref, two_ref, three_ref, own_ref)):

        @pl.when(step == place)
        def _(ref=ref):
            ref[...] = total.astype(ref.dtype)


def run_project_add(order, mix_in, weight, other):
    piece = jax.ShapeDtypeStruct((ROWS, CH), BF16)
    fixed = pl.BlockSpec((ROWS, CH), lambda i, order: (0, 0))
    return pl.pallas_call(
        project_add_kernel,
        grid_spec=pltpu.PrefetchScalarGridSpec(
            num_scalar_prefetch=1,
            grid=(4,),
            in_specs=[
                fixed,
                pl.BlockSpec((CH, CH), lambda i, order: (0, order[i])),
                pl.BlockSpec((1, ROWS, CH), lambda i, order: (i, 0, 0)),
            ],
            out_specs=[fixed] * 4,
        ),
        out_shape=[piece, piece, piece, jax.ShapeDtypeStruct((ROWS, CH), F32)],
        compiler_params=params(),
        cost_estimate=cost(8 * ROWS * CH * CH, 7_000_000),
        name="project_add",
    )(order, mix_in, weight, other)


def outer_kernel(count, place_ref, mix_ref, *refs):
    pieces, (own_ref, one_ref, two_ref, three_ref, work_ref) = refs[:count], refs[count:]
    mine = place_ref[0]
    mix_in = mix_ref[...]
    for slot, piece in enumerate(pieces):
        work_ref[...] = lax.dot_general(
            mix_in, piece[...], (((0,), (0,)), ((), ())), preferred_element_type=F32
        )
        for ahead, ref in enumerate((own_ref, one_ref, two_ref, three_ref)):
            column = pl.multiple_of(lax.rem(mine + ahead, NX) * LANES, LANES)
            ref[slot] = work_ref[:, pl.ds(column, LANES)].astype(ref.dtype)


def run_outer(place, mix_in, pieces):
    count = len(pieces)
    sent = jax.ShapeDtypeStruct((count, CH, LANES), BF16)
    return pl.pallas_call(
        functools.partial(outer_kernel, count),
        in_specs=[SMEM, VMEM] + [VMEM] * count,
        out_specs=[VMEM] * 4,
        out_shape=[jax.ShapeDtypeStruct((count, CH, LANES), F32), sent, sent, sent],
        scratch_shapes=[pltpu.VMEM((CH, CH), F32)],
        compiler_params=params(),
        cost_estimate=cost(2 * count * ROWS * CH * CH, 1_300_000 * count),
        name="outer",
    )(place, mix_in, *pieces)


def gather_x_kernel(counts, offset_ref, *refs):
    inputs, outputs, work_ref = refs[: 4 * len(counts)], refs[4 * len(counts) : -1], refs[-1]
    slab = 0
    for group, count in enumerate(counts):
        own, one, two, three = inputs[4 * group : 4 * group + 4]
        for slot in range(count):
            total = own[slot] + one[slot].astype(F32) + two[slot].astype(F32) + three[slot].astype(F32)
            work_ref[offset_ref[slab]] = total
            slab += 1
    for ahead, ref in enumerate(outputs):
        ref[...] = work_ref[ahead].astype(ref.dtype)


def run_gather_x(offsets, groups):
    counts = [group[0].shape[0] for group in groups]
    sent = jax.ShapeDtypeStruct((CH, LANES), BF16)
    return pl.pallas_call(
        functools.partial(gather_x_kernel, counts),
        in_specs=[SMEM] + [VMEM] * (4 * len(groups)),
        out_specs=[VMEM] * NZ,
        out_shape=[jax.ShapeDtypeStruct((CH, LANES), F32)] + [sent] * (NZ - 1),
        scratch_shapes=[pltpu.VMEM((NZ, CH, LANES), F32)],
        compiler_params=params(),
        cost_estimate=cost(4_000_000, 6_500_000),
        name="gather_x",
    )(offsets, *[array for group in groups for array in group])


def d_mix_kernel(count, last, info_ref, weight_ref, *refs):
    pieces, rest = refs[:count], refs[count:]
    total = None
    for slot, piece in enumerate(pieces):
        column = pl.multiple_of(info_ref[1 + slot] * CH, CH)
        part = lax.dot_general(
            piece[...], weight_ref[:, pl.ds(column, CH)], (((1,), (1,)), ((), ())),
            preferred_element_type=F32,
        )
        total = part if total is None else total + part
    if not last:
        rest[0][...] = total
        return
    acc_ref, q_ref, k_ref, v_ref, conv_ref, dconv_ref, dq_ref, msg_ref = rest
    row = lax.broadcasted_iota(jnp.int32, (ROWS, CH), 0)
    d_mix = jnp.where(row < info_ref[0], total + acc_ref[...], 0.0)
    d_conv = (d_mix * q_ref[...]).astype(BF16)
    d_q = d_mix * conv_ref[...]
    dconv_ref[...] = d_conv
    dq_ref[...] = d_q
    msg_ref[0:TAIL] = d_conv[:TAIL]
    msg_ref[TAIL : TAIL + RIM] = d_q[:RIM].astype(BF16)
    msg_ref[TAIL + RIM : TAIL + 2 * RIM] = v_ref[0:RIM].astype(BF16)
    msg_ref[TAIL + 2 * RIM : TAIL + 3 * RIM] = k_ref[0:RIM].astype(BF16)


def run_d_mix(info, weight, pieces, extra=()):
    count = len(pieces)
    full = jax.ShapeDtypeStruct((ROWS, CH), F32)
    if extra:
        shapes = [
            jax.ShapeDtypeStruct((ROWS, CH), BF16), full,
            jax.ShapeDtypeStruct((TAIL + 3 * RIM, CH), BF16),
        ]
    else:
        shapes = [full]
    return pl.pallas_call(
        functools.partial(d_mix_kernel, count, bool(extra)),
        in_specs=[SMEM, VMEM] + [VMEM] * (count + len(extra)),
        out_specs=[VMEM] * len(shapes),
        out_shape=shapes,
        compiler_params=params(),
        cost_estimate=cost(2 * count * ROWS * CH * CH, 8_000_000),
        name="d_mix",
    )(info, weight, *pieces, *extra)


def ctx_pairs(ahead_z, ahead_x):
    return [
        (z * NX + x, (z + ahead_z) % NZ * NX + (x + ahead_x) % NX) for z in range(NZ) for x in range(NX)
    ]


def along_x(array, ahead):
    return lax.ppermute(array, "ctx", ctx_pairs(0, ahead))


def along_z(array, ahead):
    return lax.ppermute(array, "ctx", ctx_pairs(ahead, 0))


def along_y(array, ahead):
    pairs = [(2 * y + core, 2 * ((y + ahead) % NY) + core) for y in range(NY) for core in range(2)]
    return lax.ppermute(array, "tp", pairs)


def other_core(array):
    return lax.ppermute(array, "tp", [(i, i ^ 1) for i in range(2 * NY)])


def neighbour(array, by):
    count = NZ * NX
    return lax.ppermute(array, "ctx", [(i, i + by) for i in range(count) if 0 <= i + by < count])


def local(qkv, short_filter, long_filter, out_weight, cotangent, valid_len):
    forward_table, causal_table, anti_table = (jnp.asarray(table) for table in tables())
    ctx, tp = lax.axis_index("ctx"), lax.axis_index("tp")
    z, x = ctx // NX, ctx % NX
    y, core = tp // 2, tp % 2
    streams = qkv.transpose(1, 0, 2)
    short = short_filter.transpose(1, 0, 2)

    def masked_tail(stream, rows):
        alive = (jnp.arange(ROWS - rows, ROWS) < valid_len[0])[:, None]
        return jnp.where(alive, streams[stream, ROWS - rows :], jnp.zeros((), BF16))

    tail = jnp.concatenate([masked_tail(0, RIM), masked_tail(1, TAIL), masked_tail(2, TAIL)], axis=0)
    halo = neighbour(tail, 1)

    def block_of(ahead, other=0):
        return (y + ahead) % NY * 2 + (core + other) % 2

    own_other = other_core(cotangent)
    below = along_y(cotangent, 1)
    above = along_y(cotangent, -1)
    held, halo = lax.optimization_barrier((cotangent, halo))
    far = along_y(held, 2)

    mix_in, q_side, k_side, v_side, conv = run_forward(
        valid_len, streams, halo, short, long_filter, forward_table, causal_table
    )

    below_other, above_other = other_core(below), other_core(above)
    far_other = other_core(far)
    near = [cotangent, own_other, below, below_other, above, above_other]
    near_blocks = [block_of(0), block_of(0, 1), block_of(-1), block_of(-1, 1), block_of(1), block_of(1, 1)]
    last = [far, far_other]
    last_blocks = [block_of(2), block_of(2, 1)]

    given = run_project(
        jnp.stack([block_of(1, 1), block_of(2, 1), block_of(3, 1), block_of(0, 1)]), mix_in, out_weight
    )
    taken = other_core(given)

    place = x.reshape(1)
    groups = []
    for pieces in (near, last):
        own, *sent = run_outer(place, mix_in, pieces)
        groups.append([own] + [along_x(array, ahead + 1) for ahead, array in enumerate(sent)])

    acc = run_d_mix(jnp.stack([valid_len[0]] + near_blocks), out_weight, near)[0]
    d_conv, d_q, msg = run_d_mix(
        jnp.stack([valid_len[0]] + last_blocks), out_weight, last, (acc, q_side, k_side, v_side, conv)
    )
    msg = neighbour(msg, -1)

    one, two, three, own_out = run_project_add(
        jnp.stack([block_of(1), block_of(2), block_of(3), block_of(0)]), mix_in, out_weight, taken
    )
    arrived = [along_y(one, 1), along_y(two, 2), along_y(three, 3)]
    mixed = own_out
    for array in arrived:
        mixed = mixed + array.astype(F32)
    mixed = mixed.astype(BF16)

    d_streams = run_backward(
        valid_len, d_conv, msg, d_q, k_side, v_side, short, long_filter, forward_table, anti_table
    )
    d_qkv = d_streams.transpose(1, 0, 2)

    offsets = jnp.stack([(block - z) % NZ for block in near_blocks + last_blocks])
    total, *sent = run_gather_x(offsets, groups)
    for ahead, array in enumerate(sent):
        total = total + along_z(array, ahead + 1).astype(F32)
    d_weight = total * (1.0 / jnp.sqrt(jnp.float32(ROWS * NZ * NX)))
    return mixed, d_qkv, d_weight


def solution(mesh):
    in_specs = (
        P("ctx", None, "tp"),
        P(None, None, "tp"),
        P(None, "tp"),
        P("tp", None),
        P("ctx", "tp"),
        P("ctx"),
    )
    out_specs = (P("ctx", "tp"), P("ctx", None, "tp"), P("tp", "ctx"))
    return jax.shard_map(local, mesh=mesh, in_specs=in_specs, out_specs=out_specs, check_vma=False)
```

```python
import functools

import jax
import jax.numpy as jnp
import ml_dtypes
import numpy as np
from jax import lax
from jax.experimental import pallas as pl
from jax.experimental.pallas import tpu as pltpu
from jax.sharding import PartitionSpec as P

SHORT = 7
LONG = 128
ROWS = 512
CH = 512
LANES = 128
TAIL = 144
RIM = 16
STEP = 64
NZ, NX, NY = 8, 4, 4
F32, BF16 = jnp.float32, jnp.bfloat16


def split_bf16(table):
    high = table.astype(ml_dtypes.bfloat16)
    low = (table - high.astype(np.float64)).astype(ml_dtypes.bfloat16)
    return high, low


def tables():
    size = 2 * LONG
    freq = np.arange(LONG)[:, None]
    angle = 2.0 * np.pi * freq * np.arange(size)[None, :] / size
    real = np.concatenate([np.cos(angle), np.sin(angle)], axis=0)
    real[LONG] = (-1.0) ** np.arange(size)
    high, low = split_bf16(real[:, :LONG])
    forward = np.concatenate([high, low], axis=1)
    weight = np.full((2 * LONG, 1), 2.0 / size)
    weight[0] = weight[LONG] = 1.0 / size
    inverse = (real * weight).T
    causal = np.concatenate(split_bf16(inverse[LONG:]), axis=0)
    anti = np.concatenate(split_bf16(inverse[:LONG]), axis=0)
    return forward, causal, anti


def signs(rows):
    row = lax.broadcasted_iota(jnp.int32, (rows, LANES), 0)
    return jnp.where(row % 2 == 0, 1.0, -1.0).astype(F32)


def spectrum(forward, block):
    return jnp.dot(forward, jnp.concatenate([block, block], axis=0), preferred_element_type=F32)


def filter_spectrum(forward, taps):
    both = spectrum(forward, taps)
    cos_part, sin_part = both[:LONG], both[LONG:]
    first = lax.broadcasted_iota(jnp.int32, (LONG, LANES), 0) == 0
    return cos_part, jnp.where(first, 0.0, sin_part), jnp.where(first, sin_part, cos_part)


def back(table, product):
    high = product.astype(BF16)
    low = (product - high.astype(F32)).astype(BF16)
    half = table.shape[0] // 2
    both = jnp.dot(table, high, preferred_element_type=F32)
    rest = jnp.dot(table[:half], low, preferred_element_type=F32)
    return both[:half] + both[half:] + rest


def live_rows(valid, start, rows):
    row = lax.broadcasted_iota(jnp.int32, (rows, LANES), 0) + start
    return jnp.where(row < valid, 1.0, 0.0).astype(F32)


def filtered(short_ref, ext_ref, stream, start, rows):
    total = short_ref[stream, 0:1] * ext_ref[stream, start : start + rows]
    for tap in range(1, SHORT):
        total += short_ref[stream, tap : tap + 1] * ext_ref[stream, start - tap : start - tap + rows]
    return total


def convolve(before, now, sign, inv, cos_h, sin_h, alt_h):
    window = before + sign * now
    cos_x, sin_x = window[:LONG], window[LONG:]
    product = jnp.concatenate(
        [cos_x * cos_h - sin_x * sin_h, cos_x * sin_h + sin_x * alt_h], axis=0
    )
    return back(inv, product)


def forward_kernel(valid_ref, qkv_ref, short_ref, long_ref, fwd_ref, inv_ref, *refs):
    mix_ref, turned_ref, q_ref, k_ref, v_ref, conv_ref, gate_ref, ext_ref = refs[-8:]
    valid = valid_ref[0]
    ext_ref[:, 0:RIM] = jnp.zeros((3, RIM, LANES), F32)
    for start in range(0, ROWS, STEP):
        live = live_rows(valid, start, STEP)
        for stream in range(3):
            ext_ref[stream, RIM + start : RIM + start + STEP] = (
                qkv_ref[stream, start : start + STEP].astype(F32) * live
            )
    for start in range(0, ROWS, STEP):
        k_side = filtered(short_ref, ext_ref, 1, RIM + start, STEP)
        v_side = filtered(short_ref, ext_ref, 2, RIM + start, STEP)
        k_ref[start : start + STEP] = k_side
        v_ref[start : start + STEP] = v_side
        q_ref[start : start + STEP] = filtered(short_ref, ext_ref, 0, RIM + start, STEP)
        gate_ref[start : start + STEP] = (k_side * v_side).astype(BF16)
    fwd = fwd_ref[...]
    inv = inv_ref[...]
    taps = filter_spectrum(fwd, long_ref[...])
    sign = signs(2 * LONG)
    before = spectrum(fwd, gate_ref[LONG : 2 * LONG])
    for start in range(2 * LONG, ROWS, LONG):
        now = spectrum(fwd, gate_ref[start : start + LONG])
        conv = convolve(before, now, sign, inv, *taps)
        before = now
        conv_ref[start : start + LONG] = conv
        mix_in = live_rows(valid, start, LONG) * q_ref[start : start + LONG] * conv
        mix_ref[start : start + LONG] = mix_in.astype(BF16)
        turned_ref[:, start : start + LONG] = mix_in.T.astype(BF16)


def finish_kernel(
    valid_ref, qkv_ref, halo_ref, short_ref, long_ref, fwd_ref, inv_ref, q_in, k_in, v_in, gate_in, *refs
):
    mix_ref, turned_ref, q_ref, k_ref, v_ref, conv_ref, ext_ref, gate_ref = refs[-8:]
    valid = valid_ref[0]
    ext_ref[0, TAIL - RIM : TAIL] = halo_ref[0:RIM].astype(F32)
    ext_ref[1, 0:TAIL] = halo_ref[RIM : RIM + TAIL].astype(F32)
    ext_ref[2, 0:TAIL] = halo_ref[RIM + TAIL : RIM + 2 * TAIL].astype(F32)
    live = live_rows(valid, 0, RIM)
    for stream in range(3):
        ext_ref[stream, TAIL : TAIL + RIM] = qkv_ref[stream].astype(F32) * live
    for start in range(0, LONG, STEP):
        k_side = filtered(short_ref, ext_ref, 1, RIM + start, STEP)
        v_side = filtered(short_ref, ext_ref, 2, RIM + start, STEP)
        gate_ref[start : start + STEP] = (k_side * v_side).astype(BF16)
    q_rim = filtered(short_ref, ext_ref, 0, TAIL, RIM)
    k_rim = filtered(short_ref, ext_ref, 1, TAIL, RIM)
    v_rim = filtered(short_ref, ext_ref, 2, TAIL, RIM)
    q_ref[...] = q_rim
    k_ref[...] = k_rim
    v_ref[...] = v_rim
    gate_ref[LONG : LONG + RIM] = (k_rim * v_rim).astype(BF16)
    gate_ref[LONG + RIM : 3 * LONG] = gate_in[RIM:]
    fwd = fwd_ref[...]
    inv = inv_ref[...]
    taps = filter_spectrum(fwd, long_ref[...])
    sign = signs(2 * LONG)
    before = spectrum(fwd, gate_ref[0:LONG])
    for start in range(0, 2 * LONG, LONG):
        now = spectrum(fwd, gate_ref[LONG + start : 2 * LONG + start])
        conv = convolve(before, now, sign, inv, *taps)
        before = now
        conv_ref[start : start + LONG] = conv
        q_side = q_in[start : start + LONG]
        if start == 0:
            q_side = jnp.concatenate([q_rim, q_side[RIM:]], axis=0)
        mix_in = live_rows(valid, start, LONG) * q_side * conv
        mix_ref[start : start + LONG] = mix_in.astype(BF16)
        turned_ref[:, start : start + LONG] = mix_in.T.astype(BF16)


def backward_kernel(
    valid_ref, dconv_ref, msg_ref, dq_ref, k_ref, v_ref, short_ref, long_ref, fwd_ref, inv_ref,
    *refs,
):
    out_ref, ext_ref, gate_ref = refs[-3:]
    valid = valid_ref[0]
    fwd = fwd_ref[...]
    inv = inv_ref[...]
    gate_ref[0:TAIL] = msg_ref[0:TAIL]
    gate_ref[TAIL : 2 * LONG] = jnp.zeros((2 * LONG - TAIL, LANES), BF16)
    cos_h, sin_h, alt_h = filter_spectrum(fwd, long_ref[...])
    sign = signs(2 * LONG)
    blocks = ROWS // LONG
    ext_ref[0, 0:ROWS] = dq_ref[...]
    ext_ref[0, ROWS : ROWS + RIM] = msg_ref[TAIL : TAIL + RIM].astype(F32)
    now = spectrum(fwd, dconv_ref[0:LONG])
    for block in range(blocks + 1):
        start = block * LONG
        if block + 1 < blocks:
            after = spectrum(fwd, dconv_ref[start + LONG : start + 2 * LONG])
        else:
            rim = (block + 1 - blocks) * LONG
            after = spectrum(fwd, gate_ref[rim : rim + LONG])
        window = now + sign * after
        now = after
        cos_x, sin_x = window[:LONG], window[LONG:]
        product = jnp.concatenate(
            [cos_x * cos_h + sin_x * sin_h, sin_x * alt_h - cos_x * sin_h], axis=0
        )
        gated = back(inv, product)
        if block < blocks:
            ext_ref[1, start : start + LONG] = gated * v_ref[start : start + LONG]
            ext_ref[2, start : start + LONG] = gated * k_ref[start : start + LONG]
        else:
            rim = gated[:RIM]
            v_rim = msg_ref[TAIL + RIM : TAIL + 2 * RIM].astype(F32)
            k_rim = msg_ref[TAIL + 2 * RIM : TAIL + 3 * RIM].astype(F32)
            ext_ref[1, ROWS : ROWS + RIM] = rim * v_rim
            ext_ref[2, ROWS : ROWS + RIM] = rim * k_rim
    for start in range(0, ROWS, STEP):
        live = live_rows(valid, start, STEP)
        for stream in range(3):
            total = short_ref[stream, 0:1] * ext_ref[stream, start : start + STEP]
            for tap in range(1, SHORT):
                total += short_ref[stream, tap : tap + 1] * ext_ref[stream, start + tap : start + tap + STEP]
            out_ref[stream, start : start + STEP] = (total * live).astype(BF16)


def params(mib=20):
    return pltpu.CompilerParams(vmem_limit_bytes=mib * 2**20)


def cost(flops, moved):
    return pl.CostEstimate(flops=flops, bytes_accessed=moved, transcendentals=0)


SMEM = pl.BlockSpec(memory_space=pltpu.SMEM)
VMEM = pl.BlockSpec(memory_space=pltpu.VMEM)
ANY = pl.BlockSpec(memory_space=pl.ANY)


def lane_spec(*lead):
    return pl.BlockSpec(lead + (LANES,), lambda i: (0,) * len(lead) + (i,))


def whole(*shape):
    return pl.BlockSpec(shape, lambda i: (0,) * len(shape))


def forward_shapes():
    side = jax.ShapeDtypeStruct((ROWS, CH), F32)
    square = jax.ShapeDtypeStruct((ROWS, CH), BF16)
    return [square, square, side, side, side, side]


def run_forward(info, streams, short, long_taps, fwd, inv, after=()):
    return pl.pallas_call(
        forward_kernel,
        grid=(CH // LANES,),
        in_specs=[
            SMEM, lane_spec(3, ROWS), lane_spec(3, SHORT), lane_spec(LONG),
            whole(2 * LONG, 2 * LONG), whole(2 * LONG, 2 * LONG),
        ] + [ANY] * len(after),
        out_specs=[lane_spec(ROWS), pl.BlockSpec((LANES, ROWS), lambda i: (i, 0))] + [lane_spec(ROWS)] * 5,
        out_shape=forward_shapes() + [jax.ShapeDtypeStruct((ROWS, CH), BF16)],
        scratch_shapes=[pltpu.VMEM((3, RIM + ROWS, LANES), F32)],
        compiler_params=params(),
        cost_estimate=cost(1000, 1000),
        name="forward",
    )(info, streams, short, long_taps, fwd, inv, *after)


def run_finish(info, streams, halo, short, long_taps, fwd, inv, own, after=()):
    mix_in, turned, q_side, k_side, v_side, conv, gate = own
    top = lane_spec(2 * LONG)
    rim = lane_spec(RIM)
    return pl.pallas_call(
        finish_kernel,
        grid=(CH // LANES,),
        in_specs=[
            SMEM, lane_spec(3, RIM), lane_spec(RIM + 2 * TAIL), lane_spec(3, SHORT), lane_spec(LONG),
            whole(2 * LONG, 2 * LONG), whole(2 * LONG, 2 * LONG), top, rim, rim, top,
        ] + [ANY] * (3 + len(after)),
        out_specs=[top, pl.BlockSpec((LANES, 2 * LONG), lambda i: (i, 0)), rim, rim, rim, top],
        out_shape=forward_shapes(),
        input_output_aliases={7: 2, 8: 3, 9: 4, 11: 0, 12: 1, 13: 5},
        scratch_shapes=[
            pltpu.VMEM((3, TAIL + RIM, LANES), F32),
            pltpu.VMEM((3 * LONG, LANES), BF16),
        ],
        compiler_params=params(),
        cost_estimate=cost(1000, 1000),
        name="finish",
    )(info, streams, halo, short, long_taps, fwd, inv, q_side, k_side, v_side, gate, mix_in, turned, conv, *after)


def run_backward(valid, d_conv, msg, d_q, k_side, v_side, short, long_taps, fwd, inv, after=()):
    return pl.pallas_call(
        backward_kernel,
        grid=(CH // LANES,),
        in_specs=[
            SMEM, lane_spec(ROWS), lane_spec(TAIL + 3 * RIM), lane_spec(ROWS), lane_spec(ROWS),
            lane_spec(ROWS), lane_spec(3, SHORT), lane_spec(LONG),
            whole(2 * LONG, 2 * LONG), whole(2 * LONG, 2 * LONG),
        ] + [ANY] * len(after),
        out_specs=lane_spec(3, ROWS),
        out_shape=jax.ShapeDtypeStruct((3, ROWS, CH), BF16),
        scratch_shapes=[
            pltpu.VMEM((3, ROWS + RIM, LANES), F32),
            pltpu.VMEM((2 * LONG, LANES), BF16),
        ],
        compiler_params=params(),
        cost_estimate=cost(1000, 1000),
        name="backward",
    )(valid, d_conv, msg, d_q, k_side, v_side, short, long_taps, fwd, inv, *after)


def project_kernel(order_ref, mix_ref, weight_ref, *refs):
    out_ref = refs[-1]
    out_ref[0] = jnp.dot(mix_ref[...], weight_ref[...], preferred_element_type=F32).astype(BF16)


def block_at(other):
    return lambda i, info: (0, info[2 + other + 2 * ((0x0132 >> (4 * i)) & 15)])


def run_project(info, mix_in, weight, after=()):
    count = 4
    return pl.pallas_call(
        project_kernel,
        grid_spec=pltpu.PrefetchScalarGridSpec(
            num_scalar_prefetch=1,
            grid=(count,),
            in_specs=[
                pl.BlockSpec((ROWS, CH), lambda i, order: (0, 0)),
                pl.BlockSpec((CH, CH), block_at(1)),
            ] + [ANY] * len(after),
            out_specs=pl.BlockSpec((1, ROWS, CH), lambda i, order: (i, 0, 0)),
        ),
        out_shape=jax.ShapeDtypeStruct((count, ROWS, CH), BF16),
        compiler_params=params(),
        cost_estimate=cost(1000, 1000),
        name="project",
    )(info, mix_in, weight, *after)


def project_add_kernel(order_ref, mix_ref, weight_ref, other_ref, *refs):
    one_ref, two_ref, three_ref, own_ref = refs[-4:]
    step = pl.program_id(0)
    total = jnp.dot(mix_ref[...], weight_ref[...], preferred_element_type=F32)
    total += other_ref[0].astype(F32)
    for place, ref in enumerate((one_ref, two_ref, three_ref, own_ref)):

        @pl.when(step == place)
        def _(ref=ref):
            ref[...] = total.astype(ref.dtype)


def run_project_add(info, mix_in, weight, other, after=()):
    piece = jax.ShapeDtypeStruct((ROWS, CH), BF16)
    fixed = pl.BlockSpec((ROWS, CH), lambda i, order: (0, 0))
    return pl.pallas_call(
        project_add_kernel,
        grid_spec=pltpu.PrefetchScalarGridSpec(
            num_scalar_prefetch=1,
            grid=(4,),
            in_specs=[
                fixed,
                pl.BlockSpec((CH, CH), block_at(0)),
                pl.BlockSpec((1, ROWS, CH), lambda i, order: (i, 0, 0)),
            ] + [ANY] * len(after),
            out_specs=[fixed] * 4,
        ),
        out_shape=[piece, piece, piece, jax.ShapeDtypeStruct((ROWS, CH), F32)],
        compiler_params=params(),
        cost_estimate=cost(1000, 1000),
        name="project_add",
    )(info, mix_in, weight, other, *after)


def prepare_kernel(info_ref, qkv_ref, cot_ref, tail_ref, *refs):
    live = live_rows(info_ref[0], ROWS - TAIL, TAIL)[:, 0:1]
    place = 0
    for stream, rows in ((0, RIM), (1, TAIL), (2, TAIL)):
        masked = qkv_ref[stream, TAIL - rows :].astype(F32) * live[TAIL - rows :]
        tail_ref[place : place + rows] = masked.astype(BF16)
        place += rows
    for ahead, ref in enumerate(refs):
        column = pl.multiple_of(lax.rem(info_ref[1] + ahead, NX) * LANES, LANES)
        ref[...] = cot_ref[:, pl.ds(column, LANES)]


def run_prepare(info, streams, cotangent):
    return pl.pallas_call(
        prepare_kernel,
        in_specs=[SMEM, VMEM, VMEM],
        out_specs=[VMEM] * (1 + NX),
        out_shape=[jax.ShapeDtypeStruct((RIM + 2 * TAIL, CH), BF16)]
        + [jax.ShapeDtypeStruct((ROWS, LANES), BF16)] * NX,
        compiler_params=params(),
        cost_estimate=cost(1000, 1000),
        name="prepare",
    )(info, streams[:, ROWS - TAIL :], cotangent)


def outer_kernel(info_ref, *refs):
    turned, mine, theirs, outputs, work_ref = refs[0], refs[1], refs[2], refs[-1 - NZ : -1], refs[-1]
    for pair in range(NZ // 2):
        total = None
        for ahead in range(NX):
            both = jnp.concatenate([mine[pair, ahead], theirs[pair, ahead]], axis=1)
            part = jnp.dot(turned[lax.rem(info_ref[1] + NX - ahead, NX)], both, preferred_element_type=F32)
            total = part if total is None else total + part
        work_ref[info_ref[10 + 2 * pair]] = total[:, :LANES]
        work_ref[info_ref[11 + 2 * pair]] = total[:, LANES:]
    for ahead, ref in enumerate(outputs):
        ref[...] = work_ref[ahead].astype(ref.dtype)


def run_outer(info, turned, slabs, slabs_other, after=()):
    sent = jax.ShapeDtypeStruct((CH, LANES), BF16)
    return pl.pallas_call(
        outer_kernel,
        in_specs=[SMEM] + [VMEM] * 3 + [ANY] * len(after),
        out_specs=[VMEM] * NZ,
        out_shape=[jax.ShapeDtypeStruct((CH, LANES), F32)] + [sent] * (NZ - 1),
        scratch_shapes=[pltpu.VMEM((NZ, CH, LANES), F32)],
        compiler_params=params(),
        cost_estimate=cost(1000, 1000),
        name="outer",
    )(info, turned, slabs, slabs_other, *after)


def d_mix_kernel(info_ref, weight_ref, mine, theirs, q_ref, k_ref, v_ref, conv_ref, *refs):
    dconv_ref, dq_ref, msg_ref = refs[-3:]
    total = None
    for slot in range(2 * NY):
        column = pl.multiple_of(info_ref[2 + slot] * CH, CH)
        piece = (mine, theirs)[slot % 2][slot // 2]
        part = lax.dot_general(
            piece, weight_ref[:, pl.ds(column, CH)], (((1,), (1,)), ((), ())),
            preferred_element_type=F32,
        )
        total = part if total is None else total + part
    row = lax.broadcasted_iota(jnp.int32, (ROWS, CH), 0)
    d_mix = jnp.where(row < info_ref[0], total, 0.0)
    d_conv = (d_mix * q_ref[...]).astype(BF16)
    d_q = d_mix * conv_ref[...]
    dconv_ref[...] = d_conv
    dq_ref[...] = d_q
    msg_ref[0:TAIL] = d_conv[:TAIL]
    msg_ref[TAIL : TAIL + RIM] = d_q[:RIM].astype(BF16)
    msg_ref[TAIL + RIM : TAIL + 2 * RIM] = v_ref[0:RIM].astype(BF16)
    msg_ref[TAIL + 2 * RIM : TAIL + 3 * RIM] = k_ref[0:RIM].astype(BF16)


def run_d_mix(info, weight, mine, theirs, sides, after=()):
    return pl.pallas_call(
        d_mix_kernel,
        in_specs=[SMEM] + [VMEM] * 7 + [ANY] * len(after),
        out_specs=[VMEM] * 3,
        out_shape=[
            jax.ShapeDtypeStruct((ROWS, CH), BF16), jax.ShapeDtypeStruct((ROWS, CH), F32),
            jax.ShapeDtypeStruct((TAIL + 3 * RIM, CH), BF16),
        ],
        compiler_params=params(),
        cost_estimate=cost(1000, 1000),
        name="d_mix",
    )(info, weight, mine, theirs, *sides, *after)


def ctx_pairs(ahead_z, ahead_x):
    return [
        (z * NX + x, (z + ahead_z) % NZ * NX + (x + ahead_x) % NX) for z in range(NZ) for x in range(NX)
    ]


def along_x(array, ahead):
    return lax.ppermute(array, "ctx", ctx_pairs(0, ahead))


def along_z(array, ahead):
    return lax.ppermute(array, "ctx", ctx_pairs(ahead, 0))


def along_y(array, ahead):
    pairs = [(2 * y + core, 2 * ((y + ahead) % NY) + core) for y in range(NY) for core in range(2)]
    return lax.ppermute(array, "tp", pairs)


def other_core(array):
    return lax.ppermute(array, "tp", [(i, i ^ 1) for i in range(2 * NY)])


def neighbour(array, by):
    count = NZ * NX
    return lax.ppermute(array, "ctx", [(i, i + by) for i in range(count) if 0 <= i + by < count])


def local(qkv, short_filter, long_filter, out_weight, cotangent, valid_len):
    forward_table, causal_table, anti_table = (jnp.asarray(table) for table in tables())
    ctx, tp = lax.axis_index("ctx"), lax.axis_index("tp")
    z, x, y, core = ctx >> 2, ctx & 3, tp >> 1, tp & 1
    ahead = jnp.array([0, 0, -1, -1, 1, 1, 2, 2], jnp.int32)
    other = jnp.array([0, 1, 0, 1, 0, 1, 0, 1], jnp.int32)
    blocks = (((y + ahead) & 3) << 1) + ((core + other) & 1)
    info = jnp.concatenate([valid_len, x[None].astype(jnp.int32), blocks, (blocks - z) & 7])
    streams = qkv.transpose(1, 0, 2)
    short = short_filter.transpose(1, 0, 2)

    tail, *quarters = run_prepare(info, streams, cotangent)
    halo = neighbour(tail, 1)
    first, second, third = (along_x(quarters[ahead], ahead) for ahead in (1, 2, 3))
    below, above = along_y(cotangent, 1), along_y(cotangent, -1)
    own = run_forward(info, streams, short, long_filter, forward_table, causal_table, (tail,))
    first, second, third, halo, *own = lax.optimization_barrier([first, second, third, halo, *own])
    slab = jnp.stack([quarters[0], first, second, third])
    slabs = [slab] + [along_y(slab, ahead) for ahead in (1, -1, 2)]
    mix_in, turned, q_side, k_side, v_side, conv = run_finish(
        info, streams, halo, short, long_filter, forward_table, causal_table, own, (slab, below)
    )
    copies = jnp.broadcast_to(turned[None], (NX, CH, ROWS))
    turned = lax.all_to_all(
        copies, "ctx", 0, 0, axis_index_groups=[[z * NX + x for x in range(NX)] for z in range(NZ)], tiled=True
    )
    turned, above, mix_in, cotangent, *slabs = lax.optimization_barrier(
        [turned, above, mix_in, cotangent, *slabs]
    )
    slabs = jnp.stack(slabs)
    slabs_other = other_core(slabs)
    far = along_y(cotangent, 2)
    given = run_project(info, mix_in, out_weight)
    taken = other_core(given)
    total, *sent = run_outer(info, turned, slabs, slabs_other, (taken,))
    sums = [along_z(sent[ahead - 1], ahead) for ahead in (1, 7, 2, 6)]
    one, two, three, own_out = run_project_add(info, mix_in, out_weight, taken, (total,))
    arrived = [along_y(one, 1), along_y(three, 3)]
    far, below, above, sums[0], sums[1], two = lax.optimization_barrier(
        (far, below, above, sums[0], sums[1], two)
    )
    cots = jnp.stack([cotangent, below, above, far])
    cots_other = other_core(cots)
    d_conv, d_q, msg = run_d_mix(info, out_weight, cots, cots_other, (q_side, k_side, v_side, conv))
    msg = neighbour(msg, -1)
    arrived.append(along_y(two, 2))
    msg, *rest = lax.optimization_barrier([msg] + [sent[ahead - 1] for ahead in (3, 5, 4)])
    sums += [along_z(array, ahead) for array, ahead in zip(rest, (3, 5, 4))]

    d_streams = run_backward(
        info, d_conv, msg, d_q, k_side, v_side, short, long_filter, forward_table, anti_table
    )
    d_qkv = d_streams.transpose(1, 0, 2)
    mixed = own_out
    for array in arrived:
        mixed = mixed + array.astype(F32)
    mixed = mixed.astype(BF16)
    for array in sums:
        total = total + array.astype(F32)
    d_weight = total * (1.0 / jnp.sqrt(jnp.float32(ROWS * NZ * NX)))
    return mixed, d_qkv, d_weight


def solution(mesh):
    in_specs = (
        P("ctx", None, "tp"),
        P(None, None, "tp"),
        P(None, "tp"),
        P("tp", None),
        P("ctx", "tp"),
        P("ctx"),
    )
    out_specs = (P("ctx", "tp"), P("ctx", None, "tp"), P("tp", "ctx"))
    return jax.shard_map(local, mesh=mesh, in_specs=in_specs, out_specs=out_specs, check_vma=False)
```

```python
import functools

import jax
import jax.numpy as jnp
import ml_dtypes
import numpy as np
from jax import lax
from jax.experimental import pallas as pl
from jax.experimental.pallas import tpu as pltpu
from jax.sharding import PartitionSpec as P

SHORT = 7
LONG = 128
ROWS = 512
CH = 512
LANES = 128
TAIL = 144
RIM = 16
STEP = 64
NZ, NX, NY = 8, 4, 4
F32, BF16 = jnp.float32, jnp.bfloat16


def split_bf16(table):
    high = table.astype(ml_dtypes.bfloat16)
    low = (table - high.astype(np.float64)).astype(ml_dtypes.bfloat16)
    return high, low


def tables():
    size = 2 * LONG
    freq = np.arange(LONG)[:, None]
    angle = 2.0 * np.pi * freq * np.arange(size)[None, :] / size
    real = np.concatenate([np.cos(angle), np.sin(angle)], axis=0)
    real[LONG] = (-1.0) ** np.arange(size)
    high, low = split_bf16(real[:, :LONG])
    forward = np.concatenate([high, low], axis=1)
    weight = np.full((2 * LONG, 1), 2.0 / size)
    weight[0] = weight[LONG] = 1.0 / size
    inverse = (real * weight).T
    causal = np.concatenate(split_bf16(inverse[LONG:]), axis=0)
    anti = np.concatenate(split_bf16(inverse[:LONG]), axis=0)
    return forward, causal, anti


def signs(rows):
    row = lax.broadcasted_iota(jnp.int32, (rows, LANES), 0)
    return jnp.where(row % 2 == 0, 1.0, -1.0).astype(F32)


def spectrum(forward, block):
    return jnp.dot(forward, jnp.concatenate([block, block], axis=0), preferred_element_type=F32)


def filter_spectrum(forward, taps):
    both = spectrum(forward, taps)
    cos_part, sin_part = both[:LONG], both[LONG:]
    first = lax.broadcasted_iota(jnp.int32, (LONG, LANES), 0) == 0
    return cos_part, jnp.where(first, 0.0, sin_part), jnp.where(first, sin_part, cos_part)


def back(table, product):
    high = product.astype(BF16)
    low = (product - high.astype(F32)).astype(BF16)
    half = table.shape[0] // 2
    both = jnp.dot(table, high, preferred_element_type=F32)
    rest = jnp.dot(table[:half], low, preferred_element_type=F32)
    return both[:half] + both[half:] + rest


def live_rows(valid, start, rows):
    row = lax.broadcasted_iota(jnp.int32, (rows, LANES), 0) + start
    return jnp.where(row < valid, 1.0, 0.0).astype(F32)


def filtered(short_ref, ext_ref, stream, start, rows):
    total = short_ref[stream, 0:1] * ext_ref[stream, start : start + rows]
    for tap in range(1, SHORT):
        total += short_ref[stream, tap : tap + 1] * ext_ref[stream, start - tap : start - tap + rows]
    return total


def convolve(before, now, sign, inv, cos_h, sin_h, alt_h):
    window = before + sign * now
    cos_x, sin_x = window[:LONG], window[LONG:]
    product = jnp.concatenate(
        [cos_x * cos_h - sin_x * sin_h, cos_x * sin_h + sin_x * alt_h], axis=0
    )
    return back(inv, product)


def forward_kernel(valid_ref, qkv_ref, short_ref, long_ref, fwd_ref, inv_ref, *refs):
    mix_ref, turned_ref, q_ref, k_ref, v_ref, conv_ref, gate_ref, ext_ref = refs[-8:]
    valid = valid_ref[0]
    ext_ref[:, 0:RIM] = jnp.zeros((3, RIM, LANES), F32)
    for start in range(0, ROWS, STEP):
        live = live_rows(valid, start, STEP)
        for stream in range(3):
            ext_ref[stream, RIM + start : RIM + start + STEP] = (
                qkv_ref[stream, start : start + STEP].astype(F32) * live
            )
    for start in range(0, ROWS, STEP):
        k_side = filtered(short_ref, ext_ref, 1, RIM + start, STEP)
        v_side = filtered(short_ref, ext_ref, 2, RIM + start, STEP)
        k_ref[start : start + STEP] = k_side
        v_ref[start : start + STEP] = v_side
        q_ref[start : start + STEP] = filtered(short_ref, ext_ref, 0, RIM + start, STEP)
        gate_ref[start : start + STEP] = (k_side * v_side).astype(BF16)
    fwd = fwd_ref[...]
    inv = inv_ref[...]
    taps = filter_spectrum(fwd, long_ref[...])
    sign = signs(2 * LONG)
    before = spectrum(fwd, gate_ref[LONG : 2 * LONG])
    for start in range(2 * LONG, ROWS, LONG):
        now = spectrum(fwd, gate_ref[start : start + LONG])
        conv = convolve(before, now, sign, inv, *taps)
        before = now
        conv_ref[start : start + LONG] = conv
        mix_in = live_rows(valid, start, LONG) * q_ref[start : start + LONG] * conv
        mix_ref[start : start + LONG] = mix_in.astype(BF16)
        turned_ref[:, start : start + LONG] = mix_in.T.astype(BF16)


def finish_kernel(
    valid_ref, qkv_ref, halo_ref, short_ref, long_ref, fwd_ref, inv_ref, q_in, k_in, v_in, gate_in, *refs
):
    mix_ref, turned_ref, q_ref, k_ref, v_ref, conv_ref, ext_ref, gate_ref = refs[-8:]
    valid = valid_ref[0]
    ext_ref[0, TAIL - RIM : TAIL] = halo_ref[0:RIM].astype(F32)
    ext_ref[1, 0:TAIL] = halo_ref[RIM : RIM + TAIL].astype(F32)
    ext_ref[2, 0:TAIL] = halo_ref[RIM + TAIL : RIM + 2 * TAIL].astype(F32)
    live = live_rows(valid, 0, RIM)
    for stream in range(3):
        ext_ref[stream, TAIL : TAIL + RIM] = qkv_ref[stream].astype(F32) * live
    for start in range(0, LONG, STEP):
        k_side = filtered(short_ref, ext_ref, 1, RIM + start, STEP)
        v_side = filtered(short_ref, ext_ref, 2, RIM + start, STEP)
        gate_ref[start : start + STEP] = (k_side * v_side).astype(BF16)
    q_rim = filtered(short_ref, ext_ref, 0, TAIL, RIM)
    k_rim = filtered(short_ref, ext_ref, 1, TAIL, RIM)
    v_rim = filtered(short_ref, ext_ref, 2, TAIL, RIM)
    q_ref[...] = q_rim
    k_ref[...] = k_rim
    v_ref[...] = v_rim
    gate_ref[LONG : LONG + RIM] = (k_rim * v_rim).astype(BF16)
    gate_ref[LONG + RIM : 3 * LONG] = gate_in[RIM:]
    fwd = fwd_ref[...]
    inv = inv_ref[...]
    taps = filter_spectrum(fwd, long_ref[...])
    sign = signs(2 * LONG)
    before = spectrum(fwd, gate_ref[0:LONG])
    for start in range(0, 2 * LONG, LONG):
        now = spectrum(fwd, gate_ref[LONG + start : 2 * LONG + start])
        conv = convolve(before, now, sign, inv, *taps)
        before = now
        conv_ref[start : start + LONG] = conv
        q_side = q_in[start : start + LONG]
        if start == 0:
            q_side = jnp.concatenate([q_rim, q_side[RIM:]], axis=0)
        mix_in = live_rows(valid, start, LONG) * q_side * conv
        mix_ref[start : start + LONG] = mix_in.astype(BF16)
        turned_ref[:, start : start + LONG] = mix_in.T.astype(BF16)


def backward_kernel(
    valid_ref, dconv_ref, msg_ref, dq_ref, k_ref, v_ref, short_ref, long_ref, fwd_ref, inv_ref,
    *refs,
):
    out_ref, ext_ref, gate_ref = refs[-3:]
    valid = valid_ref[0]
    fwd = fwd_ref[...]
    inv = inv_ref[...]
    gate_ref[0:TAIL] = msg_ref[0:TAIL]
    gate_ref[TAIL : 2 * LONG] = jnp.zeros((2 * LONG - TAIL, LANES), BF16)
    cos_h, sin_h, alt_h = filter_spectrum(fwd, long_ref[...])
    sign = signs(2 * LONG)
    blocks = ROWS // LONG
    ext_ref[0, 0:ROWS] = dq_ref[...]
    ext_ref[0, ROWS : ROWS + RIM] = msg_ref[TAIL : TAIL + RIM].astype(F32)
    now = spectrum(fwd, dconv_ref[0:LONG])
    for block in range(blocks + 1):
        start = block * LONG
        if block + 1 < blocks:
            after = spectrum(fwd, dconv_ref[start + LONG : start + 2 * LONG])
        else:
            rim = (block + 1 - blocks) * LONG
            after = spectrum(fwd, gate_ref[rim : rim + LONG])
        window = now + sign * after
        now = after
        cos_x, sin_x = window[:LONG], window[LONG:]
        product = jnp.concatenate(
            [cos_x * cos_h + sin_x * sin_h, sin_x * alt_h - cos_x * sin_h], axis=0
        )
        gated = back(inv, product)
        if block < blocks:
            ext_ref[1, start : start + LONG] = gated * v_ref[start : start + LONG]
            ext_ref[2, start : start + LONG] = gated * k_ref[start : start + LONG]
        else:
            rim = gated[:RIM]
            v_rim = msg_ref[TAIL + RIM : TAIL + 2 * RIM].astype(F32)
            k_rim = msg_ref[TAIL + 2 * RIM : TAIL + 3 * RIM].astype(F32)
            ext_ref[1, ROWS : ROWS + RIM] = rim * v_rim
            ext_ref[2, ROWS : ROWS + RIM] = rim * k_rim
    for start in range(0, ROWS, STEP):
        live = live_rows(valid, start, STEP)
        for stream in range(3):
            total = short_ref[stream, 0:1] * ext_ref[stream, start : start + STEP]
            for tap in range(1, SHORT):
                total += short_ref[stream, tap : tap + 1] * ext_ref[stream, start + tap : start + tap + STEP]
            out_ref[stream, start : start + STEP] = (total * live).astype(BF16)


def params(mib=56):
    return pltpu.CompilerParams(vmem_limit_bytes=mib * 2**20)


def cost(flops, moved):
    return pl.CostEstimate(flops=flops, bytes_accessed=moved, transcendentals=0)


SMEM = pl.BlockSpec(memory_space=pltpu.SMEM)
VMEM = pl.BlockSpec(memory_space=pltpu.VMEM)
ANY = pl.BlockSpec(memory_space=pl.ANY)


def lane_spec(*lead):
    return pl.BlockSpec(lead + (LANES,), lambda i: (0,) * len(lead) + (i,))


def whole(*shape):
    return pl.BlockSpec(shape, lambda i: (0,) * len(shape))


def forward_shapes():
    side = jax.ShapeDtypeStruct((ROWS, CH), F32)
    square = jax.ShapeDtypeStruct((ROWS, CH), BF16)
    return [square, square, side, side, side, side]


def run_forward(info, streams, short, long_taps, fwd, inv, after=()):
    return pl.pallas_call(
        forward_kernel,
        grid=(CH // LANES,),
        in_specs=[
            SMEM, lane_spec(3, ROWS), lane_spec(3, SHORT), lane_spec(LONG),
            whole(2 * LONG, 2 * LONG), whole(2 * LONG, 2 * LONG),
        ] + [ANY] * len(after),
        out_specs=[lane_spec(ROWS), pl.BlockSpec((LANES, ROWS), lambda i: (i, 0))] + [lane_spec(ROWS)] * 5,
        out_shape=forward_shapes() + [jax.ShapeDtypeStruct((ROWS, CH), BF16)],
        scratch_shapes=[pltpu.VMEM((3, RIM + ROWS, LANES), F32)],
        compiler_params=params(),
        cost_estimate=cost(1000, 1000),
        name="forward",
    )(info, streams, short, long_taps, fwd, inv, *after)


def run_finish(info, streams, halo, short, long_taps, fwd, inv, own, after=()):
    mix_in, turned, q_side, k_side, v_side, conv, gate = own
    top = lane_spec(2 * LONG)
    rim = lane_spec(RIM)
    return pl.pallas_call(
        finish_kernel,
        grid=(CH // LANES,),
        in_specs=[
            SMEM, lane_spec(3, RIM), lane_spec(RIM + 2 * TAIL), lane_spec(3, SHORT), lane_spec(LONG),
            whole(2 * LONG, 2 * LONG), whole(2 * LONG, 2 * LONG), top, rim, rim, top,
        ] + [ANY] * (3 + len(after)),
        out_specs=[top, pl.BlockSpec((LANES, 2 * LONG), lambda i: (i, 0)), rim, rim, rim, top],
        out_shape=forward_shapes(),
        input_output_aliases={7: 2, 8: 3, 9: 4, 11: 0, 12: 1, 13: 5},
        scratch_shapes=[
            pltpu.VMEM((3, TAIL + RIM, LANES), F32),
            pltpu.VMEM((3 * LONG, LANES), BF16),
        ],
        compiler_params=params(),
        cost_estimate=cost(1000, 1000),
        name="finish",
    )(info, streams, halo, short, long_taps, fwd, inv, q_side, k_side, v_side, gate, mix_in, turned, conv, *after)


def run_backward(valid, d_conv, msg, d_q, k_side, v_side, short, long_taps, fwd, inv, after=()):
    return pl.pallas_call(
        backward_kernel,
        grid=(CH // LANES,),
        in_specs=[
            SMEM, lane_spec(ROWS), lane_spec(TAIL + 3 * RIM), lane_spec(ROWS), lane_spec(ROWS),
            lane_spec(ROWS), lane_spec(3, SHORT), lane_spec(LONG),
            whole(2 * LONG, 2 * LONG), whole(2 * LONG, 2 * LONG),
        ] + [ANY] * len(after),
        out_specs=lane_spec(3, ROWS),
        out_shape=jax.ShapeDtypeStruct((3, ROWS, CH), BF16),
        scratch_shapes=[
            pltpu.VMEM((3, ROWS + RIM, LANES), F32),
            pltpu.VMEM((2 * LONG, LANES), BF16),
        ],
        compiler_params=params(),
        cost_estimate=cost(1000, 1000),
        name="backward",
    )(valid, d_conv, msg, d_q, k_side, v_side, short, long_taps, fwd, inv, *after)


def project_kernel(order_ref, mix_ref, weight_ref, *refs):
    out_ref = refs[-1]
    out_ref[0] = jnp.dot(mix_ref[...], weight_ref[...], preferred_element_type=F32).astype(BF16)


def own_block(i, info):
    return 0, 2 * ((info[3] + 1 + i) & 3) + info[1]


def other_block(i, info):
    return 0, 2 * ((info[3] + 1 + i) & 3) + 1 - info[1]


def run_project(info, mix_in, weight, after=()):
    count = 4
    return pl.pallas_call(
        project_kernel,
        grid_spec=pltpu.PrefetchScalarGridSpec(
            num_scalar_prefetch=1,
            grid=(count,),
            in_specs=[
                pl.BlockSpec((ROWS, CH), lambda i, order: (0, 0)),
                pl.BlockSpec((CH, CH), other_block),
            ] + [ANY] * len(after),
            out_specs=pl.BlockSpec((1, ROWS, CH), lambda i, order: (i, 0, 0)),
        ),
        out_shape=jax.ShapeDtypeStruct((count, ROWS, CH), BF16),
        compiler_params=params(),
        cost_estimate=cost(1000, 1000),
        name="project",
    )(info, mix_in, weight, *after)


def project_add_kernel(info_ref, mix_ref, weight_ref, other_ref, *refs):
    total = jnp.dot(mix_ref[...], weight_ref[...], preferred_element_type=F32)
    total += other_ref[0].astype(F32)
    for place, ref in enumerate(refs[-NY:]):

        @pl.when(pl.program_id(0) == place)
        def _(ref=ref):
            ref[...] = total.astype(ref.dtype)


def run_project_add(info, mix_in, weight, other, after=()):
    fixed = pl.BlockSpec((ROWS, CH), lambda i, order: (0, 0))
    return pl.pallas_call(
        project_add_kernel,
        grid_spec=pltpu.PrefetchScalarGridSpec(
            num_scalar_prefetch=1,
            grid=(4,),
            in_specs=[
                fixed,
                pl.BlockSpec((CH, CH), own_block),
                pl.BlockSpec((1, ROWS, CH), lambda i, order: (i, 0, 0)),
            ] + [ANY] * len(after),
            out_specs=[fixed] * NY,
        ),
        out_shape=[jax.ShapeDtypeStruct((ROWS, CH), BF16)] * (NY - 1) + [jax.ShapeDtypeStruct((ROWS, CH), F32)],
        compiler_params=params(),
        cost_estimate=cost(1000, 1000),
        name="project_add",
    )(info, mix_in, weight, other, *after)


def prepare_kernel(info_ref, qkv_ref, cot_ref, tail_ref, quarter_ref):
    live = live_rows(info_ref[0], ROWS // 2, ROWS // 2)[:, 0:1]
    place = 0
    for stream, rows in ((0, RIM), (1, TAIL), (2, TAIL)):
        masked = qkv_ref[stream, ROWS // 2 - rows :].astype(F32) * live[ROWS // 2 - rows :]
        tail_ref[place : place + rows] = masked.astype(BF16)
        place += rows
    for quarter in range(NX):
        quarter_ref[quarter] = cot_ref[:, quarter * LANES : (quarter + 1) * LANES]


def run_prepare(info, streams, cotangent):
    return pl.pallas_call(
        prepare_kernel,
        grid=(1,),
        in_specs=[SMEM, pl.BlockSpec((3, ROWS // 2, CH), lambda i: (0, 1, 0)), whole(ROWS, CH)],
        out_specs=[whole(RIM + 2 * TAIL, CH), whole(NX, ROWS, LANES)],
        out_shape=[
            jax.ShapeDtypeStruct((RIM + 2 * TAIL, CH), BF16),
            jax.ShapeDtypeStruct((NX, ROWS, LANES), BF16),
        ],
        compiler_params=params(),
        cost_estimate=cost(1000, 1000),
        name="prepare",
    )(info, streams, cotangent)


def outer_kernel(info_ref, mine, theirs, *refs):
    turned, out_ref = refs[:NX], refs[-1]
    core = info_ref[1]
    for y in range(NY):
        total = None
        for behind in range(NX):
            x = (info_ref[2] - behind) & 3
            both = jnp.concatenate([mine[y, x], theirs[y, x]], axis=1)
            part = jnp.dot(turned[behind][...], both, preferred_element_type=F32)
            total = part if total is None else total + part
        out_ref[2 * y + core] = total[:, :LANES].astype(BF16)
        out_ref[2 * y + 1 - core] = total[:, LANES:].astype(BF16)


def run_outer(info, turned, mine, theirs, after=()):
    return pl.pallas_call(
        outer_kernel,
        in_specs=[SMEM] + [VMEM] * 6 + [ANY] * len(after),
        out_specs=VMEM,
        out_shape=jax.ShapeDtypeStruct((NZ, CH, LANES), BF16),
        compiler_params=params(),
        cost_estimate=cost(1000, 1000),
        name="outer",
    )(info, mine, theirs, *turned, *after)


def d_mix_kernel(info_ref, weight_ref, mine, theirs, q_ref, k_ref, v_ref, conv_ref, *refs):
    dconv_ref, dq_ref, msg_ref = refs[-3:]
    total = None
    for slot in range(2 * NY):
        ahead = (0, -1, 1, 2)[slot // 2]
        block = 2 * ((info_ref[3] + ahead) & 3) + (info_ref[1] if slot % 2 == 0 else 1 - info_ref[1])
        column = pl.multiple_of(block * CH, CH)
        piece = (mine, theirs)[slot % 2][slot // 2]
        part = lax.dot_general(
            piece, weight_ref[:, pl.ds(column, CH)], (((1,), (1,)), ((), ())),
            preferred_element_type=F32,
        )
        total = part if total is None else total + part
    row = lax.broadcasted_iota(jnp.int32, (ROWS, CH), 0)
    d_mix = jnp.where(row < info_ref[0], total, 0.0)
    d_conv = (d_mix * q_ref[...]).astype(BF16)
    d_q = d_mix * conv_ref[...]
    dconv_ref[...] = d_conv
    dq_ref[...] = d_q
    msg_ref[0:TAIL] = d_conv[:TAIL]
    msg_ref[TAIL : TAIL + RIM] = d_q[:RIM].astype(BF16)
    msg_ref[TAIL + RIM : TAIL + 2 * RIM] = v_ref[0:RIM].astype(BF16)
    msg_ref[TAIL + 2 * RIM : TAIL + 3 * RIM] = k_ref[0:RIM].astype(BF16)


def run_d_mix(info, weight, mine, theirs, sides, after=()):
    return pl.pallas_call(
        d_mix_kernel,
        in_specs=[SMEM] + [VMEM] * 7 + [ANY] * len(after),
        out_specs=[VMEM] * 3,
        out_shape=[
            jax.ShapeDtypeStruct((ROWS, CH), BF16), jax.ShapeDtypeStruct((ROWS, CH), F32),
            jax.ShapeDtypeStruct((TAIL + 3 * RIM, CH), BF16),
        ],
        compiler_params=params(),
        cost_estimate=cost(1000, 1000),
        name="d_mix",
    )(info, weight, mine, theirs, *sides, *after)


def exchange(array, axis):
    groups = {
        "x": [[z * NX + x for x in range(NX)] for z in range(NZ)],
        "z": [[z * NX + x for z in range(NZ)] for x in range(NX)],
        "y": [[2 * y + core for y in range(NY)] for core in range(2)],
    }[axis]
    return lax.all_to_all(
        array, "tp" if axis == "y" else "ctx", 0, 0, axis_index_groups=groups, tiled=True
    )


def along_x(array, ahead):
    pairs = [(i, i // NX * NX + (i + ahead) % NX) for i in range(NZ * NX)]
    return lax.ppermute(array, "ctx", pairs)


def along_y(array, ahead):
    pairs = [(i, (i + 2 * ahead) % (2 * NY)) for i in range(2 * NY)]
    return lax.ppermute(array, "tp", pairs)


def copies(array):
    return jnp.broadcast_to(array[None], (NY, *array.shape))


def other_core(array):
    return lax.ppermute(array, "tp", [(i, i ^ 1) for i in range(2 * NY)])


def neighbour(array, by):
    count = NZ * NX
    return lax.ppermute(array, "ctx", [(i, i + by) for i in range(count) if 0 <= i + by < count])


def local(qkv, short_filter, long_filter, out_weight, cotangent, valid_len):
    forward_table, causal_table, anti_table = (jnp.asarray(table) for table in tables())
    ctx, tp = lax.axis_index("ctx"), lax.axis_index("tp")
    info = jnp.stack([valid_len[0], tp & 1, ctx & 3, tp >> 1])
    streams = qkv.transpose(1, 0, 2)
    short = short_filter.transpose(1, 0, 2)

    below, above = along_y(cotangent, 1), along_y(cotangent, -1)
    tail, quarters = run_prepare(info, streams, cotangent)
    halo = neighbour(tail, 1)
    slab = exchange(quarters, "x")
    own = run_forward(info, streams, short, long_filter, forward_table, causal_table, (tail,))
    slab, halo, below, above, *own = lax.optimization_barrier([slab, halo, below, above, *own])
    slab_copies = copies(slab)
    mine = exchange(slab_copies, "y").reshape(NY, NX, ROWS, LANES)
    mix_in, turned, q_side, k_side, v_side, conv = run_finish(
        info, streams, halo, short, long_filter, forward_table, causal_table, own, (slab_copies,)
    )
    turned = [turned] + [along_x(turned, ahead) for ahead in (1, 2, 3)]
    mine, cotangent, mix_in, *turned = lax.optimization_barrier([mine, cotangent, mix_in, *turned])
    theirs = other_core(mine)
    far = along_y(cotangent, 2)
    given = run_project(info, mix_in, out_weight)
    sums = run_outer(info, turned, mine, theirs, (given,))
    taken = other_core(given)
    far, taken, mix_in, sums = lax.optimization_barrier((far, taken, mix_in, sums))
    one, two, three, own_out = run_project_add(info, mix_in, out_weight, taken)
    sums = exchange(sums, "z")
    cots = jnp.stack([cotangent, below, above, far])
    cots_other = other_core(cots)
    arrived = [along_y(one, 1), along_y(two, 2), along_y(three, 3)]
    d_conv, d_q, msg = run_d_mix(info, out_weight, cots, cots_other, (q_side, k_side, v_side, conv))
    msg = neighbour(msg, -1)
    d_streams = run_backward(
        info, d_conv, msg, d_q, k_side, v_side, short, long_filter, forward_table, anti_table
    )
    sums, d_streams = lax.optimization_barrier((sums, d_streams))
    d_qkv = d_streams.transpose(1, 0, 2)
    mixed = own_out
    for array in arrived:
        mixed = mixed + array.astype(F32)
    mixed = mixed.astype(BF16)
    d_weight = jnp.sum(sums.astype(F32), axis=0) * (1.0 / jnp.sqrt(jnp.float32(ROWS * NZ * NX)))
    return mixed, d_qkv, d_weight


def solution(mesh):
    in_specs = (
        P("ctx", None, "tp"),
        P(None, None, "tp"),
        P(None, "tp"),
        P("tp", None),
        P("ctx", "tp"),
        P("ctx"),
    )
    out_specs = (P("ctx", "tp"), P("ctx", None, "tp"), P("tp", "ctx"))
    return jax.shard_map(local, mesh=mesh, in_specs=in_specs, out_specs=out_specs, check_vma=False)
```

```python
import functools

import jax
import jax.numpy as jnp
import ml_dtypes
import numpy as np
from jax import lax
from jax.experimental import pallas as pl
from jax.experimental.pallas import tpu as pltpu
from jax.sharding import PartitionSpec as P

SHORT = 7
LONG = 128
ROWS = 512
CH = 512
LANES = 128
TAIL = 144
RIM = 16
STEP = 64
NZ, NX, NY = 8, 4, 4
HALF = ROWS // 2
F32, BF16 = jnp.float32, jnp.bfloat16


def split_bf16(table):
    high = table.astype(ml_dtypes.bfloat16)
    low = (table - high.astype(np.float64)).astype(ml_dtypes.bfloat16)
    return high, low


def tables():
    size = 2 * LONG
    freq = np.arange(LONG)[:, None]
    angle = 2.0 * np.pi * freq * np.arange(size)[None, :] / size
    real = np.concatenate([np.cos(angle), np.sin(angle)], axis=0)
    real[LONG] = (-1.0) ** np.arange(size)
    high, low = split_bf16(real[:, :LONG])
    forward = np.concatenate([high, low], axis=1)
    weight = np.full((2 * LONG, 1), 2.0 / size)
    weight[0] = weight[LONG] = 1.0 / size
    inverse = (real * weight).T
    causal = np.concatenate(split_bf16(inverse[LONG:]), axis=0)
    anti = np.concatenate(split_bf16(inverse[:LONG]), axis=0)
    return forward, causal, anti


def signs(rows):
    row = lax.broadcasted_iota(jnp.int32, (rows, LANES), 0)
    return jnp.where(row % 2 == 0, 1.0, -1.0).astype(F32)


def spectrum(forward, block):
    return jnp.dot(forward, jnp.concatenate([block, block], axis=0), preferred_element_type=F32)


def filter_spectrum(forward, taps):
    both = spectrum(forward, taps)
    cos_part, sin_part = both[:LONG], both[LONG:]
    first = lax.broadcasted_iota(jnp.int32, (LONG, LANES), 0) == 0
    return cos_part, jnp.where(first, 0.0, sin_part), jnp.where(first, sin_part, cos_part)


def back(table, product):
    high = product.astype(BF16)
    low = (product - high.astype(F32)).astype(BF16)
    half = table.shape[0] // 2
    both = jnp.dot(table, high, preferred_element_type=F32)
    rest = jnp.dot(table[:half], low, preferred_element_type=F32)
    return both[:half] + both[half:] + rest


def live_rows(valid, start, rows):
    row = lax.broadcasted_iota(jnp.int32, (rows, LANES), 0) + start
    return jnp.where(row < valid, 1.0, 0.0).astype(F32)


def filtered(short_ref, ext_ref, stream, start, rows):
    total = short_ref[stream, 0:1] * ext_ref[stream, start : start + rows]
    for tap in range(1, SHORT):
        total += short_ref[stream, tap : tap + 1] * ext_ref[stream, start - tap : start - tap + rows]
    return total


def convolve(before, now, sign, inv, cos_h, sin_h, alt_h):
    window = before + sign * now
    cos_x, sin_x = window[:LONG], window[LONG:]
    product = jnp.concatenate(
        [cos_x * cos_h - sin_x * sin_h, cos_x * sin_h + sin_x * alt_h], axis=0
    )
    return back(inv, product)


def forward_kernel(valid_ref, qkv_ref, short_ref, long_ref, fwd_ref, inv_ref, *refs):
    mix_ref, turned_ref, q_ref, k_ref, v_ref, conv_ref, gate_ref, ext_ref = refs[-8:]
    valid = valid_ref[0]
    ext_ref[:, 0:RIM] = jnp.zeros((3, RIM, LANES), F32)
    for start in range(0, ROWS, STEP):
        live = live_rows(valid, start, STEP)
        for stream in range(3):
            ext_ref[stream, RIM + start : RIM + start + STEP] = (
                qkv_ref[stream, start : start + STEP].astype(F32) * live
            )
    for start in range(0, ROWS, STEP):
        k_side = filtered(short_ref, ext_ref, 1, RIM + start, STEP)
        v_side = filtered(short_ref, ext_ref, 2, RIM + start, STEP)
        k_ref[start : start + STEP] = k_side
        v_ref[start : start + STEP] = v_side
        q_ref[start : start + STEP] = filtered(short_ref, ext_ref, 0, RIM + start, STEP)
        gate_ref[start : start + STEP] = (k_side * v_side).astype(BF16)
    fwd = fwd_ref[...]
    inv = inv_ref[...]
    taps = filter_spectrum(fwd, long_ref[...])
    sign = signs(2 * LONG)
    before = spectrum(fwd, gate_ref[LONG : 2 * LONG])
    for start in range(2 * LONG, ROWS, LONG):
        now = spectrum(fwd, gate_ref[start : start + LONG])
        conv = convolve(before, now, sign, inv, *taps)
        before = now
        conv_ref[start : start + LONG] = conv
        mix_in = live_rows(valid, start, LONG) * q_ref[start : start + LONG] * conv
        mix_ref[start : start + LONG] = mix_in.astype(BF16)
        turned_ref[:, start : start + LONG] = mix_in.T.astype(BF16)


def finish_kernel(
    valid_ref, qkv_ref, halo_ref, short_ref, long_ref, fwd_ref, inv_ref, q_in, k_in, v_in, gate_in, *refs
):
    mix_ref, turned_ref, q_ref, k_ref, v_ref, conv_ref, ext_ref, gate_ref = refs[-8:]
    valid = valid_ref[0]
    ext_ref[0, TAIL - RIM : TAIL] = halo_ref[0:RIM].astype(F32)
    ext_ref[1, 0:TAIL] = halo_ref[RIM : RIM + TAIL].astype(F32)
    ext_ref[2, 0:TAIL] = halo_ref[RIM + TAIL : RIM + 2 * TAIL].astype(F32)
    live = live_rows(valid, 0, RIM)
    for stream in range(3):
        ext_ref[stream, TAIL : TAIL + RIM] = qkv_ref[stream].astype(F32) * live
    for start in range(0, LONG, STEP):
        k_side = filtered(short_ref, ext_ref, 1, RIM + start, STEP)
        v_side = filtered(short_ref, ext_ref, 2, RIM + start, STEP)
        gate_ref[start : start + STEP] = (k_side * v_side).astype(BF16)
    q_rim = filtered(short_ref, ext_ref, 0, TAIL, RIM)
    k_rim = filtered(short_ref, ext_ref, 1, TAIL, RIM)
    v_rim = filtered(short_ref, ext_ref, 2, TAIL, RIM)
    q_ref[...] = q_rim
    k_ref[...] = k_rim
    v_ref[...] = v_rim
    gate_ref[LONG : LONG + RIM] = (k_rim * v_rim).astype(BF16)
    gate_ref[LONG + RIM : 3 * LONG] = gate_in[RIM:]
    fwd = fwd_ref[...]
    inv = inv_ref[...]
    taps = filter_spectrum(fwd, long_ref[...])
    sign = signs(2 * LONG)
    before = spectrum(fwd, gate_ref[0:LONG])
    for start in range(0, 2 * LONG, LONG):
        now = spectrum(fwd, gate_ref[LONG + start : 2 * LONG + start])
        conv = convolve(before, now, sign, inv, *taps)
        before = now
        conv_ref[start : start + LONG] = conv
        q_side = q_in[start : start + LONG]
        if start == 0:
            q_side = jnp.concatenate([q_rim, q_side[RIM:]], axis=0)
        mix_in = live_rows(valid, start, LONG) * q_side * conv
        mix_ref[start : start + LONG] = mix_in.astype(BF16)
        turned_ref[:, start : start + LONG] = mix_in.T.astype(BF16)


def backward_kernel(
    valid_ref, dconv_ref, msg_ref, dq_ref, k_ref, v_ref, short_ref, long_ref, fwd_ref, inv_ref,
    *refs,
):
    out_ref, ext_ref, gate_ref = refs[-3:]
    valid = valid_ref[0]
    fwd = fwd_ref[...]
    inv = inv_ref[...]
    gate_ref[0:TAIL] = msg_ref[0:TAIL]
    gate_ref[TAIL : 2 * LONG] = jnp.zeros((2 * LONG - TAIL, LANES), BF16)
    cos_h, sin_h, alt_h = filter_spectrum(fwd, long_ref[...])
    sign = signs(2 * LONG)
    blocks = ROWS // LONG
    ext_ref[0, 0:ROWS] = dq_ref[...]
    ext_ref[0, ROWS : ROWS + RIM] = msg_ref[TAIL : TAIL + RIM].astype(F32)
    now = spectrum(fwd, dconv_ref[0:LONG])
    for block in range(blocks + 1):
        start = block * LONG
        if block + 1 < blocks:
            after = spectrum(fwd, dconv_ref[start + LONG : start + 2 * LONG])
        else:
            rim = (block + 1 - blocks) * LONG
            after = spectrum(fwd, gate_ref[rim : rim + LONG])
        window = now + sign * after
        now = after
        cos_x, sin_x = window[:LONG], window[LONG:]
        product = jnp.concatenate(
            [cos_x * cos_h + sin_x * sin_h, sin_x * alt_h - cos_x * sin_h], axis=0
        )
        gated = back(inv, product)
        if block < blocks:
            ext_ref[1, start : start + LONG] = gated * v_ref[start : start + LONG]
            ext_ref[2, start : start + LONG] = gated * k_ref[start : start + LONG]
        else:
            rim = gated[:RIM]
            v_rim = msg_ref[TAIL + RIM : TAIL + 2 * RIM].astype(F32)
            k_rim = msg_ref[TAIL + 2 * RIM : TAIL + 3 * RIM].astype(F32)
            ext_ref[1, ROWS : ROWS + RIM] = rim * v_rim
            ext_ref[2, ROWS : ROWS + RIM] = rim * k_rim
    for start in range(0, ROWS, STEP):
        live = live_rows(valid, start, STEP)
        for stream in range(3):
            total = short_ref[stream, 0:1] * ext_ref[stream, start : start + STEP]
            for tap in range(1, SHORT):
                total += short_ref[stream, tap : tap + 1] * ext_ref[stream, start + tap : start + tap + STEP]
            out_ref[stream, start : start + STEP] = (total * live).astype(BF16)


def params(mib=20):
    return pltpu.CompilerParams(vmem_limit_bytes=mib * 2**20)


def cost(flops, moved):
    return pl.CostEstimate(flops=flops, bytes_accessed=moved, transcendentals=0)


SMEM = pl.BlockSpec(memory_space=pltpu.SMEM)
VMEM = pl.BlockSpec(memory_space=pltpu.VMEM)
ANY = pl.BlockSpec(memory_space=pl.ANY)


def lane_spec(*lead):
    return pl.BlockSpec(lead + (LANES,), lambda i: (0,) * len(lead) + (i,))


def whole(*shape):
    return pl.BlockSpec(shape, lambda i: (0,) * len(shape))


def forward_shapes():
    side = jax.ShapeDtypeStruct((ROWS, CH), F32)
    square = jax.ShapeDtypeStruct((ROWS, CH), BF16)
    return [square, square, side, side, side, side]


def run_forward(info, streams, short, long_taps, fwd, inv, after=()):
    return pl.pallas_call(
        forward_kernel,
        grid=(CH // LANES,),
        in_specs=[
            SMEM, lane_spec(3, ROWS), lane_spec(3, SHORT), lane_spec(LONG),
            whole(2 * LONG, 2 * LONG), whole(2 * LONG, 2 * LONG),
        ] + [ANY] * len(after),
        out_specs=[lane_spec(ROWS), pl.BlockSpec((LANES, ROWS), lambda i: (i, 0))] + [lane_spec(ROWS)] * 5,
        out_shape=forward_shapes() + [jax.ShapeDtypeStruct((ROWS, CH), BF16)],
        scratch_shapes=[pltpu.VMEM((3, RIM + ROWS, LANES), F32)],
        compiler_params=params(56),
        cost_estimate=cost(1000, 1000),
        name="forward",
    )(info, streams, short, long_taps, fwd, inv, *after)


def run_finish(info, streams, halo, short, long_taps, fwd, inv, own, after=()):
    mix_in, turned, q_side, k_side, v_side, conv, gate = own
    top = lane_spec(2 * LONG)
    rim = lane_spec(RIM)
    return pl.pallas_call(
        finish_kernel,
        grid=(CH // LANES,),
        in_specs=[
            SMEM, lane_spec(3, RIM), lane_spec(RIM + 2 * TAIL), lane_spec(3, SHORT), lane_spec(LONG),
            whole(2 * LONG, 2 * LONG), whole(2 * LONG, 2 * LONG), top, rim, rim, top,
        ] + [ANY] * (3 + len(after)),
        out_specs=[top, pl.BlockSpec((LANES, 2 * LONG), lambda i: (i, 0)), rim, rim, rim, top],
        out_shape=forward_shapes(),
        input_output_aliases={7: 2, 8: 3, 9: 4, 11: 0, 12: 1, 13: 5},
        scratch_shapes=[
            pltpu.VMEM((3, TAIL + RIM, LANES), F32),
            pltpu.VMEM((3 * LONG, LANES), BF16),
        ],
        compiler_params=params(56),
        cost_estimate=cost(1000, 1000),
        name="finish",
    )(info, streams, halo, short, long_taps, fwd, inv, q_side, k_side, v_side, gate, mix_in, turned, conv, *after)


def run_backward(valid, d_conv, msg, d_q, k_side, v_side, short, long_taps, fwd, inv, after=()):
    return pl.pallas_call(
        backward_kernel,
        grid=(CH // LANES,),
        in_specs=[
            SMEM, lane_spec(ROWS), lane_spec(TAIL + 3 * RIM), lane_spec(ROWS), lane_spec(ROWS),
            lane_spec(ROWS), lane_spec(3, SHORT), lane_spec(LONG),
            whole(2 * LONG, 2 * LONG), whole(2 * LONG, 2 * LONG),
        ] + [ANY] * len(after),
        out_specs=lane_spec(3, ROWS),
        out_shape=jax.ShapeDtypeStruct((3, ROWS, CH), BF16),
        scratch_shapes=[
            pltpu.VMEM((3, ROWS + RIM, LANES), F32),
            pltpu.VMEM((2 * LONG, LANES), BF16),
        ],
        compiler_params=params(56),
        cost_estimate=cost(1000, 1000),
        name="backward",
    )(valid, d_conv, msg, d_q, k_side, v_side, short, long_taps, fwd, inv, *after)


def project_kernel(order_ref, mix_ref, weight_ref, *refs):
    out_ref = refs[-1]
    out_ref[0] = jnp.dot(mix_ref[...], weight_ref[...], preferred_element_type=F32).astype(BF16)


def own_block(i, info):
    return 0, 2 * ((info[3] + 1 + i) & 3) + info[1]


def other_block(i, info):
    return 0, 2 * ((info[3] + 1 + i) & 3) + 1 - info[1]


def run_project(info, mix_in, weight, after=()):
    count = 4
    return pl.pallas_call(
        project_kernel,
        grid_spec=pltpu.PrefetchScalarGridSpec(
            num_scalar_prefetch=1,
            grid=(count,),
            in_specs=[
                pl.BlockSpec((ROWS, CH), lambda i, order: (0, 0)),
                pl.BlockSpec((CH, CH), other_block),
            ] + [ANY] * len(after),
            out_specs=pl.BlockSpec((1, ROWS, CH), lambda i, order: (i, 0, 0)),
        ),
        out_shape=jax.ShapeDtypeStruct((count, ROWS, CH), BF16),
        compiler_params=params(),
        cost_estimate=cost(1000, 1000),
        name="project",
    )(info, mix_in, weight, *after)


def project_add_kernel(info_ref, mix_ref, weight_ref, other_ref, *refs):
    total = jnp.dot(mix_ref[...], weight_ref[...], preferred_element_type=F32)
    total += other_ref[0].astype(F32)
    up_ref, down_ref, next_ref, last_ref, own_ref = refs[-5:]
    top, bottom = total[:HALF].astype(BF16), total[HALF:].astype(BF16)

    @pl.when(pl.program_id(0) == 0)
    def _():
        next_ref[...] = top
        up_ref[HALF:] = bottom

    @pl.when(pl.program_id(0) == 1)
    def _():
        up_ref[:HALF] = top
        down_ref[HALF:] = bottom

    @pl.when(pl.program_id(0) == 2)
    def _():
        down_ref[:HALF] = top
        last_ref[...] = bottom

    @pl.when(pl.program_id(0) == 3)
    def _():
        own_ref[...] = total


def run_project_add(info, mix_in, weight, other, after=()):
    fixed = pl.BlockSpec((ROWS, CH), lambda i, order: (0, 0))
    half = pl.BlockSpec((HALF, CH), lambda i, order: (0, 0))
    return pl.pallas_call(
        project_add_kernel,
        grid_spec=pltpu.PrefetchScalarGridSpec(
            num_scalar_prefetch=1,
            grid=(4,),
            in_specs=[
                fixed,
                pl.BlockSpec((CH, CH), own_block),
                pl.BlockSpec((1, ROWS, CH), lambda i, order: (i, 0, 0)),
            ] + [ANY] * len(after),
            out_specs=[fixed, fixed, half, half, fixed],
        ),
        out_shape=[jax.ShapeDtypeStruct((rows, CH), BF16) for rows in (ROWS, ROWS, HALF, HALF)]
        + [jax.ShapeDtypeStruct((ROWS, CH), F32)],
        compiler_params=params(),
        cost_estimate=cost(1000, 1000),
        name="project_add",
    )(info, mix_in, weight, other, *after)


def prepare_kernel(info_ref, qkv_ref, cot_ref, tail_ref, quarter_ref):
    live = live_rows(info_ref[0], ROWS // 2, ROWS // 2)[:, 0:1]
    place = 0
    for stream, rows in ((0, RIM), (1, TAIL), (2, TAIL)):
        masked = qkv_ref[stream, ROWS // 2 - rows :].astype(F32) * live[ROWS // 2 - rows :]
        tail_ref[place : place + rows] = masked.astype(BF16)
        place += rows
    for quarter in range(NX):
        quarter_ref[quarter] = cot_ref[:, quarter * LANES : (quarter + 1) * LANES]


def run_prepare(info, streams, cotangent):
    return pl.pallas_call(
        prepare_kernel,
        grid=(1,),
        in_specs=[SMEM, pl.BlockSpec((3, ROWS // 2, CH), lambda i: (0, 1, 0)), whole(ROWS, CH)],
        out_specs=[whole(RIM + 2 * TAIL, CH), whole(NX, ROWS, LANES)],
        out_shape=[
            jax.ShapeDtypeStruct((RIM + 2 * TAIL, CH), BF16),
            jax.ShapeDtypeStruct((NX, ROWS, LANES), BF16),
        ],
        compiler_params=params(),
        cost_estimate=cost(1000, 1000),
        name="prepare",
    )(info, streams, cotangent)


def outer_kernel(info_ref, mine, theirs, *refs):
    turned, out_ref = refs[:NX], refs[-1]
    core = info_ref[1]
    for y in range(NY):
        total = None
        for behind in range(NX):
            x = (info_ref[2] - behind) & 3
            both = jnp.concatenate([mine[y, x], theirs[y, x]], axis=1)
            part = jnp.dot(turned[behind][...], both, preferred_element_type=F32)
            total = part if total is None else total + part
        out_ref[2 * y + core] = total[:, :LANES].astype(BF16)
        out_ref[2 * y + 1 - core] = total[:, LANES:].astype(BF16)


def run_outer(info, turned, mine, theirs, after=()):
    return pl.pallas_call(
        outer_kernel,
        in_specs=[SMEM] + [VMEM] * 6 + [ANY] * len(after),
        out_specs=VMEM,
        out_shape=jax.ShapeDtypeStruct((NZ, CH, LANES), BF16),
        compiler_params=params(),
        cost_estimate=cost(1000, 1000),
        name="outer",
    )(info, mine, theirs, *turned, *after)


def d_mix_kernel(info_ref, weight_ref, mine, theirs, q_ref, k_ref, v_ref, conv_ref, *refs):
    dconv_ref, dq_ref, msg_ref = refs[-3:]
    total = None
    for slot in range(2 * NY):
        ahead = (0, -1, 1, 2)[slot // 2]
        block = 2 * ((info_ref[3] + ahead) & 3) + (info_ref[1] if slot % 2 == 0 else 1 - info_ref[1])
        column = pl.multiple_of(block * CH, CH)
        piece = (mine, theirs)[slot % 2][slot // 2]
        part = lax.dot_general(
            piece, weight_ref[:, pl.ds(column, CH)], (((1,), (1,)), ((), ())),
            preferred_element_type=F32,
        )
        total = part if total is None else total + part
    row = lax.broadcasted_iota(jnp.int32, (ROWS, CH), 0)
    d_mix = jnp.where(row < info_ref[0], total, 0.0)
    d_conv = (d_mix * q_ref[...]).astype(BF16)
    d_q = d_mix * conv_ref[...]
    dconv_ref[...] = d_conv
    dq_ref[...] = d_q
    msg_ref[0:TAIL] = d_conv[:TAIL]
    msg_ref[TAIL : TAIL + RIM] = d_q[:RIM].astype(BF16)
    msg_ref[TAIL + RIM : TAIL + 2 * RIM] = v_ref[0:RIM].astype(BF16)
    msg_ref[TAIL + 2 * RIM : TAIL + 3 * RIM] = k_ref[0:RIM].astype(BF16)


def run_d_mix(info, weight, mine, theirs, sides, after=()):
    return pl.pallas_call(
        d_mix_kernel,
        in_specs=[SMEM] + [VMEM] * 7 + [ANY] * len(after),
        out_specs=[VMEM] * 3,
        out_shape=[
            jax.ShapeDtypeStruct((ROWS, CH), BF16), jax.ShapeDtypeStruct((ROWS, CH), F32),
            jax.ShapeDtypeStruct((TAIL + 3 * RIM, CH), BF16),
        ],
        compiler_params=params(),
        cost_estimate=cost(1000, 1000),
        name="d_mix",
    )(info, weight, mine, theirs, *sides, *after)


def exchange(array, axis):
    groups = {
        "x": [[z * NX + x for x in range(NX)] for z in range(NZ)],
        "z": [[z * NX + x for z in range(NZ)] for x in range(NX)],
        "y": [[2 * y + core for y in range(NY)] for core in range(2)],
    }[axis]
    return lax.all_to_all(
        array, "tp" if axis == "y" else "ctx", 0, 0, axis_index_groups=groups, tiled=True
    )


def add(one, other):
    return (one.astype(F32) + other.astype(F32)).astype(BF16)


def along_x(array, ahead):
    pairs = [(i, i // NX * NX + (i + ahead) % NX) for i in range(NZ * NX)]
    return lax.ppermute(array, "ctx", pairs)


def along_y(array, ahead):
    pairs = [(i, (i + 2 * ahead) % (2 * NY)) for i in range(2 * NY)]
    return lax.ppermute(array, "tp", pairs)


def copies(array):
    return jnp.broadcast_to(array[None], (NY, *array.shape))


def other_core(array):
    return lax.ppermute(array, "tp", [(i, i ^ 1) for i in range(2 * NY)])


def neighbour(array, by):
    count = NZ * NX
    return lax.ppermute(array, "ctx", [(i, i + by) for i in range(count) if 0 <= i + by < count])


def local(qkv, short_filter, long_filter, out_weight, cotangent, valid_len):
    forward_table, causal_table, anti_table = (jnp.asarray(table) for table in tables())
    ctx, tp = lax.axis_index("ctx"), lax.axis_index("tp")
    info = jnp.stack([valid_len[0], tp & 1, ctx & 3, tp >> 1])
    streams = qkv.transpose(1, 0, 2)
    short = short_filter.transpose(1, 0, 2)

    below, above = along_y(cotangent, 1), along_y(cotangent, -1)
    tail, quarters = run_prepare(info, streams, cotangent)
    halo = neighbour(tail, 1)
    slab = exchange(quarters, "x")
    own = run_forward(info, streams, short, long_filter, forward_table, causal_table, (tail,))
    slab, halo, below, above, held, *own = lax.optimization_barrier([slab, halo, below, above, cotangent, *own])
    slab_copies = copies(slab)
    mine = exchange(slab_copies, "y").reshape(NY, NX, ROWS, LANES)
    mix_in, turned, q_side, k_side, v_side, conv = run_finish(
        info, streams, halo, short, long_filter, forward_table, causal_table, own, (slab_copies,)
    )
    turned = [turned] + [along_x(turned, ahead) for ahead in (1, 2, 3)]
    far = along_y(held, 2)
    turned[1], mix_in = lax.optimization_barrier((turned[1], mix_in))
    given = run_project(info, mix_in, out_weight)
    taken = other_core(given)
    mine, far, given, *turned = lax.optimization_barrier([mine, far, given, *turned])
    theirs = other_core(mine)
    cots = jnp.stack([cotangent, below, above, far])
    cots_other = other_core(cots)
    partial = run_outer(info, turned, mine, theirs)
    sums = exchange(partial, "z")
    up, down, next_top, last_bottom, own_out = run_project_add(info, mix_in, out_weight, taken, (partial,))
    from_below, from_above = along_y(up, 1), along_y(down, -1)
    d_conv, d_q, msg = run_d_mix(
        info, out_weight, cots, cots_other, (q_side, k_side, v_side, conv), (up,)
    )
    top = along_y(add(next_top, from_below[:HALF]), 1)
    bottom = along_y(add(last_bottom, from_above[HALF:]), -1)
    msg = neighbour(msg, -1)
    d_streams = run_backward(
        info, d_conv, msg, d_q, k_side, v_side, short, long_filter, forward_table, anti_table
    )
    sums, d_streams, own_out = lax.optimization_barrier((sums, d_streams, own_out))
    d_qkv = d_streams.transpose(1, 0, 2)
    top = own_out[:HALF] + top.astype(F32) + from_above[:HALF].astype(F32)
    bottom = own_out[HALF:] + bottom.astype(F32) + from_below[HALF:].astype(F32)
    mixed = jnp.concatenate([top, bottom], axis=0).astype(BF16)
    d_weight = jnp.sum(sums.astype(F32), axis=0) * (1.0 / jnp.sqrt(jnp.float32(ROWS * NZ * NX)))
    return mixed, d_qkv, d_weight


def solution(mesh):
    in_specs = (
        P("ctx", None, "tp"),
        P(None, None, "tp"),
        P(None, "tp"),
        P("tp", None),
        P("ctx", "tp"),
        P("ctx"),
    )
    out_specs = (P("ctx", "tp"), P("ctx", None, "tp"), P("tp", "ctx"))
    return jax.shard_map(local, mesh=mesh, in_specs=in_specs, out_specs=out_specs, check_vma=False)
```

```python
import functools

import jax
import jax.numpy as jnp
import ml_dtypes
import numpy as np
from jax import lax
from jax.experimental import pallas as pl
from jax.experimental.pallas import tpu as pltpu
from jax.sharding import PartitionSpec as P

SHORT = 7
LONG = 128
ROWS = 512
CH = 512
LANES = 128
TAIL = 144
RIM = 16
STEP = 64
NZ, NX, NY = 8, 4, 4
HALF = ROWS // 2
F32, BF16 = jnp.float32, jnp.bfloat16


def split_bf16(table):
    high = table.astype(ml_dtypes.bfloat16)
    low = (table - high.astype(np.float64)).astype(ml_dtypes.bfloat16)
    return high, low


def tables():
    size = 2 * LONG
    freq = np.arange(LONG)[:, None]
    angle = 2.0 * np.pi * freq * np.arange(size)[None, :] / size
    real = np.concatenate([np.cos(angle), np.sin(angle)], axis=0)
    real[LONG] = (-1.0) ** np.arange(size)
    high, low = split_bf16(real[:, :LONG])
    forward = np.concatenate([high, low], axis=1)
    weight = np.full((2 * LONG, 1), 2.0 / size)
    weight[0] = weight[LONG] = 1.0 / size
    inverse = (real * weight).T
    causal = np.concatenate(split_bf16(inverse[LONG:]), axis=0)
    anti = np.concatenate(split_bf16(inverse[:LONG]), axis=0)
    return forward, causal, anti


def signs(rows):
    row = lax.broadcasted_iota(jnp.int32, (rows, LANES), 0)
    return jnp.where(row % 2 == 0, 1.0, -1.0).astype(F32)


def spectrum(forward, block):
    return jnp.dot(forward, jnp.concatenate([block, block], axis=0), preferred_element_type=F32)


def filter_spectrum(forward, taps):
    both = spectrum(forward, taps)
    cos_part, sin_part = both[:LONG], both[LONG:]
    first = lax.broadcasted_iota(jnp.int32, (LONG, LANES), 0) == 0
    return cos_part, jnp.where(first, 0.0, sin_part), jnp.where(first, sin_part, cos_part)


def back(table, product):
    high = product.astype(BF16)
    low = (product - high.astype(F32)).astype(BF16)
    half = table.shape[0] // 2
    both = jnp.dot(table, high, preferred_element_type=F32)
    rest = jnp.dot(table[:half], low, preferred_element_type=F32)
    return both[:half] + both[half:] + rest


def live_rows(valid, start, rows):
    row = lax.broadcasted_iota(jnp.int32, (rows, LANES), 0) + start
    return jnp.where(row < valid, 1.0, 0.0).astype(F32)


def filtered(short_ref, ext_ref, stream, start, rows):
    total = short_ref[stream, 0:1] * ext_ref[stream, start : start + rows]
    for tap in range(1, SHORT):
        total += short_ref[stream, tap : tap + 1] * ext_ref[stream, start - tap : start - tap + rows]
    return total


def convolve(before, now, sign, inv, cos_h, sin_h, alt_h):
    window = before + sign * now
    cos_x, sin_x = window[:LONG], window[LONG:]
    product = jnp.concatenate(
        [cos_x * cos_h - sin_x * sin_h, cos_x * sin_h + sin_x * alt_h], axis=0
    )
    return back(inv, product)


def forward_kernel(valid_ref, qkv_ref, short_ref, long_ref, fwd_ref, inv_ref, *refs):
    mix_ref, turned_ref, q_ref, k_ref, v_ref, conv_ref, gate_ref, ext_ref = refs[-8:]
    valid = valid_ref[0]
    ext_ref[:, 0:RIM] = jnp.zeros((3, RIM, LANES), F32)
    for start in range(0, ROWS, STEP):
        live = live_rows(valid, start, STEP)
        for stream in range(3):
            ext_ref[stream, RIM + start : RIM + start + STEP] = (
                qkv_ref[stream, start : start + STEP].astype(F32) * live
            )
    for start in range(0, ROWS, STEP):
        k_side = filtered(short_ref, ext_ref, 1, RIM + start, STEP)
        v_side = filtered(short_ref, ext_ref, 2, RIM + start, STEP)
        k_ref[start : start + STEP] = k_side
        v_ref[start : start + STEP] = v_side
        q_ref[start : start + STEP] = filtered(short_ref, ext_ref, 0, RIM + start, STEP)
        gate_ref[start : start + STEP] = (k_side * v_side).astype(BF16)
    fwd = fwd_ref[...]
    inv = inv_ref[...]
    taps = filter_spectrum(fwd, long_ref[...])
    sign = signs(2 * LONG)
    before = spectrum(fwd, gate_ref[LONG : 2 * LONG])
    for start in range(2 * LONG, ROWS, LONG):
        now = spectrum(fwd, gate_ref[start : start + LONG])
        conv = convolve(before, now, sign, inv, *taps)
        before = now
        conv_ref[start : start + LONG] = conv
        mix_in = live_rows(valid, start, LONG) * q_ref[start : start + LONG] * conv
        mix_ref[start : start + LONG] = mix_in.astype(BF16)
        turned_ref[:, start : start + LONG] = mix_in.T.astype(BF16)


def finish_kernel(
    valid_ref, qkv_ref, halo_ref, short_ref, long_ref, fwd_ref, inv_ref, q_in, k_in, v_in, gate_in, *refs
):
    mix_ref, turned_ref, q_ref, k_ref, v_ref, conv_ref, ext_ref, gate_ref = refs[-8:]
    valid = valid_ref[0]
    ext_ref[0, TAIL - RIM : TAIL] = halo_ref[0:RIM].astype(F32)
    ext_ref[1, 0:TAIL] = halo_ref[RIM : RIM + TAIL].astype(F32)
    ext_ref[2, 0:TAIL] = halo_ref[RIM + TAIL : RIM + 2 * TAIL].astype(F32)
    live = live_rows(valid, 0, RIM)
    for stream in range(3):
        ext_ref[stream, TAIL : TAIL + RIM] = qkv_ref[stream].astype(F32) * live
    for start in range(0, LONG, STEP):
        k_side = filtered(short_ref, ext_ref, 1, RIM + start, STEP)
        v_side = filtered(short_ref, ext_ref, 2, RIM + start, STEP)
        gate_ref[start : start + STEP] = (k_side * v_side).astype(BF16)
    q_rim = filtered(short_ref, ext_ref, 0, TAIL, RIM)
    k_rim = filtered(short_ref, ext_ref, 1, TAIL, RIM)
    v_rim = filtered(short_ref, ext_ref, 2, TAIL, RIM)
    q_ref[...] = q_rim
    k_ref[...] = k_rim
    v_ref[...] = v_rim
    gate_ref[LONG : LONG + RIM] = (k_rim * v_rim).astype(BF16)
    gate_ref[LONG + RIM : 3 * LONG] = gate_in[RIM:]
    fwd = fwd_ref[...]
    inv = inv_ref[...]
    taps = filter_spectrum(fwd, long_ref[...])
    sign = signs(2 * LONG)
    before = spectrum(fwd, gate_ref[0:LONG])
    for start in range(0, 2 * LONG, LONG):
        now = spectrum(fwd, gate_ref[LONG + start : 2 * LONG + start])
        conv = convolve(before, now, sign, inv, *taps)
        before = now
        conv_ref[start : start + LONG] = conv
        q_side = q_in[start : start + LONG]
        if start == 0:
            q_side = jnp.concatenate([q_rim, q_side[RIM:]], axis=0)
        mix_in = live_rows(valid, start, LONG) * q_side * conv
        mix_ref[start : start + LONG] = mix_in.astype(BF16)
        turned_ref[:, start : start + LONG] = mix_in.T.astype(BF16)


def correlate(now, after, sign, inv, cos_h, sin_h, alt_h):
    window = now + sign * after
    cos_x, sin_x = window[:LONG], window[LONG:]
    product = jnp.concatenate(
        [cos_x * cos_h + sin_x * sin_h, sin_x * alt_h - cos_x * sin_h], axis=0
    )
    return back(inv, product)


def filter_back(valid, first, short_ref, ext_ref, out_ref):
    for start in range(0, HALF, STEP):
        live = live_rows(valid, first + start, STEP)
        for stream in range(3):
            total = short_ref[stream, 0:1] * ext_ref[stream, start : start + STEP]
            for tap in range(1, SHORT):
                total += short_ref[stream, tap : tap + 1] * ext_ref[stream, start + tap : start + tap + STEP]
            out_ref[stream, start : start + STEP] = (total * live).astype(BF16)


def backward_kernel(
    valid_ref, dconv_ref, dq_ref, k_ref, v_ref, short_ref, long_ref, fwd_ref, inv_ref, *refs
):
    out_ref, ext_ref = refs[-2:]
    fwd = fwd_ref[...]
    inv = inv_ref[...]
    taps = filter_spectrum(fwd, long_ref[...])
    sign = signs(2 * LONG)
    ext_ref[0, 0 : HALF + RIM] = dq_ref[0 : HALF + RIM]
    now = spectrum(fwd, dconv_ref[0:LONG])
    for start in range(0, HALF + LONG, LONG):
        after = spectrum(fwd, dconv_ref[start + LONG : start + 2 * LONG])
        gated = correlate(now, after, sign, inv, *taps)
        now = after
        rows = LONG if start < HALF else RIM
        ext_ref[1, start : start + rows] = gated[:rows] * v_ref[start : start + rows]
        ext_ref[2, start : start + rows] = gated[:rows] * k_ref[start : start + rows]
    filter_back(valid_ref[0], 0, short_ref, ext_ref, out_ref)


def backward_end_kernel(
    valid_ref, dconv_ref, msg_ref, dq_ref, k_ref, v_ref, short_ref, long_ref, fwd_ref, inv_ref, *refs
):
    out_ref, ext_ref, gate_ref = refs[-3:]
    fwd = fwd_ref[...]
    inv = inv_ref[...]
    taps = filter_spectrum(fwd, long_ref[...])
    sign = signs(2 * LONG)
    gate_ref[0:HALF] = dconv_ref[...]
    gate_ref[HALF : HALF + TAIL] = msg_ref[0:TAIL]
    gate_ref[HALF + TAIL : HALF + 2 * LONG] = jnp.zeros((2 * LONG - TAIL, LANES), BF16)
    ext_ref[0, 0:HALF] = dq_ref[...]
    ext_ref[0, HALF : HALF + RIM] = msg_ref[TAIL : TAIL + RIM].astype(F32)
    now = spectrum(fwd, gate_ref[0:LONG])
    for start in range(0, HALF + LONG, LONG):
        after = spectrum(fwd, gate_ref[start + LONG : start + 2 * LONG])
        gated = correlate(now, after, sign, inv, *taps)
        now = after
        if start < HALF:
            ext_ref[1, start : start + LONG] = gated * v_ref[start : start + LONG]
            ext_ref[2, start : start + LONG] = gated * k_ref[start : start + LONG]
        else:
            v_rim = msg_ref[TAIL + RIM : TAIL + 2 * RIM].astype(F32)
            k_rim = msg_ref[TAIL + 2 * RIM : TAIL + 3 * RIM].astype(F32)
            ext_ref[1, HALF : HALF + RIM] = gated[:RIM] * v_rim
            ext_ref[2, HALF : HALF + RIM] = gated[:RIM] * k_rim
    filter_back(valid_ref[0], HALF, short_ref, ext_ref, out_ref)


def params(mib=20):
    return pltpu.CompilerParams(vmem_limit_bytes=mib * 2**20)


def cost(flops, moved):
    return pl.CostEstimate(flops=flops, bytes_accessed=moved, transcendentals=0)


SMEM = pl.BlockSpec(memory_space=pltpu.SMEM)
VMEM = pl.BlockSpec(memory_space=pltpu.VMEM)
ANY = pl.BlockSpec(memory_space=pl.ANY)


def lane_spec(*lead):
    return pl.BlockSpec(lead + (LANES,), lambda i: (0,) * len(lead) + (i,))


def whole(*shape):
    return pl.BlockSpec(shape, lambda i: (0,) * len(shape))


def forward_shapes():
    side = jax.ShapeDtypeStruct((ROWS, CH), F32)
    square = jax.ShapeDtypeStruct((ROWS, CH), BF16)
    return [square, square, side, side, side, side]


def run_forward(info, streams, short, long_taps, fwd, inv, after=()):
    return pl.pallas_call(
        forward_kernel,
        grid=(CH // LANES,),
        in_specs=[
            SMEM, lane_spec(3, ROWS), lane_spec(3, SHORT), lane_spec(LONG),
            whole(2 * LONG, 2 * LONG), whole(2 * LONG, 2 * LONG),
        ] + [ANY] * len(after),
        out_specs=[lane_spec(ROWS), pl.BlockSpec((LANES, ROWS), lambda i: (i, 0))] + [lane_spec(ROWS)] * 5,
        out_shape=forward_shapes() + [jax.ShapeDtypeStruct((ROWS, CH), BF16)],
        scratch_shapes=[pltpu.VMEM((3, RIM + ROWS, LANES), F32)],
        compiler_params=params(56),
        cost_estimate=cost(1000, 1000),
        name="forward",
    )(info, streams, short, long_taps, fwd, inv, *after)


def run_finish(info, streams, halo, short, long_taps, fwd, inv, own, after=()):
    mix_in, turned, q_side, k_side, v_side, conv, gate = own
    top = lane_spec(2 * LONG)
    rim = lane_spec(RIM)
    return pl.pallas_call(
        finish_kernel,
        grid=(CH // LANES,),
        in_specs=[
            SMEM, lane_spec(3, RIM), lane_spec(RIM + 2 * TAIL), lane_spec(3, SHORT), lane_spec(LONG),
            whole(2 * LONG, 2 * LONG), whole(2 * LONG, 2 * LONG), top, rim, rim, top,
        ] + [ANY] * (3 + len(after)),
        out_specs=[top, pl.BlockSpec((LANES, 2 * LONG), lambda i: (i, 0)), rim, rim, rim, top],
        out_shape=forward_shapes(),
        input_output_aliases={7: 2, 8: 3, 9: 4, 11: 0, 12: 1, 13: 5},
        scratch_shapes=[
            pltpu.VMEM((3, TAIL + RIM, LANES), F32),
            pltpu.VMEM((3 * LONG, LANES), BF16),
        ],
        compiler_params=params(56),
        cost_estimate=cost(1000, 1000),
        name="finish",
    )(info, streams, halo, short, long_taps, fwd, inv, q_side, k_side, v_side, gate, mix_in, turned, conv, *after)


def run_backward(info, d_conv, d_q, k_side, v_side, short, long_taps, fwd, inv, after=()):
    return pl.pallas_call(
        backward_kernel,
        grid=(CH // LANES,),
        in_specs=[
            SMEM, lane_spec(ROWS), lane_spec(ROWS), lane_spec(ROWS), lane_spec(ROWS),
            lane_spec(3, SHORT), lane_spec(LONG),
            whole(2 * LONG, 2 * LONG), whole(2 * LONG, 2 * LONG),
        ] + [ANY] * len(after),
        out_specs=lane_spec(3, HALF),
        out_shape=jax.ShapeDtypeStruct((3, ROWS, CH), BF16),
        scratch_shapes=[pltpu.VMEM((3, HALF + RIM, LANES), F32)],
        compiler_params=params(56),
        cost_estimate=cost(1000, 1000),
        name="backward",
    )(info, d_conv, d_q, k_side, v_side, short, long_taps, fwd, inv, *after)


def run_backward_end(info, d_conv, msg, d_q, k_side, v_side, short, long_taps, fwd, inv, out, after=()):
    low = pl.BlockSpec((HALF, LANES), lambda i: (1, i))
    return pl.pallas_call(
        backward_end_kernel,
        grid=(CH // LANES,),
        in_specs=[
            SMEM, low, lane_spec(TAIL + 3 * RIM), low, low, low,
            lane_spec(3, SHORT), lane_spec(LONG),
            whole(2 * LONG, 2 * LONG), whole(2 * LONG, 2 * LONG), ANY,
        ] + [ANY] * len(after),
        out_specs=pl.BlockSpec((3, HALF, LANES), lambda i: (0, 1, i)),
        out_shape=jax.ShapeDtypeStruct((3, ROWS, CH), BF16),
        input_output_aliases={10: 0},
        scratch_shapes=[
            pltpu.VMEM((3, HALF + RIM, LANES), F32),
            pltpu.VMEM((HALF + 2 * LONG, LANES), BF16),
        ],
        compiler_params=params(56),
        cost_estimate=cost(1000, 1000),
        name="backward_end",
    )(info, d_conv, msg, d_q, k_side, v_side, short, long_taps, fwd, inv, out, *after)


def project_kernel(order_ref, mix_ref, weight_ref, *refs):
    out_ref = refs[-1]
    out_ref[0] = jnp.dot(mix_ref[...], weight_ref[...], preferred_element_type=F32).astype(BF16)


def own_block(i, info):
    return 0, 2 * ((info[3] + 1 + i) & 3) + info[1]


def other_block(i, info):
    return 0, 2 * ((info[3] + 1 + i) & 3) + 1 - info[1]


def run_project(info, mix_in, weight, after=()):
    count = 4
    return pl.pallas_call(
        project_kernel,
        grid_spec=pltpu.PrefetchScalarGridSpec(
            num_scalar_prefetch=1,
            grid=(count,),
            in_specs=[
                pl.BlockSpec((ROWS, CH), lambda i, order: (0, 0)),
                pl.BlockSpec((CH, CH), other_block),
            ] + [ANY] * len(after),
            out_specs=pl.BlockSpec((1, ROWS, CH), lambda i, order: (i, 0, 0)),
        ),
        out_shape=jax.ShapeDtypeStruct((count, ROWS, CH), BF16),
        compiler_params=params(),
        cost_estimate=cost(1000, 1000),
        name="project",
    )(info, mix_in, weight, *after)


def project_add_kernel(info_ref, mix_ref, weight_ref, other_ref, *refs):
    total = jnp.dot(mix_ref[...], weight_ref[...], preferred_element_type=F32)
    total += other_ref[0].astype(F32)
    up_ref, down_ref, next_ref, last_ref, own_ref = refs[-5:]
    top, bottom = total[:HALF].astype(BF16), total[HALF:].astype(BF16)

    @pl.when(pl.program_id(0) == 0)
    def _():
        next_ref[...] = top
        up_ref[HALF:] = bottom

    @pl.when(pl.program_id(0) == 1)
    def _():
        up_ref[:HALF] = top
        down_ref[HALF:] = bottom

    @pl.when(pl.program_id(0) == 2)
    def _():
        down_ref[:HALF] = top
        last_ref[...] = bottom

    @pl.when(pl.program_id(0) == 3)
    def _():
        own_ref[...] = total


def run_project_add(info, mix_in, weight, other, after=()):
    fixed = pl.BlockSpec((ROWS, CH), lambda i, order: (0, 0))
    half = pl.BlockSpec((HALF, CH), lambda i, order: (0, 0))
    return pl.pallas_call(
        project_add_kernel,
        grid_spec=pltpu.PrefetchScalarGridSpec(
            num_scalar_prefetch=1,
            grid=(4,),
            in_specs=[
                fixed,
                pl.BlockSpec((CH, CH), own_block),
                pl.BlockSpec((1, ROWS, CH), lambda i, order: (i, 0, 0)),
            ] + [ANY] * len(after),
            out_specs=[fixed, fixed, half, half, fixed],
        ),
        out_shape=[jax.ShapeDtypeStruct((rows, CH), BF16) for rows in (ROWS, ROWS, HALF, HALF)]
        + [jax.ShapeDtypeStruct((ROWS, CH), F32)],
        compiler_params=params(),
        cost_estimate=cost(1000, 1000),
        name="project_add",
    )(info, mix_in, weight, other, *after)


def prepare_kernel(info_ref, qkv_ref, cot_ref, tail_ref, quarter_ref):
    live = live_rows(info_ref[0], ROWS // 2, ROWS // 2)[:, 0:1]
    place = 0
    for stream, rows in ((0, RIM), (1, TAIL), (2, TAIL)):
        masked = qkv_ref[stream, ROWS // 2 - rows :].astype(F32) * live[ROWS // 2 - rows :]
        tail_ref[place : place + rows] = masked.astype(BF16)
        place += rows
    for quarter in range(NX):
        quarter_ref[quarter] = cot_ref[:, quarter * LANES : (quarter + 1) * LANES]


def run_prepare(info, streams, cotangent):
    return pl.pallas_call(
        prepare_kernel,
        grid=(1,),
        in_specs=[SMEM, pl.BlockSpec((3, ROWS // 2, CH), lambda i: (0, 1, 0)), whole(ROWS, CH)],
        out_specs=[whole(RIM + 2 * TAIL, CH), whole(NX, ROWS, LANES)],
        out_shape=[
            jax.ShapeDtypeStruct((RIM + 2 * TAIL, CH), BF16),
            jax.ShapeDtypeStruct((NX, ROWS, LANES), BF16),
        ],
        compiler_params=params(),
        cost_estimate=cost(1000, 1000),
        name="prepare",
    )(info, streams, cotangent)


def outer_kernel(info_ref, mine, theirs, *refs):
    turned, out_ref = refs[:NX], refs[-1]
    core = info_ref[1]
    for y in range(NY):
        total = None
        for behind in range(NX):
            x = (info_ref[2] - behind) & 3
            both = jnp.concatenate([mine[y, x], theirs[y, x]], axis=1)
            part = jnp.dot(turned[behind][...], both, preferred_element_type=F32)
            total = part if total is None else total + part
        out_ref[2 * y + core] = total[:, :LANES].astype(BF16)
        out_ref[2 * y + 1 - core] = total[:, LANES:].astype(BF16)


def run_outer(info, turned, mine, theirs, after=()):
    return pl.pallas_call(
        outer_kernel,
        in_specs=[SMEM] + [VMEM] * 6 + [ANY] * len(after),
        out_specs=VMEM,
        out_shape=jax.ShapeDtypeStruct((NZ, CH, LANES), BF16),
        compiler_params=params(),
        cost_estimate=cost(1000, 1000),
        name="outer",
    )(info, mine, theirs, *turned, *after)


def d_mix_kernel(info_ref, weight_ref, mine, theirs, q_ref, k_ref, v_ref, conv_ref, *refs):
    dconv_ref, dq_ref, msg_ref = refs[-3:]
    total = None
    for slot in range(2 * NY):
        ahead = (0, -1, 1, 2)[slot // 2]
        block = 2 * ((info_ref[3] + ahead) & 3) + (info_ref[1] if slot % 2 == 0 else 1 - info_ref[1])
        column = pl.multiple_of(block * CH, CH)
        piece = (mine, theirs)[slot % 2][slot // 2]
        part = lax.dot_general(
            piece, weight_ref[:, pl.ds(column, CH)], (((1,), (1,)), ((), ())),
            preferred_element_type=F32,
        )
        total = part if total is None else total + part
    row = lax.broadcasted_iota(jnp.int32, (ROWS, CH), 0)
    d_mix = jnp.where(row < info_ref[0], total, 0.0)
    d_conv = (d_mix * q_ref[...]).astype(BF16)
    d_q = d_mix * conv_ref[...]
    dconv_ref[...] = d_conv
    dq_ref[...] = d_q
    msg_ref[0:TAIL] = d_conv[:TAIL]
    msg_ref[TAIL : TAIL + RIM] = d_q[:RIM].astype(BF16)
    msg_ref[TAIL + RIM : TAIL + 2 * RIM] = v_ref[0:RIM].astype(BF16)
    msg_ref[TAIL + 2 * RIM : TAIL + 3 * RIM] = k_ref[0:RIM].astype(BF16)


def run_d_mix(info, weight, mine, theirs, sides, after=()):
    return pl.pallas_call(
        d_mix_kernel,
        in_specs=[SMEM] + [VMEM] * 7 + [ANY] * len(after),
        out_specs=[VMEM] * 3,
        out_shape=[
            jax.ShapeDtypeStruct((ROWS, CH), BF16), jax.ShapeDtypeStruct((ROWS, CH), F32),
            jax.ShapeDtypeStruct((TAIL + 3 * RIM, CH), BF16),
        ],
        compiler_params=params(),
        cost_estimate=cost(1000, 1000),
        name="d_mix",
    )(info, weight, mine, theirs, *sides, *after)


def exchange(array, axis):
    groups = {
        "x": [[z * NX + x for x in range(NX)] for z in range(NZ)],
        "z": [[z * NX + x for z in range(NZ)] for x in range(NX)],
        "y": [[2 * y + core for y in range(NY)] for core in range(2)],
    }[axis]
    return lax.all_to_all(
        array, "tp" if axis == "y" else "ctx", 0, 0, axis_index_groups=groups, tiled=True
    )


def add(one, other):
    return (one.astype(F32) + other.astype(F32)).astype(BF16)


def along_x(array, ahead):
    pairs = [(i, i // NX * NX + (i + ahead) % NX) for i in range(NZ * NX)]
    return lax.ppermute(array, "ctx", pairs)


def along_y(array, ahead):
    pairs = [(i, (i + 2 * ahead) % (2 * NY)) for i in range(2 * NY)]
    return lax.ppermute(array, "tp", pairs)


def copies(array):
    return jnp.broadcast_to(array[None], (NY, *array.shape))


def other_core(array):
    return lax.ppermute(array, "tp", [(i, i ^ 1) for i in range(2 * NY)])


def neighbour(array, by):
    count = NZ * NX
    return lax.ppermute(array, "ctx", [(i, i + by) for i in range(count) if 0 <= i + by < count])


def local(qkv, short_filter, long_filter, out_weight, cotangent, valid_len):
    forward_table, causal_table, anti_table = (jnp.asarray(table) for table in tables())
    ctx, tp = lax.axis_index("ctx"), lax.axis_index("tp")
    info = jnp.stack([valid_len[0], tp & 1, ctx & 3, tp >> 1])
    streams = qkv.transpose(1, 0, 2)
    short = short_filter.transpose(1, 0, 2)

    tail, quarters = run_prepare(info, streams, cotangent)
    halo = neighbour(tail, 1)
    slab = exchange(quarters, "x")
    own = run_forward(info, streams, short, long_filter, forward_table, causal_table, (tail,))
    slab, halo, held, *own = lax.optimization_barrier([slab, halo, cotangent, *own])
    slab_copies = copies(slab)
    mine = exchange(slab_copies, "y").reshape(NY, NX, ROWS, LANES)
    mix_in, turned, q_side, k_side, v_side, conv = run_finish(
        info, streams, halo, short, long_filter, forward_table, causal_table, own, (slab_copies,)
    )
    turned = [turned] + [along_x(turned, ahead) for ahead in (1, 2, 3)]
    far = along_y(held, 2)
    turned[1], mix_in = lax.optimization_barrier((turned[1], mix_in))
    given = run_project(info, mix_in, out_weight)
    taken = other_core(given)
    mine, far, given, held, *turned = lax.optimization_barrier([mine, far, given, held, *turned])
    below, above = along_y(held, 1), along_y(held, -1)
    theirs = other_core(mine)
    partial = run_outer(info, turned, mine, theirs)
    below, above, far, partial = lax.optimization_barrier((below, above, far, partial))
    cots = jnp.stack([cotangent, below, above, far])
    cots_other = other_core(cots)
    sums = exchange(partial, "z")
    up, down, next_top, last_bottom, own_out = run_project_add(info, mix_in, out_weight, taken, (partial,))
    from_below, from_above = along_y(up, 1), along_y(down, -1)
    d_conv, d_q, msg = run_d_mix(
        info, out_weight, cots, cots_other, (q_side, k_side, v_side, conv), (up,)
    )
    from_below, from_above, msg = lax.optimization_barrier((from_below, from_above, msg))
    next_top, last_bottom = add(next_top, from_below[:HALF]), add(last_bottom, from_above[HALF:])
    top, bottom = along_y(next_top, 1), along_y(last_bottom, -1)
    msg = neighbour(msg, -1)
    sides = (d_q, k_side, v_side, short, long_filter, forward_table, anti_table)
    begun = run_backward(info, d_conv, *sides)
    d_streams = run_backward_end(info, d_conv, msg, *sides, begun, (next_top, last_bottom))
    sums, d_streams, own_out = lax.optimization_barrier((sums, d_streams, own_out))
    d_qkv = d_streams.transpose(1, 0, 2)
    top = own_out[:HALF] + top.astype(F32) + from_above[:HALF].astype(F32)
    bottom = own_out[HALF:] + bottom.astype(F32) + from_below[HALF:].astype(F32)
    mixed = jnp.concatenate([top, bottom], axis=0).astype(BF16)
    d_weight = jnp.sum(sums.astype(F32), axis=0) * (1.0 / jnp.sqrt(jnp.float32(ROWS * NZ * NX)))
    return mixed, d_qkv, d_weight


def solution(mesh):
    in_specs = (
        P("ctx", None, "tp"),
        P(None, None, "tp"),
        P(None, "tp"),
        P("tp", None),
        P("ctx", "tp"),
        P("ctx"),
    )
    out_specs = (P("ctx", "tp"), P("ctx", None, "tp"), P("tp", "ctx"))
    return jax.shard_map(local, mesh=mesh, in_specs=in_specs, out_specs=out_specs, check_vma=False)
```

```python
import functools

import jax
import jax.numpy as jnp
import ml_dtypes
import numpy as np
from jax import lax
from jax.experimental import pallas as pl
from jax.experimental.pallas import tpu as pltpu
from jax.sharding import PartitionSpec as P

SHORT = 7
LONG = 128
ROWS = 512
CH = 512
LANES = 128
TAIL = 144
RIM = 16
STEP = 64
NZ, NX, NY = 8, 4, 4
HALF = ROWS // 2
F32, BF16 = jnp.float32, jnp.bfloat16


def split_bf16(table):
    high = table.astype(ml_dtypes.bfloat16)
    low = (table - high.astype(np.float64)).astype(ml_dtypes.bfloat16)
    return high, low


def tables():
    size = 2 * LONG
    freq = np.arange(LONG)[:, None]
    angle = 2.0 * np.pi * freq * np.arange(size)[None, :] / size
    real = np.concatenate([np.cos(angle), np.sin(angle)], axis=0)
    real[LONG] = (-1.0) ** np.arange(size)
    high, low = split_bf16(real[:, :LONG])
    forward = np.concatenate([high, low], axis=1)
    weight = np.full((2 * LONG, 1), 2.0 / size)
    weight[0] = weight[LONG] = 1.0 / size
    inverse = (real * weight).T
    causal = np.concatenate(split_bf16(inverse[LONG:]), axis=0)
    anti = np.concatenate(split_bf16(inverse[:LONG]), axis=0)
    return forward, causal, anti


def signs(rows):
    row = lax.broadcasted_iota(jnp.int32, (rows, LANES), 0)
    return jnp.where(row % 2 == 0, 1.0, -1.0).astype(F32)


def spectrum(forward, block):
    return jnp.dot(forward, jnp.concatenate([block, block], axis=0), preferred_element_type=F32)


def filter_spectrum(forward, taps):
    both = spectrum(forward, taps)
    cos_part, sin_part = both[:LONG], both[LONG:]
    first = lax.broadcasted_iota(jnp.int32, (LONG, LANES), 0) == 0
    return cos_part, jnp.where(first, 0.0, sin_part), jnp.where(first, sin_part, cos_part)


def back(table, product):
    high = product.astype(BF16)
    low = (product - high.astype(F32)).astype(BF16)
    half = table.shape[0] // 2
    both = jnp.dot(table, high, preferred_element_type=F32)
    rest = jnp.dot(table[:half], low, preferred_element_type=F32)
    return both[:half] + both[half:] + rest


def live_rows(valid, start, rows):
    row = lax.broadcasted_iota(jnp.int32, (rows, LANES), 0) + start
    return jnp.where(row < valid, 1.0, 0.0).astype(F32)


def filtered(short_ref, ext_ref, stream, start, rows):
    total = short_ref[stream, 0:1] * ext_ref[stream, start : start + rows]
    for tap in range(1, SHORT):
        total += short_ref[stream, tap : tap + 1] * ext_ref[stream, start - tap : start - tap + rows]
    return total


def convolve(before, now, sign, inv, cos_h, sin_h, alt_h):
    window = before + sign * now
    cos_x, sin_x = window[:LONG], window[LONG:]
    product = jnp.concatenate(
        [cos_x * cos_h - sin_x * sin_h, cos_x * sin_h + sin_x * alt_h], axis=0
    )
    return back(inv, product)


def forward_kernel(valid_ref, qkv_ref, short_ref, long_ref, fwd_ref, inv_ref, *refs):
    mix_ref, turned_ref, q_ref, k_ref, v_ref, conv_ref, gate_ref, ext_ref = refs[-8:]
    valid = valid_ref[0]
    ext_ref[:, 0:RIM] = jnp.zeros((3, RIM, LANES), F32)
    for start in range(0, ROWS, STEP):
        live = live_rows(valid, start, STEP)
        for stream in range(3):
            ext_ref[stream, RIM + start : RIM + start + STEP] = (
                qkv_ref[stream, start : start + STEP].astype(F32) * live
            )
    for start in range(0, ROWS, STEP):
        k_side = filtered(short_ref, ext_ref, 1, RIM + start, STEP)
        v_side = filtered(short_ref, ext_ref, 2, RIM + start, STEP)
        k_ref[start : start + STEP] = k_side
        v_ref[start : start + STEP] = v_side
        q_ref[start : start + STEP] = filtered(short_ref, ext_ref, 0, RIM + start, STEP)
        gate_ref[start : start + STEP] = (k_side * v_side).astype(BF16)
    fwd = fwd_ref[...]
    inv = inv_ref[...]
    taps = filter_spectrum(fwd, long_ref[...])
    sign = signs(2 * LONG)
    before = spectrum(fwd, gate_ref[LONG : 2 * LONG])
    for start in range(2 * LONG, ROWS, LONG):
        now = spectrum(fwd, gate_ref[start : start + LONG])
        conv = convolve(before, now, sign, inv, *taps)
        before = now
        conv_ref[start : start + LONG] = conv
        mix_in = live_rows(valid, start, LONG) * q_ref[start : start + LONG] * conv
        mix_ref[start : start + LONG] = mix_in.astype(BF16)
        turned_ref[:, start : start + LONG] = mix_in.T.astype(BF16)


def finish_kernel(
    valid_ref, qkv_ref, halo_ref, short_ref, long_ref, fwd_ref, inv_ref, q_in, k_in, v_in, gate_in, *refs
):
    mix_ref, turned_ref, q_ref, k_ref, v_ref, conv_ref, ext_ref, gate_ref = refs[-8:]
    valid = valid_ref[0]
    ext_ref[0, TAIL - RIM : TAIL] = halo_ref[0:RIM].astype(F32)
    ext_ref[1, 0:TAIL] = halo_ref[RIM : RIM + TAIL].astype(F32)
    ext_ref[2, 0:TAIL] = halo_ref[RIM + TAIL : RIM + 2 * TAIL].astype(F32)
    live = live_rows(valid, 0, RIM)
    for stream in range(3):
        ext_ref[stream, TAIL : TAIL + RIM] = qkv_ref[stream].astype(F32) * live
    for start in range(0, LONG, STEP):
        k_side = filtered(short_ref, ext_ref, 1, RIM + start, STEP)
        v_side = filtered(short_ref, ext_ref, 2, RIM + start, STEP)
        gate_ref[start : start + STEP] = (k_side * v_side).astype(BF16)
    q_rim = filtered(short_ref, ext_ref, 0, TAIL, RIM)
    k_rim = filtered(short_ref, ext_ref, 1, TAIL, RIM)
    v_rim = filtered(short_ref, ext_ref, 2, TAIL, RIM)
    q_ref[...] = q_rim
    k_ref[...] = k_rim
    v_ref[...] = v_rim
    gate_ref[LONG : LONG + RIM] = (k_rim * v_rim).astype(BF16)
    gate_ref[LONG + RIM : 3 * LONG] = gate_in[RIM:]
    fwd = fwd_ref[...]
    inv = inv_ref[...]
    taps = filter_spectrum(fwd, long_ref[...])
    sign = signs(2 * LONG)
    before = spectrum(fwd, gate_ref[0:LONG])
    for start in range(0, 2 * LONG, LONG):
        now = spectrum(fwd, gate_ref[LONG + start : 2 * LONG + start])
        conv = convolve(before, now, sign, inv, *taps)
        before = now
        conv_ref[start : start + LONG] = conv
        q_side = q_in[start : start + LONG]
        if start == 0:
            q_side = jnp.concatenate([q_rim, q_side[RIM:]], axis=0)
        mix_in = live_rows(valid, start, LONG) * q_side * conv
        mix_ref[start : start + LONG] = mix_in.astype(BF16)
        turned_ref[:, start : start + LONG] = mix_in.T.astype(BF16)


def backward_kernel(
    valid_ref, dconv_ref, msg_ref, dq_ref, k_ref, v_ref, short_ref, long_ref, fwd_ref, inv_ref,
    *refs,
):
    out_ref, ext_ref, gate_ref = refs[-3:]
    valid = valid_ref[0]
    fwd = fwd_ref[...]
    inv = inv_ref[...]
    gate_ref[0:TAIL] = msg_ref[0:TAIL]
    gate_ref[TAIL : 2 * LONG] = jnp.zeros((2 * LONG - TAIL, LANES), BF16)
    cos_h, sin_h, alt_h = filter_spectrum(fwd, long_ref[...])
    sign = signs(2 * LONG)
    blocks = ROWS // LONG
    ext_ref[0, 0:ROWS] = dq_ref[...]
    ext_ref[0, ROWS : ROWS + RIM] = msg_ref[TAIL : TAIL + RIM].astype(F32)
    now = spectrum(fwd, dconv_ref[0:LONG])
    for block in range(blocks + 1):
        start = block * LONG
        if block + 1 < blocks:
            after = spectrum(fwd, dconv_ref[start + LONG : start + 2 * LONG])
        else:
            rim = (block + 1 - blocks) * LONG
            after = spectrum(fwd, gate_ref[rim : rim + LONG])
        window = now + sign * after
        now = after
        cos_x, sin_x = window[:LONG], window[LONG:]
        product = jnp.concatenate(
            [cos_x * cos_h + sin_x * sin_h, sin_x * alt_h - cos_x * sin_h], axis=0
        )
        gated = back(inv, product)
        if block < blocks:
            ext_ref[1, start : start + LONG] = gated * v_ref[start : start + LONG]
            ext_ref[2, start : start + LONG] = gated * k_ref[start : start + LONG]
        else:
            rim = gated[:RIM]
            v_rim = msg_ref[TAIL + RIM : TAIL + 2 * RIM].astype(F32)
            k_rim = msg_ref[TAIL + 2 * RIM : TAIL + 3 * RIM].astype(F32)
            ext_ref[1, ROWS : ROWS + RIM] = rim * v_rim
            ext_ref[2, ROWS : ROWS + RIM] = rim * k_rim
    for start in range(0, ROWS, STEP):
        live = live_rows(valid, start, STEP)
        for stream in range(3):
            total = short_ref[stream, 0:1] * ext_ref[stream, start : start + STEP]
            for tap in range(1, SHORT):
                total += short_ref[stream, tap : tap + 1] * ext_ref[stream, start + tap : start + tap + STEP]
            out_ref[stream, start : start + STEP] = (total * live).astype(BF16)


def params(mib=20):
    return pltpu.CompilerParams(vmem_limit_bytes=mib * 2**20)


def cost(flops, moved):
    return pl.CostEstimate(flops=flops, bytes_accessed=moved, transcendentals=0)


SMEM = pl.BlockSpec(memory_space=pltpu.SMEM)
VMEM = pl.BlockSpec(memory_space=pltpu.VMEM)
ANY = pl.BlockSpec(memory_space=pl.ANY)


def lane_spec(*lead):
    return pl.BlockSpec(lead + (LANES,), lambda i: (0,) * len(lead) + (i,))


def whole(*shape):
    return pl.BlockSpec(shape, lambda i: (0,) * len(shape))


def forward_shapes():
    side = jax.ShapeDtypeStruct((ROWS, CH), F32)
    square = jax.ShapeDtypeStruct((ROWS, CH), BF16)
    return [square, square, side, side, side, side]


def run_forward(info, streams, short, long_taps, fwd, inv, after=()):
    return pl.pallas_call(
        forward_kernel,
        grid=(CH // LANES,),
        in_specs=[
            SMEM, lane_spec(3, ROWS), lane_spec(3, SHORT), lane_spec(LONG),
            whole(2 * LONG, 2 * LONG), whole(2 * LONG, 2 * LONG),
        ] + [ANY] * len(after),
        out_specs=[lane_spec(ROWS), pl.BlockSpec((LANES, ROWS), lambda i: (i, 0))] + [lane_spec(ROWS)] * 5,
        out_shape=forward_shapes() + [jax.ShapeDtypeStruct((ROWS, CH), BF16)],
        scratch_shapes=[pltpu.VMEM((3, RIM + ROWS, LANES), F32)],
        compiler_params=params(56),
        cost_estimate=cost(1000, 1000),
        name="forward",
    )(info, streams, short, long_taps, fwd, inv, *after)


def run_finish(info, streams, halo, short, long_taps, fwd, inv, own, after=()):
    mix_in, turned, q_side, k_side, v_side, conv, gate = own
    top = lane_spec(2 * LONG)
    rim = lane_spec(RIM)
    return pl.pallas_call(
        finish_kernel,
        grid=(CH // LANES,),
        in_specs=[
            SMEM, lane_spec(3, RIM), lane_spec(RIM + 2 * TAIL), lane_spec(3, SHORT), lane_spec(LONG),
            whole(2 * LONG, 2 * LONG), whole(2 * LONG, 2 * LONG), top, rim, rim, top,
        ] + [ANY] * (3 + len(after)),
        out_specs=[top, pl.BlockSpec((LANES, 2 * LONG), lambda i: (i, 0)), rim, rim, rim, top],
        out_shape=forward_shapes(),
        input_output_aliases={7: 2, 8: 3, 9: 4, 11: 0, 12: 1, 13: 5},
        scratch_shapes=[
            pltpu.VMEM((3, TAIL + RIM, LANES), F32),
            pltpu.VMEM((3 * LONG, LANES), BF16),
        ],
        compiler_params=params(56),
        cost_estimate=cost(1000, 1000),
        name="finish",
    )(info, streams, halo, short, long_taps, fwd, inv, q_side, k_side, v_side, gate, mix_in, turned, conv, *after)


def run_backward(valid, d_conv, msg, d_q, k_side, v_side, short, long_taps, fwd, inv, after=()):
    return pl.pallas_call(
        backward_kernel,
        grid=(CH // LANES,),
        in_specs=[
            SMEM, lane_spec(ROWS), lane_spec(TAIL + 3 * RIM), lane_spec(ROWS), lane_spec(ROWS),
            lane_spec(ROWS), lane_spec(3, SHORT), lane_spec(LONG),
            whole(2 * LONG, 2 * LONG), whole(2 * LONG, 2 * LONG),
        ] + [ANY] * len(after),
        out_specs=lane_spec(3, ROWS),
        out_shape=jax.ShapeDtypeStruct((3, ROWS, CH), BF16),
        scratch_shapes=[
            pltpu.VMEM((3, ROWS + RIM, LANES), F32),
            pltpu.VMEM((2 * LONG, LANES), BF16),
        ],
        compiler_params=params(56),
        cost_estimate=cost(1000, 1000),
        name="backward",
    )(valid, d_conv, msg, d_q, k_side, v_side, short, long_taps, fwd, inv, *after)


def project_kernel(order_ref, mix_ref, weight_ref, *refs):
    out_ref = refs[-1]
    out_ref[0] = jnp.dot(mix_ref[...], weight_ref[...], preferred_element_type=F32).astype(BF16)


def own_block(i, info):
    return 0, 2 * ((info[3] + 1 + i) & 3) + info[1]


def other_block(i, info):
    return 0, 2 * ((info[3] + 1 + i) & 3) + 1 - info[1]


def run_project(info, mix_in, weight, after=()):
    count = 4
    return pl.pallas_call(
        project_kernel,
        grid_spec=pltpu.PrefetchScalarGridSpec(
            num_scalar_prefetch=1,
            grid=(count,),
            in_specs=[
                pl.BlockSpec((ROWS, CH), lambda i, order: (0, 0)),
                pl.BlockSpec((CH, CH), other_block),
            ] + [ANY] * len(after),
            out_specs=pl.BlockSpec((1, ROWS, CH), lambda i, order: (i, 0, 0)),
        ),
        out_shape=jax.ShapeDtypeStruct((count, ROWS, CH), BF16),
        compiler_params=params(),
        cost_estimate=cost(1000, 1000),
        name="project",
    )(info, mix_in, weight, *after)


def project_add_kernel(info_ref, mix_ref, weight_ref, other_ref, *refs):
    total = jnp.dot(mix_ref[...], weight_ref[...], preferred_element_type=F32)
    total += other_ref[0].astype(F32)
    up_ref, down_ref, next_ref, last_ref, own_ref = refs[-5:]
    top, bottom = total[:HALF].astype(BF16), total[HALF:].astype(BF16)

    @pl.when(pl.program_id(0) == 0)
    def _():
        next_ref[...] = top
        up_ref[HALF:] = bottom

    @pl.when(pl.program_id(0) == 1)
    def _():
        up_ref[:HALF] = top
        down_ref[HALF:] = bottom

    @pl.when(pl.program_id(0) == 2)
    def _():
        down_ref[:HALF] = top
        last_ref[...] = bottom

    @pl.when(pl.program_id(0) == 3)
    def _():
        own_ref[...] = total


def run_project_add(info, mix_in, weight, other, after=()):
    fixed = pl.BlockSpec((ROWS, CH), lambda i, order: (0, 0))
    half = pl.BlockSpec((HALF, CH), lambda i, order: (0, 0))
    return pl.pallas_call(
        project_add_kernel,
        grid_spec=pltpu.PrefetchScalarGridSpec(
            num_scalar_prefetch=1,
            grid=(4,),
            in_specs=[
                fixed,
                pl.BlockSpec((CH, CH), own_block),
                pl.BlockSpec((1, ROWS, CH), lambda i, order: (i, 0, 0)),
            ] + [ANY] * len(after),
            out_specs=[fixed, fixed, half, half, fixed],
        ),
        out_shape=[jax.ShapeDtypeStruct((rows, CH), BF16) for rows in (ROWS, ROWS, HALF, HALF)]
        + [jax.ShapeDtypeStruct((ROWS, CH), F32)],
        compiler_params=params(),
        cost_estimate=cost(1000, 1000),
        name="project_add",
    )(info, mix_in, weight, other, *after)


def prepare_kernel(info_ref, qkv_ref, cot_ref, tail_ref, quarter_ref):
    live = live_rows(info_ref[0], ROWS // 2, ROWS // 2)[:, 0:1]
    place = 0
    for stream, rows in ((0, RIM), (1, TAIL), (2, TAIL)):
        masked = qkv_ref[stream, ROWS // 2 - rows :].astype(F32) * live[ROWS // 2 - rows :]
        tail_ref[place : place + rows] = masked.astype(BF16)
        place += rows
    for quarter in range(NX):
        quarter_ref[quarter] = cot_ref[:, quarter * LANES : (quarter + 1) * LANES]


def run_prepare(info, streams, cotangent):
    return pl.pallas_call(
        prepare_kernel,
        grid=(1,),
        in_specs=[SMEM, pl.BlockSpec((3, ROWS // 2, CH), lambda i: (0, 1, 0)), whole(ROWS, CH)],
        out_specs=[whole(RIM + 2 * TAIL, CH), whole(NX, ROWS, LANES)],
        out_shape=[
            jax.ShapeDtypeStruct((RIM + 2 * TAIL, CH), BF16),
            jax.ShapeDtypeStruct((NX, ROWS, LANES), BF16),
        ],
        compiler_params=params(56),
        cost_estimate=cost(1000, 1000),
        name="prepare",
    )(info, streams, cotangent)


def outer_kernel(info_ref, mine, theirs, *refs):
    turned, out_ref = refs[:NX], refs[-1]
    core = info_ref[1]
    for y in range(NY):
        total = None
        for behind in range(NX):
            x = (info_ref[2] - behind) & 3
            both = jnp.concatenate([mine[y, x], theirs[y, x]], axis=1)
            part = jnp.dot(turned[behind][...], both, preferred_element_type=F32)
            total = part if total is None else total + part
        total = total * (1.0 / np.sqrt(float(ROWS * NZ * NX)))
        out_ref[2 * y + core] = total[:, :LANES].astype(BF16)
        out_ref[2 * y + 1 - core] = total[:, LANES:].astype(BF16)


def run_outer(info, turned, mine, theirs, after=()):
    return pl.pallas_call(
        outer_kernel,
        in_specs=[SMEM] + [VMEM] * 6 + [ANY] * len(after),
        out_specs=VMEM,
        out_shape=jax.ShapeDtypeStruct((NZ, CH, LANES), BF16),
        compiler_params=params(),
        cost_estimate=cost(1000, 1000),
        name="outer",
    )(info, mine, theirs, *turned, *after)


def d_mix_kernel(info_ref, weight_ref, mine, theirs, q_ref, k_ref, v_ref, conv_ref, *refs):
    dconv_ref, dq_ref, msg_ref = refs[-3:]
    total = None
    for slot in range(2 * NY):
        ahead = (0, -1, 1, 2)[slot // 2]
        block = 2 * ((info_ref[3] + ahead) & 3) + (info_ref[1] if slot % 2 == 0 else 1 - info_ref[1])
        column = pl.multiple_of(block * CH, CH)
        piece = (mine, theirs)[slot % 2][slot // 2]
        part = lax.dot_general(
            piece, weight_ref[:, pl.ds(column, CH)], (((1,), (1,)), ((), ())),
            preferred_element_type=F32,
        )
        total = part if total is None else total + part
    row = lax.broadcasted_iota(jnp.int32, (ROWS, CH), 0)
    d_mix = jnp.where(row < info_ref[0], total, 0.0)
    d_conv = (d_mix * q_ref[...]).astype(BF16)
    d_q = d_mix * conv_ref[...]
    dconv_ref[...] = d_conv
    dq_ref[...] = d_q
    msg_ref[0:TAIL] = d_conv[:TAIL]
    msg_ref[TAIL : TAIL + RIM] = d_q[:RIM].astype(BF16)
    msg_ref[TAIL + RIM : TAIL + 2 * RIM] = v_ref[0:RIM].astype(BF16)
    msg_ref[TAIL + 2 * RIM : TAIL + 3 * RIM] = k_ref[0:RIM].astype(BF16)


def run_d_mix(info, weight, mine, theirs, sides, after=()):
    return pl.pallas_call(
        d_mix_kernel,
        in_specs=[SMEM] + [VMEM] * 7 + [ANY] * len(after),
        out_specs=[VMEM] * 3,
        out_shape=[
            jax.ShapeDtypeStruct((ROWS, CH), BF16), jax.ShapeDtypeStruct((ROWS, CH), F32),
            jax.ShapeDtypeStruct((TAIL + 3 * RIM, CH), BF16),
        ],
        compiler_params=params(),
        cost_estimate=cost(1000, 1000),
        name="d_mix",
    )(info, weight, mine, theirs, *sides, *after)


def exchange(array, axis):
    groups = {
        "x": [[z * NX + x for x in range(NX)] for z in range(NZ)],
        "z": [[z * NX + x for z in range(NZ)] for x in range(NX)],
        "y": [[2 * y + core for y in range(NY)] for core in range(2)],
    }[axis]
    return lax.all_to_all(
        array, "tp" if axis == "y" else "ctx", 0, 0, axis_index_groups=groups, tiled=True
    )


def add(one, other):
    return (one.astype(F32) + other.astype(F32)).astype(BF16)


def along_x(array, ahead):
    pairs = [(i, i // NX * NX + (i + ahead) % NX) for i in range(NZ * NX)]
    return lax.ppermute(array, "ctx", pairs)


def along_y(array, ahead):
    pairs = [(i, (i + 2 * ahead) % (2 * NY)) for i in range(2 * NY)]
    return lax.ppermute(array, "tp", pairs)


def copies(array):
    return jnp.broadcast_to(array[None], (NY, *array.shape))


def other_core(array):
    return lax.ppermute(array, "tp", [(i, i ^ 1) for i in range(2 * NY)])


def neighbour(array, by):
    count = NZ * NX
    return lax.ppermute(array, "ctx", [(i, i + by) for i in range(count) if 0 <= i + by < count])


def local(qkv, short_filter, long_filter, out_weight, cotangent, valid_len):
    forward_table, causal_table, anti_table = (jnp.asarray(table) for table in tables())
    ctx, tp = lax.axis_index("ctx"), lax.axis_index("tp")
    info = jnp.stack([valid_len[0], tp & 1, ctx & 3, tp >> 1])
    streams = qkv.transpose(1, 0, 2)
    short = short_filter.transpose(1, 0, 2)

    tail, quarters = run_prepare(info, streams, cotangent)
    halo = neighbour(tail, 1)
    slab = exchange(quarters, "x")
    own = run_forward(info, streams, short, long_filter, forward_table, causal_table, (tail,))
    slab, held, *_ = lax.optimization_barrier([slab, cotangent, halo, *own])
    slab_copies = copies(slab)
    mine = exchange(slab_copies, "y").reshape(NY, NX, ROWS, LANES)
    mix_in, turned, q_side, k_side, v_side, conv = run_finish(
        info, streams, halo, short, long_filter, forward_table, causal_table, own, (slab_copies,)
    )
    turned = [turned] + [along_x(turned, ahead) for ahead in (1, 2, 3)]
    far = along_y(held, 2)
    given = run_project(info, mix_in, out_weight, (turned[1],))
    taken = other_core(given)
    held, _ = lax.optimization_barrier((held, turned[1]))
    below, above = along_y(held, 1), along_y(held, -1)
    ready, *_ = lax.optimization_barrier([mine, far, given, *turned])
    theirs = other_core(ready)
    partial = run_outer(info, turned, mine, theirs)
    held, _ = lax.optimization_barrier((cotangent, partial))
    cots = jnp.stack([held, below, above, far])
    cots_other = other_core(cots)
    sums = exchange(partial, "z")
    up, down, next_top, last_bottom, own_out = run_project_add(info, mix_in, out_weight, taken, (partial,))
    from_below, from_above = along_y(up, 1), along_y(down, -1)
    d_conv, d_q, msg = run_d_mix(
        info, out_weight, cots, cots_other, (q_side, k_side, v_side, conv), (up,)
    )
    from_below, from_above, _ = lax.optimization_barrier((from_below, from_above, msg))
    next_top, last_bottom = add(next_top, from_below[:HALF]), add(last_bottom, from_above[HALF:])
    top, bottom = along_y(next_top, 1), along_y(last_bottom, -1)
    msg = neighbour(msg, -1)
    d_streams = run_backward(
        info, d_conv, msg, d_q, k_side, v_side, short, long_filter, forward_table, anti_table,
        (next_top, last_bottom),
    )
    sums, own_out, _ = lax.optimization_barrier((sums, own_out, d_streams))
    d_qkv = d_streams.transpose(1, 0, 2)
    top = own_out[:HALF] + top.astype(F32) + from_above[:HALF].astype(F32)
    bottom = own_out[HALF:] + bottom.astype(F32) + from_below[HALF:].astype(F32)
    mixed = jnp.concatenate([top, bottom], axis=0).astype(BF16)
    d_weight = jnp.sum(sums.astype(F32), axis=0)
    return mixed, d_qkv, d_weight


def solution(mesh):
    in_specs = (
        P("ctx", None, "tp"),
        P(None, None, "tp"),
        P(None, "tp"),
        P("tp", None),
        P("ctx", "tp"),
        P("ctx"),
    )
    out_specs = (P("ctx", "tp"), P("ctx", None, "tp"), P("tp", "ctx"))
    return jax.shard_map(local, mesh=mesh, in_specs=in_specs, out_specs=out_specs, check_vma=False)
```

```python
import functools

import jax
import jax.numpy as jnp
import ml_dtypes
import numpy as np
from jax import lax
from jax.experimental import pallas as pl
from jax.experimental.pallas import tpu as pltpu
from jax.sharding import PartitionSpec as P

SHORT = 7
LONG = 128
ROWS = 512
CH = 512
LANES = 128
TAIL = 144
RIM = 16
STEP = 64
NZ, NX, NY = 8, 4, 4
HALF = ROWS // 2
F32, BF16 = jnp.float32, jnp.bfloat16


def split_bf16(table):
    high = table.astype(ml_dtypes.bfloat16)
    low = (table - high.astype(np.float64)).astype(ml_dtypes.bfloat16)
    return high, low


def tables():
    size = 2 * LONG
    freq = np.arange(LONG)[:, None]
    angle = 2.0 * np.pi * freq * np.arange(size)[None, :] / size
    real = np.concatenate([np.cos(angle), np.sin(angle)], axis=0)
    real[LONG] = (-1.0) ** np.arange(size)
    high, low = split_bf16(real[:, :LONG])
    forward = np.concatenate([high, low], axis=1)
    weight = np.full((2 * LONG, 1), 2.0 / size)
    weight[0] = weight[LONG] = 1.0 / size
    inverse = (real * weight).T
    causal = np.concatenate(split_bf16(inverse[LONG:]), axis=0)
    anti = np.concatenate(split_bf16(inverse[:LONG]), axis=0)
    return forward, causal, anti


def signs(rows):
    row = lax.broadcasted_iota(jnp.int32, (rows, LANES), 0)
    return jnp.where(row % 2 == 0, 1.0, -1.0).astype(F32)


def spectrum(forward, block):
    return jnp.dot(forward, jnp.concatenate([block, block], axis=0), preferred_element_type=F32)


def filter_spectrum(forward, taps):
    both = spectrum(forward, taps)
    cos_part, sin_part = both[:LONG], both[LONG:]
    first = lax.broadcasted_iota(jnp.int32, (LONG, LANES), 0) == 0
    return cos_part, jnp.where(first, 0.0, sin_part), jnp.where(first, sin_part, cos_part)


def back(table, product):
    high = product.astype(BF16)
    low = (product - high.astype(F32)).astype(BF16)
    half = table.shape[0] // 2
    both = jnp.dot(table, high, preferred_element_type=F32)
    rest = jnp.dot(table[:half], low, preferred_element_type=F32)
    return both[:half] + both[half:] + rest


def live_rows(valid, start, rows):
    row = lax.broadcasted_iota(jnp.int32, (rows, LANES), 0) + start
    return jnp.where(row < valid, 1.0, 0.0).astype(F32)


def filtered(short_ref, ext_ref, stream, start, rows):
    total = short_ref[stream, 0:1] * ext_ref[stream, start : start + rows]
    for tap in range(1, SHORT):
        total += short_ref[stream, tap : tap + 1] * ext_ref[stream, start - tap : start - tap + rows]
    return total


def convolve(before, now, sign, inv, cos_h, sin_h, alt_h):
    window = before + sign * now
    cos_x, sin_x = window[:LONG], window[LONG:]
    product = jnp.concatenate(
        [cos_x * cos_h - sin_x * sin_h, cos_x * sin_h + sin_x * alt_h], axis=0
    )
    return back(inv, product)


def forward_kernel(valid_ref, qkv_ref, short_ref, long_ref, fwd_ref, inv_ref, *refs):
    mix_ref, turned_ref, q_ref, k_ref, v_ref, conv_ref, gate_ref, ext_ref = refs[-8:]
    valid = valid_ref[0]
    ext_ref[:, 0:RIM] = jnp.zeros((3, RIM, LANES), F32)
    for start in range(0, ROWS, STEP):
        live = live_rows(valid, start, STEP)
        for stream in range(3):
            ext_ref[stream, RIM + start : RIM + start + STEP] = (
                qkv_ref[stream, start : start + STEP].astype(F32) * live
            )
    for start in range(0, ROWS, STEP):
        k_side = filtered(short_ref, ext_ref, 1, RIM + start, STEP)
        v_side = filtered(short_ref, ext_ref, 2, RIM + start, STEP)
        k_ref[start : start + STEP] = k_side
        v_ref[start : start + STEP] = v_side
        q_ref[start : start + STEP] = filtered(short_ref, ext_ref, 0, RIM + start, STEP)
        gate_ref[start : start + STEP] = (k_side * v_side).astype(BF16)
    fwd = fwd_ref[...]
    inv = inv_ref[...]
    taps = filter_spectrum(fwd, long_ref[...])
    sign = signs(2 * LONG)
    before = spectrum(fwd, gate_ref[LONG : 2 * LONG])
    for start in range(2 * LONG, ROWS, LONG):
        now = spectrum(fwd, gate_ref[start : start + LONG])
        conv = convolve(before, now, sign, inv, *taps)
        before = now
        conv_ref[start : start + LONG] = conv
        mix_in = live_rows(valid, start, LONG) * q_ref[start : start + LONG] * conv
        mix_ref[start : start + LONG] = mix_in.astype(BF16)
        turned_ref[:, start : start + LONG] = mix_in.T.astype(BF16)


def finish_kernel(
    valid_ref, qkv_ref, halo_ref, short_ref, long_ref, fwd_ref, inv_ref, q_in, k_in, v_in, gate_in, *refs
):
    mix_ref, turned_ref, q_ref, k_ref, v_ref, conv_ref, ext_ref, gate_ref = refs[-8:]
    valid = valid_ref[0]
    ext_ref[0, TAIL - RIM : TAIL] = halo_ref[0:RIM].astype(F32)
    ext_ref[1, 0:TAIL] = halo_ref[RIM : RIM + TAIL].astype(F32)
    ext_ref[2, 0:TAIL] = halo_ref[RIM + TAIL : RIM + 2 * TAIL].astype(F32)
    live = live_rows(valid, 0, RIM)
    for stream in range(3):
        ext_ref[stream, TAIL : TAIL + RIM] = qkv_ref[stream].astype(F32) * live
    for start in range(0, LONG, STEP):
        k_side = filtered(short_ref, ext_ref, 1, RIM + start, STEP)
        v_side = filtered(short_ref, ext_ref, 2, RIM + start, STEP)
        gate_ref[start : start + STEP] = (k_side * v_side).astype(BF16)
    q_rim = filtered(short_ref, ext_ref, 0, TAIL, RIM)
    k_rim = filtered(short_ref, ext_ref, 1, TAIL, RIM)
    v_rim = filtered(short_ref, ext_ref, 2, TAIL, RIM)
    q_ref[...] = q_rim
    k_ref[...] = k_rim
    v_ref[...] = v_rim
    gate_ref[LONG : LONG + RIM] = (k_rim * v_rim).astype(BF16)
    gate_ref[LONG + RIM : 3 * LONG] = gate_in[RIM:]
    fwd = fwd_ref[...]
    inv = inv_ref[...]
    taps = filter_spectrum(fwd, long_ref[...])
    sign = signs(2 * LONG)
    before = spectrum(fwd, gate_ref[0:LONG])
    for start in range(0, 2 * LONG, LONG):
        now = spectrum(fwd, gate_ref[LONG + start : 2 * LONG + start])
        conv = convolve(before, now, sign, inv, *taps)
        before = now
        conv_ref[start : start + LONG] = conv
        q_side = q_in[start : start + LONG]
        if start == 0:
            q_side = jnp.concatenate([q_rim, q_side[RIM:]], axis=0)
        mix_in = live_rows(valid, start, LONG) * q_side * conv
        mix_ref[start : start + LONG] = mix_in.astype(BF16)
        turned_ref[:, start : start + LONG] = mix_in.T.astype(BF16)


def correlate(now, after, sign, inv, cos_h, sin_h, alt_h):
    window = now + sign * after
    cos_x, sin_x = window[:LONG], window[LONG:]
    product = jnp.concatenate(
        [cos_x * cos_h + sin_x * sin_h, sin_x * alt_h - cos_x * sin_h], axis=0
    )
    return back(inv, product)


def filter_back(valid, first, short_ref, ext_ref, out_ref):
    for start in range(0, HALF, STEP):
        live = live_rows(valid, first + start, STEP)
        for stream in range(3):
            total = short_ref[stream, 0:1] * ext_ref[stream, start : start + STEP]
            for tap in range(1, SHORT):
                total += short_ref[stream, tap : tap + 1] * ext_ref[stream, start + tap : start + tap + STEP]
            out_ref[stream, start : start + STEP] = (total * live).astype(BF16)


def backward_kernel(
    valid_ref, dconv_ref, dq_ref, k_ref, v_ref, short_ref, long_ref, fwd_ref, inv_ref, *refs
):
    out_ref, ext_ref = refs[-2:]
    fwd = fwd_ref[...]
    inv = inv_ref[...]
    taps = filter_spectrum(fwd, long_ref[...])
    sign = signs(2 * LONG)
    ext_ref[0, 0 : HALF + RIM] = dq_ref[0 : HALF + RIM]
    now = spectrum(fwd, dconv_ref[0:LONG])
    for start in range(0, HALF + LONG, LONG):
        after = spectrum(fwd, dconv_ref[start + LONG : start + 2 * LONG])
        gated = correlate(now, after, sign, inv, *taps)
        now = after
        rows = LONG if start < HALF else RIM
        ext_ref[1, start : start + rows] = gated[:rows] * v_ref[start : start + rows]
        ext_ref[2, start : start + rows] = gated[:rows] * k_ref[start : start + rows]
    filter_back(valid_ref[0], 0, short_ref, ext_ref, out_ref)


def backward_end_kernel(
    valid_ref, dconv_ref, msg_ref, dq_ref, k_ref, v_ref, short_ref, long_ref, fwd_ref, inv_ref, *refs
):
    out_ref, ext_ref, gate_ref = refs[-3:]
    fwd = fwd_ref[...]
    inv = inv_ref[...]
    taps = filter_spectrum(fwd, long_ref[...])
    sign = signs(2 * LONG)
    gate_ref[0:HALF] = dconv_ref[...]
    gate_ref[HALF : HALF + TAIL] = msg_ref[0:TAIL]
    gate_ref[HALF + TAIL : HALF + 2 * LONG] = jnp.zeros((2 * LONG - TAIL, LANES), BF16)
    ext_ref[0, 0:HALF] = dq_ref[...]
    ext_ref[0, HALF : HALF + RIM] = msg_ref[TAIL : TAIL + RIM].astype(F32)
    now = spectrum(fwd, gate_ref[0:LONG])
    for start in range(0, HALF + LONG, LONG):
        after = spectrum(fwd, gate_ref[start + LONG : start + 2 * LONG])
        gated = correlate(now, after, sign, inv, *taps)
        now = after
        if start < HALF:
            ext_ref[1, start : start + LONG] = gated * v_ref[start : start + LONG]
            ext_ref[2, start : start + LONG] = gated * k_ref[start : start + LONG]
        else:
            v_rim = msg_ref[TAIL + RIM : TAIL + 2 * RIM].astype(F32)
            k_rim = msg_ref[TAIL + 2 * RIM : TAIL + 3 * RIM].astype(F32)
            ext_ref[1, HALF : HALF + RIM] = gated[:RIM] * v_rim
            ext_ref[2, HALF : HALF + RIM] = gated[:RIM] * k_rim
    filter_back(valid_ref[0], HALF, short_ref, ext_ref, out_ref)


def params(mib=20):
    return pltpu.CompilerParams(vmem_limit_bytes=mib * 2**20)


def cost(flops, moved):
    return pl.CostEstimate(flops=flops, bytes_accessed=moved, transcendentals=0)


SMEM = pl.BlockSpec(memory_space=pltpu.SMEM)
VMEM = pl.BlockSpec(memory_space=pltpu.VMEM)
ANY = pl.BlockSpec(memory_space=pl.ANY)


def lane_spec(*lead):
    return pl.BlockSpec(lead + (LANES,), lambda i: (0,) * len(lead) + (i,))


def whole(*shape):
    return pl.BlockSpec(shape, lambda i: (0,) * len(shape))


def forward_shapes():
    side = jax.ShapeDtypeStruct((ROWS, CH), F32)
    square = jax.ShapeDtypeStruct((ROWS, CH), BF16)
    return [square, square, side, side, side, side]


def run_forward(info, streams, short, long_taps, fwd, inv, after=()):
    return pl.pallas_call(
        forward_kernel,
        grid=(CH // LANES,),
        in_specs=[
            SMEM, lane_spec(3, ROWS), lane_spec(3, SHORT), lane_spec(LONG),
            whole(2 * LONG, 2 * LONG), whole(2 * LONG, 2 * LONG),
        ] + [ANY] * len(after),
        out_specs=[lane_spec(ROWS), pl.BlockSpec((LANES, ROWS), lambda i: (i, 0))] + [lane_spec(ROWS)] * 5,
        out_shape=forward_shapes() + [jax.ShapeDtypeStruct((ROWS, CH), BF16)],
        scratch_shapes=[pltpu.VMEM((3, RIM + ROWS, LANES), F32)],
        compiler_params=params(56),
        cost_estimate=cost(1000, 1000),
        name="forward",
    )(info, streams, short, long_taps, fwd, inv, *after)


def run_finish(info, streams, halo, short, long_taps, fwd, inv, own, after=()):
    mix_in, turned, q_side, k_side, v_side, conv, gate = own
    top = lane_spec(2 * LONG)
    rim = lane_spec(RIM)
    return pl.pallas_call(
        finish_kernel,
        grid=(CH // LANES,),
        in_specs=[
            SMEM, lane_spec(3, RIM), lane_spec(RIM + 2 * TAIL), lane_spec(3, SHORT), lane_spec(LONG),
            whole(2 * LONG, 2 * LONG), whole(2 * LONG, 2 * LONG), top, rim, rim, top,
        ] + [ANY] * (3 + len(after)),
        out_specs=[top, pl.BlockSpec((LANES, 2 * LONG), lambda i: (i, 0)), rim, rim, rim, top],
        out_shape=forward_shapes(),
        input_output_aliases={7: 2, 8: 3, 9: 4, 11: 0, 12: 1, 13: 5},
        scratch_shapes=[
            pltpu.VMEM((3, TAIL + RIM, LANES), F32),
            pltpu.VMEM((3 * LONG, LANES), BF16),
        ],
        compiler_params=params(56),
        cost_estimate=cost(1000, 1000),
        name="finish",
    )(info, streams, halo, short, long_taps, fwd, inv, q_side, k_side, v_side, gate, mix_in, turned, conv, *after)


def run_backward(info, d_conv, d_q, k_side, v_side, short, long_taps, fwd, inv, after=()):
    return pl.pallas_call(
        backward_kernel,
        grid=(CH // LANES,),
        in_specs=[
            SMEM, lane_spec(ROWS), lane_spec(ROWS), lane_spec(ROWS), lane_spec(ROWS),
            lane_spec(3, SHORT), lane_spec(LONG),
            whole(2 * LONG, 2 * LONG), whole(2 * LONG, 2 * LONG),
        ] + [ANY] * len(after),
        out_specs=lane_spec(3, HALF),
        out_shape=jax.ShapeDtypeStruct((3, ROWS, CH), BF16),
        scratch_shapes=[pltpu.VMEM((3, HALF + RIM, LANES), F32)],
        compiler_params=params(56),
        cost_estimate=cost(1000, 1000),
        name="backward",
    )(info, d_conv, d_q, k_side, v_side, short, long_taps, fwd, inv, *after)


def run_backward_end(info, d_conv, msg, d_q, k_side, v_side, short, long_taps, fwd, inv, out, after=()):
    low = pl.BlockSpec((HALF, LANES), lambda i: (1, i))
    return pl.pallas_call(
        backward_end_kernel,
        grid=(CH // LANES,),
        in_specs=[
            SMEM, low, lane_spec(TAIL + 3 * RIM), low, low, low,
            lane_spec(3, SHORT), lane_spec(LONG),
            whole(2 * LONG, 2 * LONG), whole(2 * LONG, 2 * LONG), ANY,
        ] + [ANY] * len(after),
        out_specs=pl.BlockSpec((3, HALF, LANES), lambda i: (0, 1, i)),
        out_shape=jax.ShapeDtypeStruct((3, ROWS, CH), BF16),
        input_output_aliases={10: 0},
        scratch_shapes=[
            pltpu.VMEM((3, HALF + RIM, LANES), F32),
            pltpu.VMEM((HALF + 2 * LONG, LANES), BF16),
        ],
        compiler_params=params(56),
        cost_estimate=cost(1000, 1000),
        name="backward_end",
    )(info, d_conv, msg, d_q, k_side, v_side, short, long_taps, fwd, inv, out, *after)


def project_kernel(order_ref, mix_ref, weight_ref, *refs):
    out_ref = refs[-1]
    out_ref[0] = jnp.dot(mix_ref[...], weight_ref[...], preferred_element_type=F32).astype(BF16)


def own_block(i, info):
    return 0, 2 * ((info[3] + 1 + i) & 3) + info[1]


def other_block(i, info):
    return 0, 2 * ((info[3] + 1 + i) & 3) + 1 - info[1]


def run_project(info, mix_in, weight, after=()):
    count = 4
    return pl.pallas_call(
        project_kernel,
        grid_spec=pltpu.PrefetchScalarGridSpec(
            num_scalar_prefetch=1,
            grid=(count,),
            in_specs=[
                pl.BlockSpec((ROWS, CH), lambda i, order: (0, 0)),
                pl.BlockSpec((CH, CH), other_block),
            ] + [ANY] * len(after),
            out_specs=pl.BlockSpec((1, ROWS, CH), lambda i, order: (i, 0, 0)),
        ),
        out_shape=jax.ShapeDtypeStruct((count, ROWS, CH), BF16),
        compiler_params=params(),
        cost_estimate=cost(1000, 1000),
        name="project",
    )(info, mix_in, weight, *after)


def project_add_kernel(info_ref, mix_ref, weight_ref, other_ref, *refs):
    total = jnp.dot(mix_ref[...], weight_ref[...], preferred_element_type=F32)
    total += other_ref[0].astype(F32)
    up_ref, down_ref, next_ref, last_ref, own_ref = refs[-5:]
    top, bottom = total[:HALF].astype(BF16), total[HALF:].astype(BF16)

    @pl.when(pl.program_id(0) == 0)
    def _():
        next_ref[...] = top
        up_ref[HALF:] = bottom

    @pl.when(pl.program_id(0) == 1)
    def _():
        up_ref[:HALF] = top
        down_ref[HALF:] = bottom

    @pl.when(pl.program_id(0) == 2)
    def _():
        down_ref[:HALF] = top
        last_ref[...] = bottom

    @pl.when(pl.program_id(0) == 3)
    def _():
        own_ref[...] = total


def run_project_add(info, mix_in, weight, other, after=()):
    fixed = pl.BlockSpec((ROWS, CH), lambda i, order: (0, 0))
    half = pl.BlockSpec((HALF, CH), lambda i, order: (0, 0))
    return pl.pallas_call(
        project_add_kernel,
        grid_spec=pltpu.PrefetchScalarGridSpec(
            num_scalar_prefetch=1,
            grid=(4,),
            in_specs=[
                fixed,
                pl.BlockSpec((CH, CH), own_block),
                pl.BlockSpec((1, ROWS, CH), lambda i, order: (i, 0, 0)),
            ] + [ANY] * len(after),
            out_specs=[fixed, fixed, half, half, fixed],
        ),
        out_shape=[jax.ShapeDtypeStruct((rows, CH), BF16) for rows in (ROWS, ROWS, HALF, HALF)]
        + [jax.ShapeDtypeStruct((ROWS, CH), F32)],
        compiler_params=params(),
        cost_estimate=cost(1000, 1000),
        name="project_add",
    )(info, mix_in, weight, other, *after)


def prepare_kernel(info_ref, qkv_ref, cot_ref, tail_ref, quarter_ref):
    live = live_rows(info_ref[0], ROWS // 2, ROWS // 2)[:, 0:1]
    place = 0
    for stream, rows in ((0, RIM), (1, TAIL), (2, TAIL)):
        masked = qkv_ref[stream, ROWS // 2 - rows :].astype(F32) * live[ROWS // 2 - rows :]
        tail_ref[place : place + rows] = masked.astype(BF16)
        place += rows
    for quarter in range(NX):
        quarter_ref[quarter] = cot_ref[:, quarter * LANES : (quarter + 1) * LANES]


def run_prepare(info, streams, cotangent):
    return pl.pallas_call(
        prepare_kernel,
        grid=(1,),
        in_specs=[SMEM, pl.BlockSpec((3, ROWS // 2, CH), lambda i: (0, 1, 0)), whole(ROWS, CH)],
        out_specs=[whole(RIM + 2 * TAIL, CH), whole(NX, ROWS, LANES)],
        out_shape=[
            jax.ShapeDtypeStruct((RIM + 2 * TAIL, CH), BF16),
            jax.ShapeDtypeStruct((NX, ROWS, LANES), BF16),
        ],
        compiler_params=params(56),
        cost_estimate=cost(1000, 1000),
        name="prepare",
    )(info, streams, cotangent)


def outer_kernel(info_ref, mine, theirs, *refs):
    turned, out_ref = refs[:NX], refs[-1]
    core = info_ref[1]
    for y in range(NY):
        total = None
        for behind in range(NX):
            x = (info_ref[2] - behind) & 3
            both = jnp.concatenate([mine[y, x], theirs[y, x]], axis=1)
            part = jnp.dot(turned[behind][...], both, preferred_element_type=F32)
            total = part if total is None else total + part
        total = total * (1.0 / np.sqrt(float(ROWS * NZ * NX)))
        out_ref[2 * y + core] = total[:, :LANES].astype(BF16)
        out_ref[2 * y + 1 - core] = total[:, LANES:].astype(BF16)


def run_outer(info, turned, mine, theirs, after=()):
    return pl.pallas_call(
        outer_kernel,
        in_specs=[SMEM] + [VMEM] * 6 + [ANY] * len(after),
        out_specs=VMEM,
        out_shape=jax.ShapeDtypeStruct((NZ, CH, LANES), BF16),
        compiler_params=params(),
        cost_estimate=cost(1000, 1000),
        name="outer",
    )(info, mine, theirs, *turned, *after)


def d_mix_kernel(info_ref, weight_ref, mine, theirs, q_ref, k_ref, v_ref, conv_ref, *refs):
    dconv_ref, dq_ref, msg_ref = refs[-3:]
    total = None
    for slot in range(2 * NY):
        ahead = (0, -1, 1, 2)[slot // 2]
        block = 2 * ((info_ref[3] + ahead) & 3) + (info_ref[1] if slot % 2 == 0 else 1 - info_ref[1])
        column = pl.multiple_of(block * CH, CH)
        piece = (mine, theirs)[slot % 2][slot // 2]
        part = lax.dot_general(
            piece, weight_ref[:, pl.ds(column, CH)], (((1,), (1,)), ((), ())),
            preferred_element_type=F32,
        )
        total = part if total is None else total + part
    row = lax.broadcasted_iota(jnp.int32, (ROWS, CH), 0)
    d_mix = jnp.where(row < info_ref[0], total, 0.0)
    d_conv = (d_mix * q_ref[...]).astype(BF16)
    d_q = d_mix * conv_ref[...]
    dconv_ref[...] = d_conv
    dq_ref[...] = d_q
    msg_ref[0:TAIL] = d_conv[:TAIL]
    msg_ref[TAIL : TAIL + RIM] = d_q[:RIM].astype(BF16)
    msg_ref[TAIL + RIM : TAIL + 2 * RIM] = v_ref[0:RIM].astype(BF16)
    msg_ref[TAIL + 2 * RIM : TAIL + 3 * RIM] = k_ref[0:RIM].astype(BF16)


def run_d_mix(info, weight, mine, theirs, sides, after=()):
    return pl.pallas_call(
        d_mix_kernel,
        in_specs=[SMEM] + [VMEM] * 7 + [ANY] * len(after),
        out_specs=[VMEM] * 3,
        out_shape=[
            jax.ShapeDtypeStruct((ROWS, CH), BF16), jax.ShapeDtypeStruct((ROWS, CH), F32),
            jax.ShapeDtypeStruct((TAIL + 3 * RIM, CH), BF16),
        ],
        compiler_params=params(),
        cost_estimate=cost(1000, 1000),
        name="d_mix",
    )(info, weight, mine, theirs, *sides, *after)


def exchange(array, axis):
    groups = {
        "x": [[z * NX + x for x in range(NX)] for z in range(NZ)],
        "z": [[z * NX + x for z in range(NZ)] for x in range(NX)],
        "y": [[2 * y + core for y in range(NY)] for core in range(2)],
    }[axis]
    return lax.all_to_all(
        array, "tp" if axis == "y" else "ctx", 0, 0, axis_index_groups=groups, tiled=True
    )


def add(one, other):
    return (one.astype(F32) + other.astype(F32)).astype(BF16)


def along_x(array, ahead):
    pairs = [(i, i // NX * NX + (i + ahead) % NX) for i in range(NZ * NX)]
    return lax.ppermute(array, "ctx", pairs)


def along_y(array, ahead):
    pairs = [(i, (i + 2 * ahead) % (2 * NY)) for i in range(2 * NY)]
    return lax.ppermute(array, "tp", pairs)


def copies(array):
    return jnp.broadcast_to(array[None], (NY, *array.shape))


def other_core(array):
    return lax.ppermute(array, "tp", [(i, i ^ 1) for i in range(2 * NY)])


def neighbour(array, by):
    count = NZ * NX
    return lax.ppermute(array, "ctx", [(i, i + by) for i in range(count) if 0 <= i + by < count])


def local(qkv, short_filter, long_filter, out_weight, cotangent, valid_len):
    forward_table, causal_table, anti_table = (jnp.asarray(table) for table in tables())
    ctx, tp = lax.axis_index("ctx"), lax.axis_index("tp")
    info = jnp.stack([valid_len[0], tp & 1, ctx & 3, tp >> 1])
    streams = qkv.transpose(1, 0, 2)
    short = short_filter.transpose(1, 0, 2)

    tail, quarters = run_prepare(info, streams, cotangent)
    halo = neighbour(tail, 1)
    slab = exchange(quarters, "x")
    own = run_forward(info, streams, short, long_filter, forward_table, causal_table, (tail,))
    slab, held, *_ = lax.optimization_barrier([slab, cotangent, halo, *own])
    slab_copies = copies(slab)
    mine = exchange(slab_copies, "y").reshape(NY, NX, ROWS, LANES)
    mix_in, turned, q_side, k_side, v_side, conv = run_finish(
        info, streams, halo, short, long_filter, forward_table, causal_table, own, (slab_copies,)
    )
    turned = [turned] + [along_x(turned, ahead) for ahead in (1, 2, 3)]
    far = along_y(held, 2)
    given = run_project(info, mix_in, out_weight, (turned[1],))
    taken = other_core(given)
    ready, held, *_ = lax.optimization_barrier([mine, held, far, given, *turned])
    below, above = along_y(held, 1), along_y(held, -1)
    theirs = other_core(ready)
    partial = run_outer(info, turned, mine, theirs)
    sums = exchange(partial, "z")
    up, down, next_top, last_bottom, own_out = run_project_add(info, mix_in, out_weight, taken, (partial,))
    from_below, from_above = along_y(up, 1), along_y(down, -1)
    held, _ = lax.optimization_barrier((cotangent, up))
    cots = jnp.stack([held, below, above, far])
    cots_other = other_core(cots)
    d_conv, d_q, msg = run_d_mix(
        info, out_weight, cots, cots_other, (q_side, k_side, v_side, conv), (up,)
    )
    from_below, from_above, _ = lax.optimization_barrier((from_below, from_above, msg))
    next_top, last_bottom = add(next_top, from_below[:HALF]), add(last_bottom, from_above[HALF:])
    top, bottom = along_y(next_top, 1), along_y(last_bottom, -1)
    msg = neighbour(msg, -1)
    sides = (d_q, k_side, v_side, short, long_filter, forward_table, anti_table)
    begun = run_backward(info, d_conv, *sides)
    d_streams = run_backward_end(info, d_conv, msg, *sides, begun, (next_top, last_bottom))
    sums, own_out, _ = lax.optimization_barrier((sums, own_out, d_streams))
    d_qkv = d_streams.transpose(1, 0, 2)
    top = own_out[:HALF] + top.astype(F32) + from_above[:HALF].astype(F32)
    bottom = own_out[HALF:] + bottom.astype(F32) + from_below[HALF:].astype(F32)
    mixed = jnp.concatenate([top, bottom], axis=0).astype(BF16)
    d_weight = jnp.sum(sums.astype(F32), axis=0)
    return mixed, d_qkv, d_weight


def solution(mesh):
    in_specs = (
        P("ctx", None, "tp"),
        P(None, None, "tp"),
        P(None, "tp"),
        P("tp", None),
        P("ctx", "tp"),
        P("ctx"),
    )
    out_specs = (P("ctx", "tp"), P("ctx", None, "tp"), P("tp", "ctx"))
    return jax.shard_map(local, mesh=mesh, in_specs=in_specs, out_specs=out_specs, check_vma=False)
```

```python
import functools

import jax
import jax.numpy as jnp
import ml_dtypes
import numpy as np
from jax import lax
from jax.experimental import pallas as pl
from jax.experimental.pallas import tpu as pltpu
from jax.sharding import PartitionSpec as P

SHORT = 7
LONG = 128
ROWS = 512
CH = 512
LANES = 128
TAIL = 144
RIM = 16
STEP = 64
NZ, NX, NY = 8, 4, 4
HALF = ROWS // 2
F32, BF16 = jnp.float32, jnp.bfloat16


def split_bf16(table):
    high = table.astype(ml_dtypes.bfloat16)
    low = (table - high.astype(np.float64)).astype(ml_dtypes.bfloat16)
    return high, low


def tables():
    size = 2 * LONG
    freq = np.arange(LONG)[:, None]
    angle = 2.0 * np.pi * freq * np.arange(size)[None, :] / size
    real = np.concatenate([np.cos(angle), np.sin(angle)], axis=0)
    real[LONG] = (-1.0) ** np.arange(size)
    high, low = split_bf16(real[:, :LONG])
    forward = np.concatenate([high, low], axis=1)
    weight = np.full((2 * LONG, 1), 2.0 / size)
    weight[0] = weight[LONG] = 1.0 / size
    inverse = (real * weight).T
    causal = np.concatenate(split_bf16(inverse[LONG:]), axis=0)
    anti = np.concatenate(split_bf16(inverse[:LONG]), axis=0)
    return forward, causal, anti


def signs(rows):
    row = lax.broadcasted_iota(jnp.int32, (rows, LANES), 0)
    return jnp.where(row % 2 == 0, 1.0, -1.0).astype(F32)


def spectrum(forward, block):
    return jnp.dot(forward, jnp.concatenate([block, block], axis=0), preferred_element_type=F32)


def filter_spectrum(forward, taps):
    both = spectrum(forward, taps)
    cos_part, sin_part = both[:LONG], both[LONG:]
    first = lax.broadcasted_iota(jnp.int32, (LONG, LANES), 0) == 0
    return cos_part, jnp.where(first, 0.0, sin_part), jnp.where(first, sin_part, cos_part)


def back(table, product):
    high = product.astype(BF16)
    low = (product - high.astype(F32)).astype(BF16)
    half = table.shape[0] // 2
    both = jnp.dot(table, high, preferred_element_type=F32)
    rest = jnp.dot(table[:half], low, preferred_element_type=F32)
    return both[:half] + both[half:] + rest


def live_rows(valid, start, rows):
    row = lax.broadcasted_iota(jnp.int32, (rows, LANES), 0) + start
    return jnp.where(row < valid, 1.0, 0.0).astype(F32)


def filtered(short_ref, ext_ref, stream, start, rows):
    total = short_ref[stream, 0:1] * ext_ref[stream, start : start + rows]
    for tap in range(1, SHORT):
        total += short_ref[stream, tap : tap + 1] * ext_ref[stream, start - tap : start - tap + rows]
    return total


def convolve(before, now, sign, inv, cos_h, sin_h, alt_h):
    window = before + sign * now
    cos_x, sin_x = window[:LONG], window[LONG:]
    product = jnp.concatenate(
        [cos_x * cos_h - sin_x * sin_h, cos_x * sin_h + sin_x * alt_h], axis=0
    )
    return back(inv, product)


def forward_kernel(valid_ref, qkv_ref, short_ref, long_ref, fwd_ref, inv_ref, *refs):
    mix_ref, turned_ref, q_ref, k_ref, v_ref, conv_ref, gate_ref, ext_ref = refs[-8:]
    valid = valid_ref[0]
    ext_ref[:, 0:RIM] = jnp.zeros((3, RIM, LANES), F32)
    for start in range(0, ROWS, STEP):
        live = live_rows(valid, start, STEP)
        for stream in range(3):
            ext_ref[stream, RIM + start : RIM + start + STEP] = (
                qkv_ref[stream, start : start + STEP].astype(F32) * live
            )
    for start in range(0, ROWS, STEP):
        k_side = filtered(short_ref, ext_ref, 1, RIM + start, STEP)
        v_side = filtered(short_ref, ext_ref, 2, RIM + start, STEP)
        k_ref[start : start + STEP] = k_side.astype(BF16)
        v_ref[start : start + STEP] = v_side.astype(BF16)
        q_ref[start : start + STEP] = filtered(short_ref, ext_ref, 0, RIM + start, STEP)
        gate_ref[start : start + STEP] = (k_side * v_side).astype(BF16)
    fwd = fwd_ref[...]
    inv = inv_ref[...]
    taps = filter_spectrum(fwd, long_ref[...])
    sign = signs(2 * LONG)
    before = spectrum(fwd, gate_ref[LONG : 2 * LONG])
    for start in range(2 * LONG, ROWS, LONG):
        now = spectrum(fwd, gate_ref[start : start + LONG])
        conv = convolve(before, now, sign, inv, *taps)
        before = now
        conv_ref[start : start + LONG] = conv.astype(BF16)
        mix_in = live_rows(valid, start, LONG) * q_ref[start : start + LONG] * conv
        mix_ref[start : start + LONG] = mix_in.astype(BF16)
        turned_ref[:, start : start + LONG] = mix_in.T.astype(BF16)


def finish_kernel(
    valid_ref, qkv_ref, halo_ref, short_ref, long_ref, fwd_ref, inv_ref, q_in, k_in, v_in, gate_in, *refs
):
    mix_ref, turned_ref, q_ref, k_ref, v_ref, conv_ref, ext_ref, gate_ref = refs[-8:]
    valid = valid_ref[0]
    ext_ref[0, TAIL - RIM : TAIL] = halo_ref[0:RIM].astype(F32)
    ext_ref[1, 0:TAIL] = halo_ref[RIM : RIM + TAIL].astype(F32)
    ext_ref[2, 0:TAIL] = halo_ref[RIM + TAIL : RIM + 2 * TAIL].astype(F32)
    live = live_rows(valid, 0, RIM)
    for stream in range(3):
        ext_ref[stream, TAIL : TAIL + RIM] = qkv_ref[stream].astype(F32) * live
    for start in range(0, LONG, STEP):
        k_side = filtered(short_ref, ext_ref, 1, RIM + start, STEP)
        v_side = filtered(short_ref, ext_ref, 2, RIM + start, STEP)
        gate_ref[start : start + STEP] = (k_side * v_side).astype(BF16)
    q_rim = filtered(short_ref, ext_ref, 0, TAIL, RIM)
    k_rim = filtered(short_ref, ext_ref, 1, TAIL, RIM)
    v_rim = filtered(short_ref, ext_ref, 2, TAIL, RIM)
    q_ref[...] = q_rim
    k_ref[...] = k_rim.astype(BF16)
    v_ref[...] = v_rim.astype(BF16)
    gate_ref[LONG : LONG + RIM] = (k_rim * v_rim).astype(BF16)
    gate_ref[LONG + RIM : 3 * LONG] = gate_in[RIM:]
    fwd = fwd_ref[...]
    inv = inv_ref[...]
    taps = filter_spectrum(fwd, long_ref[...])
    sign = signs(2 * LONG)
    before = spectrum(fwd, gate_ref[0:LONG])
    for start in range(0, 2 * LONG, LONG):
        now = spectrum(fwd, gate_ref[LONG + start : 2 * LONG + start])
        conv = convolve(before, now, sign, inv, *taps)
        before = now
        conv_ref[start : start + LONG] = conv.astype(BF16)
        q_side = q_in[start : start + LONG]
        if start == 0:
            q_side = jnp.concatenate([q_rim, q_side[RIM:]], axis=0)
        mix_in = live_rows(valid, start, LONG) * q_side * conv
        mix_ref[start : start + LONG] = mix_in.astype(BF16)
        turned_ref[:, start : start + LONG] = mix_in.T.astype(BF16)


def correlate(now, after, sign, inv, cos_h, sin_h, alt_h):
    window = now + sign * after
    cos_x, sin_x = window[:LONG], window[LONG:]
    product = jnp.concatenate(
        [cos_x * cos_h + sin_x * sin_h, sin_x * alt_h - cos_x * sin_h], axis=0
    )
    return back(inv, product)


def filter_back(valid, first, short_ref, ext_ref, out_ref):
    for start in range(0, HALF, STEP):
        live = live_rows(valid, first + start, STEP)
        for stream in range(3):
            total = short_ref[stream, 0:1] * ext_ref[stream, start : start + STEP]
            for tap in range(1, SHORT):
                total += short_ref[stream, tap : tap + 1] * ext_ref[stream, start + tap : start + tap + STEP]
            out_ref[stream, start : start + STEP] = (total * live).astype(BF16)


def backward_kernel(
    valid_ref, dconv_ref, dq_ref, k_ref, v_ref, short_ref, long_ref, fwd_ref, inv_ref, *refs
):
    out_ref, ext_ref = refs[-2:]
    fwd = fwd_ref[...]
    inv = inv_ref[...]
    taps = filter_spectrum(fwd, long_ref[...])
    sign = signs(2 * LONG)
    ext_ref[0, 0 : HALF + RIM] = dq_ref[0 : HALF + RIM].astype(F32)
    now = spectrum(fwd, dconv_ref[0:LONG])
    for start in range(0, HALF + LONG, LONG):
        after = spectrum(fwd, dconv_ref[start + LONG : start + 2 * LONG])
        gated = correlate(now, after, sign, inv, *taps)
        now = after
        rows = LONG if start < HALF else RIM
        ext_ref[1, start : start + rows] = gated[:rows] * v_ref[start : start + rows].astype(F32)
        ext_ref[2, start : start + rows] = gated[:rows] * k_ref[start : start + rows].astype(F32)
    filter_back(valid_ref[0], 0, short_ref, ext_ref, out_ref)


def backward_end_kernel(
    valid_ref, dconv_ref, msg_ref, dq_ref, k_ref, v_ref, short_ref, long_ref, fwd_ref, inv_ref, *refs
):
    out_ref, ext_ref, gate_ref = refs[-3:]
    fwd = fwd_ref[...]
    inv = inv_ref[...]
    taps = filter_spectrum(fwd, long_ref[...])
    sign = signs(2 * LONG)
    gate_ref[0:HALF] = dconv_ref[...]
    gate_ref[HALF : HALF + TAIL] = msg_ref[0:TAIL]
    gate_ref[HALF + TAIL : HALF + 2 * LONG] = jnp.zeros((2 * LONG - TAIL, LANES), BF16)
    ext_ref[0, 0:HALF] = dq_ref[...].astype(F32)
    ext_ref[0, HALF : HALF + RIM] = msg_ref[TAIL : TAIL + RIM].astype(F32)
    now = spectrum(fwd, gate_ref[0:LONG])
    for start in range(0, HALF + LONG, LONG):
        after = spectrum(fwd, gate_ref[start + LONG : start + 2 * LONG])
        gated = correlate(now, after, sign, inv, *taps)
        now = after
        if start < HALF:
            ext_ref[1, start : start + LONG] = gated * v_ref[start : start + LONG].astype(F32)
            ext_ref[2, start : start + LONG] = gated * k_ref[start : start + LONG].astype(F32)
        else:
            v_rim = msg_ref[TAIL + RIM : TAIL + 2 * RIM].astype(F32)
            k_rim = msg_ref[TAIL + 2 * RIM : TAIL + 3 * RIM].astype(F32)
            ext_ref[1, HALF : HALF + RIM] = gated[:RIM] * v_rim
            ext_ref[2, HALF : HALF + RIM] = gated[:RIM] * k_rim
    filter_back(valid_ref[0], HALF, short_ref, ext_ref, out_ref)


def params(mib=20):
    return pltpu.CompilerParams(vmem_limit_bytes=mib * 2**20)


def cost(flops, moved):
    return pl.CostEstimate(flops=flops, bytes_accessed=moved, transcendentals=0)


SMEM = pl.BlockSpec(memory_space=pltpu.SMEM)
VMEM = pl.BlockSpec(memory_space=pltpu.VMEM)
ANY = pl.BlockSpec(memory_space=pl.ANY)


def lane_spec(*lead):
    return pl.BlockSpec(lead + (LANES,), lambda i: (0,) * len(lead) + (i,))


def whole(*shape):
    return pl.BlockSpec(shape, lambda i: (0,) * len(shape))


def forward_shapes():
    side = jax.ShapeDtypeStruct((ROWS, CH), F32)
    square = jax.ShapeDtypeStruct((ROWS, CH), BF16)
    return [square, square, side, square, square, square]


def run_forward(info, streams, short, long_taps, fwd, inv, after=()):
    return pl.pallas_call(
        forward_kernel,
        grid=(CH // LANES,),
        in_specs=[
            SMEM, lane_spec(3, ROWS), lane_spec(3, SHORT), lane_spec(LONG),
            whole(2 * LONG, 2 * LONG), whole(2 * LONG, 2 * LONG),
        ] + [ANY] * len(after),
        out_specs=[lane_spec(ROWS), pl.BlockSpec((LANES, ROWS), lambda i: (i, 0))] + [lane_spec(ROWS)] * 5,
        out_shape=forward_shapes() + [jax.ShapeDtypeStruct((ROWS, CH), BF16)],
        scratch_shapes=[pltpu.VMEM((3, RIM + ROWS, LANES), F32)],
        compiler_params=params(56),
        cost_estimate=cost(1000, 1000),
        name="forward",
    )(info, streams, short, long_taps, fwd, inv, *after)


def run_finish(info, streams, halo, short, long_taps, fwd, inv, own, after=()):
    mix_in, turned, q_side, k_side, v_side, conv, gate = own
    top = lane_spec(2 * LONG)
    rim = lane_spec(RIM)
    return pl.pallas_call(
        finish_kernel,
        grid=(CH // LANES,),
        in_specs=[
            SMEM, lane_spec(3, RIM), lane_spec(RIM + 2 * TAIL), lane_spec(3, SHORT), lane_spec(LONG),
            whole(2 * LONG, 2 * LONG), whole(2 * LONG, 2 * LONG), top, rim, rim, top,
        ] + [ANY] * (3 + len(after)),
        out_specs=[top, pl.BlockSpec((LANES, 2 * LONG), lambda i: (i, 0)), rim, rim, rim, top],
        out_shape=forward_shapes(),
        input_output_aliases={7: 2, 8: 3, 9: 4, 11: 0, 12: 1, 13: 5},
        scratch_shapes=[
            pltpu.VMEM((3, TAIL + RIM, LANES), F32),
            pltpu.VMEM((3 * LONG, LANES), BF16),
        ],
        compiler_params=params(56),
        cost_estimate=cost(1000, 1000),
        name="finish",
    )(info, streams, halo, short, long_taps, fwd, inv, q_side, k_side, v_side, gate, mix_in, turned, conv, *after)


def run_backward(info, d_conv, d_q, k_side, v_side, short, long_taps, fwd, inv, after=()):
    return pl.pallas_call(
        backward_kernel,
        grid=(CH // LANES,),
        in_specs=[
            SMEM, lane_spec(ROWS), lane_spec(ROWS), lane_spec(ROWS), lane_spec(ROWS),
            lane_spec(3, SHORT), lane_spec(LONG),
            whole(2 * LONG, 2 * LONG), whole(2 * LONG, 2 * LONG),
        ] + [ANY] * len(after),
        out_specs=lane_spec(3, HALF),
        out_shape=jax.ShapeDtypeStruct((3, ROWS, CH), BF16),
        scratch_shapes=[pltpu.VMEM((3, HALF + RIM, LANES), F32)],
        compiler_params=params(56),
        cost_estimate=cost(1000, 1000),
        name="backward",
    )(info, d_conv, d_q, k_side, v_side, short, long_taps, fwd, inv, *after)


def run_backward_end(info, d_conv, msg, d_q, k_side, v_side, short, long_taps, fwd, inv, out, after=()):
    low = pl.BlockSpec((HALF, LANES), lambda i: (1, i))
    return pl.pallas_call(
        backward_end_kernel,
        grid=(CH // LANES,),
        in_specs=[
            SMEM, low, lane_spec(TAIL + 3 * RIM), low, low, low,
            lane_spec(3, SHORT), lane_spec(LONG),
            whole(2 * LONG, 2 * LONG), whole(2 * LONG, 2 * LONG), ANY,
        ] + [ANY] * len(after),
        out_specs=pl.BlockSpec((3, HALF, LANES), lambda i: (0, 1, i)),
        out_shape=jax.ShapeDtypeStruct((3, ROWS, CH), BF16),
        input_output_aliases={10: 0},
        scratch_shapes=[
            pltpu.VMEM((3, HALF + RIM, LANES), F32),
            pltpu.VMEM((HALF + 2 * LONG, LANES), BF16),
        ],
        compiler_params=params(56),
        cost_estimate=cost(1000, 1000),
        name="backward_end",
    )(info, d_conv, msg, d_q, k_side, v_side, short, long_taps, fwd, inv, out, *after)


def project_kernel(order_ref, mix_ref, weight_ref, *refs):
    out_ref = refs[-1]
    out_ref[0] = jnp.dot(mix_ref[...], weight_ref[...], preferred_element_type=F32).astype(BF16)


def own_block(i, info):
    return 0, 2 * ((info[3] + 1 + i) & 3) + info[1]


def other_block(i, info):
    return 0, 2 * ((info[3] + 1 + i) & 3) + 1 - info[1]


def run_project(info, mix_in, weight, after=()):
    count = 4
    return pl.pallas_call(
        project_kernel,
        grid_spec=pltpu.PrefetchScalarGridSpec(
            num_scalar_prefetch=1,
            grid=(count,),
            in_specs=[
                pl.BlockSpec((ROWS, CH), lambda i, order: (0, 0)),
                pl.BlockSpec((CH, CH), other_block),
            ] + [ANY] * len(after),
            out_specs=pl.BlockSpec((1, ROWS, CH), lambda i, order: (i, 0, 0)),
        ),
        out_shape=jax.ShapeDtypeStruct((count, ROWS, CH), BF16),
        compiler_params=params(),
        cost_estimate=cost(1000, 1000),
        name="project",
    )(info, mix_in, weight, *after)


def project_add_kernel(info_ref, mix_ref, weight_ref, other_ref, *refs):
    total = jnp.dot(mix_ref[...], weight_ref[...], preferred_element_type=F32)
    total += other_ref[0].astype(F32)
    up_ref, down_ref, next_ref, last_ref, own_ref = refs[-5:]
    top, bottom = total[:HALF].astype(BF16), total[HALF:].astype(BF16)

    @pl.when(pl.program_id(0) == 0)
    def _():
        next_ref[...] = top
        up_ref[HALF:] = bottom

    @pl.when(pl.program_id(0) == 1)
    def _():
        up_ref[:HALF] = top
        down_ref[HALF:] = bottom

    @pl.when(pl.program_id(0) == 2)
    def _():
        down_ref[:HALF] = top
        last_ref[...] = bottom

    @pl.when(pl.program_id(0) == 3)
    def _():
        own_ref[...] = total


def run_project_add(info, mix_in, weight, other, after=()):
    fixed = pl.BlockSpec((ROWS, CH), lambda i, order: (0, 0))
    half = pl.BlockSpec((HALF, CH), lambda i, order: (0, 0))
    return pl.pallas_call(
        project_add_kernel,
        grid_spec=pltpu.PrefetchScalarGridSpec(
            num_scalar_prefetch=1,
            grid=(4,),
            in_specs=[
                fixed,
                pl.BlockSpec((CH, CH), own_block),
                pl.BlockSpec((1, ROWS, CH), lambda i, order: (i, 0, 0)),
            ] + [ANY] * len(after),
            out_specs=[fixed, fixed, half, half, fixed],
        ),
        out_shape=[jax.ShapeDtypeStruct((rows, CH), BF16) for rows in (ROWS, ROWS, HALF, HALF)]
        + [jax.ShapeDtypeStruct((ROWS, CH), F32)],
        compiler_params=params(),
        cost_estimate=cost(1000, 1000),
        name="project_add",
    )(info, mix_in, weight, other, *after)


def prepare_kernel(info_ref, qkv_ref, cot_ref, tail_ref, quarter_ref):
    live = live_rows(info_ref[0], ROWS // 2, ROWS // 2)[:, 0:1]
    place = 0
    for stream, rows in ((0, RIM), (1, TAIL), (2, TAIL)):
        masked = qkv_ref[stream, ROWS // 2 - rows :].astype(F32) * live[ROWS // 2 - rows :]
        tail_ref[place : place + rows] = masked.astype(BF16)
        place += rows
    for quarter in range(NX):
        quarter_ref[quarter] = cot_ref[:, quarter * LANES : (quarter + 1) * LANES]


def run_prepare(info, streams, cotangent):
    return pl.pallas_call(
        prepare_kernel,
        grid=(1,),
        in_specs=[SMEM, pl.BlockSpec((3, ROWS // 2, CH), lambda i: (0, 1, 0)), whole(ROWS, CH)],
        out_specs=[whole(RIM + 2 * TAIL, CH), whole(NX, ROWS, LANES)],
        out_shape=[
            jax.ShapeDtypeStruct((RIM + 2 * TAIL, CH), BF16),
            jax.ShapeDtypeStruct((NX, ROWS, LANES), BF16),
        ],
        compiler_params=params(56),
        cost_estimate=cost(1000, 1000),
        name="prepare",
    )(info, streams, cotangent)


def outer_kernel(info_ref, mine, theirs, *refs):
    turned, out_ref = refs[:NX], refs[-1]
    core = info_ref[1]
    for y in range(NY):
        total = None
        for behind in range(NX):
            x = (info_ref[2] - behind) & 3
            both = jnp.concatenate([mine[y, x], theirs[y, x]], axis=1)
            part = jnp.dot(turned[behind][...], both, preferred_element_type=F32)
            total = part if total is None else total + part
        total = total * (1.0 / np.sqrt(float(ROWS * NZ * NX)))
        out_ref[2 * y + core] = total[:, :LANES].astype(BF16)
        out_ref[2 * y + 1 - core] = total[:, LANES:].astype(BF16)


def run_outer(info, turned, mine, theirs, after=()):
    return pl.pallas_call(
        outer_kernel,
        in_specs=[SMEM] + [VMEM] * 6 + [ANY] * len(after),
        out_specs=VMEM,
        out_shape=jax.ShapeDtypeStruct((NZ, CH, LANES), BF16),
        compiler_params=params(),
        cost_estimate=cost(1000, 1000),
        name="outer",
    )(info, mine, theirs, *turned, *after)


def d_mix_kernel(info_ref, weight_ref, mine, theirs, q_ref, k_ref, v_ref, conv_ref, *refs):
    dconv_ref, dq_ref, msg_ref = refs[-3:]
    total = None
    for slot in range(2 * NY):
        ahead = (0, -1, 1, 2)[slot // 2]
        block = 2 * ((info_ref[3] + ahead) & 3) + (info_ref[1] if slot % 2 == 0 else 1 - info_ref[1])
        column = pl.multiple_of(block * CH, CH)
        piece = (mine, theirs)[slot % 2][slot // 2]
        part = lax.dot_general(
            piece, weight_ref[:, pl.ds(column, CH)], (((1,), (1,)), ((), ())),
            preferred_element_type=F32,
        )
        total = part if total is None else total + part
    row = lax.broadcasted_iota(jnp.int32, (ROWS, CH), 0)
    d_mix = jnp.where(row < info_ref[0], total, 0.0)
    d_conv = (d_mix * q_ref[...]).astype(BF16)
    d_q = (d_mix * conv_ref[...].astype(F32)).astype(BF16)
    dconv_ref[...] = d_conv
    dq_ref[...] = d_q
    msg_ref[0:TAIL] = d_conv[:TAIL]
    msg_ref[TAIL : TAIL + RIM] = d_q[:RIM]
    msg_ref[TAIL + RIM : TAIL + 2 * RIM] = v_ref[...]
    msg_ref[TAIL + 2 * RIM : TAIL + 3 * RIM] = k_ref[...]


def run_d_mix(info, weight, mine, theirs, sides, after=()):
    return pl.pallas_call(
        d_mix_kernel,
        in_specs=[SMEM] + [VMEM] * 7 + [ANY] * len(after),
        out_specs=[VMEM] * 3,
        out_shape=[
            jax.ShapeDtypeStruct((ROWS, CH), BF16), jax.ShapeDtypeStruct((ROWS, CH), BF16),
            jax.ShapeDtypeStruct((TAIL + 3 * RIM, CH), BF16),
        ],
        compiler_params=params(),
        cost_estimate=cost(1000, 1000),
        name="d_mix",
    )(info, weight, mine, theirs, *sides, *after)


def exchange(array, axis):
    groups = {
        "x": [[z * NX + x for x in range(NX)] for z in range(NZ)],
        "z": [[z * NX + x for z in range(NZ)] for x in range(NX)],
        "y": [[2 * y + core for y in range(NY)] for core in range(2)],
    }[axis]
    return lax.all_to_all(
        array, "tp" if axis == "y" else "ctx", 0, 0, axis_index_groups=groups, tiled=True
    )


def add(one, other):
    return (one.astype(F32) + other.astype(F32)).astype(BF16)


def along_x(array, ahead):
    pairs = [(i, i // NX * NX + (i + ahead) % NX) for i in range(NZ * NX)]
    return lax.ppermute(array, "ctx", pairs)


def along_y(array, ahead):
    pairs = [(i, (i + 2 * ahead) % (2 * NY)) for i in range(2 * NY)]
    return lax.ppermute(array, "tp", pairs)


def copies(array):
    return jnp.broadcast_to(array[None], (NY, *array.shape))


def other_core(array):
    return lax.ppermute(array, "tp", [(i, i ^ 1) for i in range(2 * NY)])


def neighbour(array, by):
    count = NZ * NX
    return lax.ppermute(array, "ctx", [(i, i + by) for i in range(count) if 0 <= i + by < count])


def local(qkv, short_filter, long_filter, out_weight, cotangent, valid_len):
    forward_table, causal_table, anti_table = (jnp.asarray(table) for table in tables())
    ctx, tp = lax.axis_index("ctx"), lax.axis_index("tp")
    info = jnp.stack([valid_len[0], tp & 1, ctx & 3, tp >> 1])
    streams = qkv.transpose(1, 0, 2)
    short = short_filter.transpose(1, 0, 2)

    tail, quarters = run_prepare(info, streams, cotangent)
    halo = neighbour(tail, 1)
    slab = exchange(quarters, "x")
    own = run_forward(info, streams, short, long_filter, forward_table, causal_table, (tail,))
    slab, held, *_ = lax.optimization_barrier([slab, cotangent, halo, *own])
    slab_copies = copies(slab)
    mine = exchange(slab_copies, "y").reshape(NY, NX, ROWS, LANES)
    mix_in, turned, q_side, k_side, v_side, conv = run_finish(
        info, streams, halo, short, long_filter, forward_table, causal_table, own, (slab_copies,)
    )
    turned = [turned] + [along_x(turned, ahead) for ahead in (1, 2, 3)]
    far = along_y(held, 2)
    given = run_project(info, mix_in, out_weight, (turned[1],))
    taken = other_core(given)
    ready, held, *_ = lax.optimization_barrier([mine, held, far, given, *turned])
    below, above = along_y(held, 1), along_y(held, -1)
    theirs = other_core(ready)
    partial = run_outer(info, turned, mine, theirs)
    sums = exchange(partial, "z")
    up, down, next_top, last_bottom, own_out = run_project_add(info, mix_in, out_weight, taken, (partial,))
    from_below, from_above = along_y(up, 1), along_y(down, -1)
    held, _ = lax.optimization_barrier((cotangent, up))
    cots = jnp.stack([held, below, above, far])
    cots_other = other_core(cots)
    d_conv, d_q, msg = run_d_mix(
        info, out_weight, cots, cots_other, (q_side, k_side[:RIM], v_side[:RIM], conv), (up,)
    )
    from_below, from_above, _ = lax.optimization_barrier((from_below, from_above, msg))
    next_top, last_bottom = add(next_top, from_below[:HALF]), add(last_bottom, from_above[HALF:])
    top, bottom = along_y(next_top, 1), along_y(last_bottom, -1)
    msg = neighbour(msg, -1)
    sides = (d_q, k_side, v_side, short, long_filter, forward_table, anti_table)
    begun = run_backward(info, d_conv, *sides)
    d_streams = run_backward_end(info, d_conv, msg, *sides, begun, (next_top, last_bottom))
    sums, own_out, _ = lax.optimization_barrier((sums, own_out, d_streams))
    d_qkv = d_streams.transpose(1, 0, 2)
    top = own_out[:HALF] + top.astype(F32) + from_above[:HALF].astype(F32)
    bottom = own_out[HALF:] + bottom.astype(F32) + from_below[HALF:].astype(F32)
    mixed = jnp.concatenate([top, bottom], axis=0).astype(BF16)
    d_weight = jnp.sum(sums.astype(F32), axis=0)
    return mixed, d_qkv, d_weight


def solution(mesh):
    in_specs = (
        P("ctx", None, "tp"),
        P(None, None, "tp"),
        P(None, "tp"),
        P("tp", None),
        P("ctx", "tp"),
        P("ctx"),
    )
    out_specs = (P("ctx", "tp"), P("ctx", None, "tp"), P("tp", "ctx"))
    return jax.shard_map(local, mesh=mesh, in_specs=in_specs, out_specs=out_specs, check_vma=False)
```
